32 devices in a mesh: net: 8 (over z, y), scen: 4 (over x, core).
Axes of the slice: x: 2, y: 2, z: 4, core: 2. Of those that a mesh axis runs over, the one named last changes fastest.
Arguments:
- volt_mag: float32 [1920, 8], P('net', 'scen'), parts along dimension 1, may hold values from 0.94 to 1.06
- volt_ang: float32 [1920, 8], P('net', 'scen'), parts along dimension 1, may hold values from -0.5 to 0.5
- gradient: float32 [1920, 2, 8], P('net', None, 'scen'), parts along dimension 2, may hold values from -40 to 40
- branch_from: int32 [2560], P('net'), may hold values from 0 to 239, as said below
- branch_to: int32 [2560], P('net'), may hold values from 0 to 479, as said below
- branch_count: int32 [8], P('net'), may hold values from 160 to 320, as said below
- boundary: int32 [1920], P('net'), may hold values from 0 to 239, as said below
- conductance: float32 [2560], P('net'), may hold values from 0.2 to 2
- susceptance: float32 [2560], P('net'), may hold values from 1 to 10
- duals: float32 [2, 2560, 8], P(None, 'net', 'scen'), parts along dimension 2, may hold values from 0.02 to 0.2
- slacks: float32 [2, 2560, 8], P(None, 'net', 'scen'), parts along dimension 2, may hold values from 0.2 to 2
- gen_bus: int32 [320], P('net'), may hold values from 0 to 239
- gen_curvature: float32 [320], P('net'), may hold values from 1 to 10
Outputs:
- search_step: float32 [1920, 2, 8], P('net', None, 'scen'), parts along dimension 2
- residual: float32 [1920, 2, 8], P('net', None, 'scen'), parts along dimension 2
The draws below stay inside these ranges and needn't reach their ends.
There are 4 independent parts, one for each index of `scen`. The reference program is written for one: setup_inputs(seed, part) draws one part's arguments, and reference() takes and returns one part's arrays. A program takes and returns all parts, laid end to end along the dimension named above; an argument that names none is the same for every part. Nothing has to cross between parts.
Inputs may be any that keep to these rules, and one draw needn't show every extreme that they name: `branch_from`: A bus index within the branch's own device. A branch whose branch_to is 240 + e with e >= 0 starts at boundary entry e of its own device. `branch_to`: below 240: a bus of the same device other than the from-bus. 240 + e for e < 120: entry e of the previous device's list toward this device; 360 + e: entry e of the next device's list toward this device. Only the first 240 slots of a device end at a neighbour, each such value at most once a device; the first device has no ends of the first kind, the last none of the second. `branch_count`: slots at or past a device's count contribute nothing. Some device is full in every draw. `boundary`: per device 2 * 120 distinct local buses: the first 120 face the previous device, the rest the next device.
All inputs are finite; a program needn't handle non-finite values.
Results may differ from the reference program's by a relative error of at most 0.0003.
Values sent between devices are 32-bit elements; how exact they have to be, the bound alone decides.
No kernel may reach another device: no remote copies, remote signals or barrier semaphores. Data moves between devices by JAX's collectives and lax.ppermute only.
A program may use at most 64 MiB of HBM per device.

```python
import math
import jax
import jax.numpy as jnp

B_DEV = 240
S = 2
ITERS = 4
BR_DEV = 320
GH = 120
GEN_DEV = 40
BUSES = 1920
BRANCHES = 2560
GENS = 320
N_NET = 8


def network_layout(key):
    devices = BUSES // B_DEV
    key_lists = jax.random.fold_in(key, 101)
    key_order = jax.random.fold_in(key, 202)
    key_from = jax.random.fold_in(key, 303)
    key_to = jax.random.fold_in(key, 404)
    key_count = jax.random.fold_in(key, 505)
    key_full = jax.random.fold_in(key, 606)
    key_low = jax.random.fold_in(key, 707)
    lists = jax.vmap(lambda single: jax.random.permutation(single, B_DEV)[:2 * GH])(jax.random.split(key_lists, devices)).astype(jnp.int32)
    ghost_order = jax.vmap(lambda single: jax.random.permutation(single, 2 * GH))(jax.random.split(key_order, devices)).astype(jnp.int32)
    local_from = jax.random.randint(key_from, (devices, BR_DEV), 0, B_DEV).astype(jnp.int32)
    local_to = ((local_from + 1 + jax.random.randint(key_to, (devices, BR_DEV), 0, B_DEV - 1)) % B_DEV).astype(jnp.int32)
    slot_ids = jnp.arange(BR_DEV, dtype=jnp.int32)[None, :]
    device_ids = jnp.arange(devices, dtype=jnp.int32)[:, None]
    order_padded = jnp.concatenate([ghost_order, jnp.zeros((devices, BR_DEV - 2 * GH), jnp.int32)], axis=1)
    crossing = slot_ids < 2 * GH
    bad_first = (device_ids == 0) & (order_padded < GH)
    bad_last = (device_ids == devices - 1) & (order_padded >= GH)
    valid = crossing & jnp.logical_not(bad_first) & jnp.logical_not(bad_last)
    cross_from = jnp.take_along_axis(lists, order_padded, axis=1)
    from_all = jnp.where(valid, cross_from, local_from).astype(jnp.int32)
    to_all = jnp.where(valid, B_DEV + order_padded, local_to).astype(jnp.int32)
    counts = jax.random.randint(key_count, (devices,), BR_DEV // 2, BR_DEV + 1).astype(jnp.int32)
    full_dev = jax.random.randint(key_full, (), 0, devices)
    low_dev = (full_dev + 1 + jax.random.randint(key_low, (), 0, devices - 1)) % devices
    flat_ids = jnp.arange(devices, dtype=jnp.int32)
    counts = jnp.where(flat_ids == full_dev, BR_DEV, jnp.where(flat_ids == low_dev, BR_DEV // 2, counts)).astype(jnp.int32)
    return (from_all.reshape(-1), to_all.reshape(-1), counts, lists.reshape(-1))


def draw_branch_from(key, part):
    return network_layout(key)[0]


def draw_branch_to(key, part):
    return network_layout(key)[1]


def draw_branch_count(key, part):
    return network_layout(key)[2]


def draw_boundary(key, part):
    return network_layout(key)[3]


def draw_gradient(key, part):
    devices = BUSES // B_DEV
    key_bus = jax.random.fold_in(key, 11)
    key_scen = jax.random.fold_in(key, 12)
    key_rough = jax.random.fold_in(key, 13)
    position = (jnp.arange(BUSES) // B_DEV).astype(jnp.float32)
    ramp = (1.0 + 2.0 * position / max(devices - 1, 1))[:, None, None]
    scen_scale = jnp.exp(jax.random.uniform(key_scen, (1, 1, S), minval=0.0, maxval=math.log(4.0)))
    bus_scale = jnp.exp(jax.random.uniform(key_bus, (BUSES, 1, 1), minval=0.0, maxval=math.log(10.0)))
    values = 0.3 * ramp * bus_scale * scen_scale * jax.random.normal(key_rough, (BUSES, 2, S))
    return jnp.clip(values, -40.0, 40.0).astype(jnp.float32)


def place_ends(entries, own_key, least, high):
    spot = [jax.random.randint(jax.random.fold_in(own_key, axis), (), 0, length) for axis, length in enumerate(entries.shape)]
    main_axis = entries.shape.index(max(entries.shape))
    next_to = spot[:main_axis] + [(spot[main_axis] + 1) % entries.shape[main_axis]] + spot[main_axis + 1:]
    return entries.at[tuple(spot)].set(least).at[tuple(next_to)].set(high)


def block_scale(own_key, extent, shards, smallest, largest):
    gain, own = 1.0, jax.random.fold_in(own_key, 6)
    for dim, shards_of in shards:
        draws = jnp.exp(jax.random.uniform(jax.random.fold_in(own, dim), (shards_of,), jnp.float32, smallest / len(shards), largest / len(shards)))
        gain = gain * jnp.repeat(draws, extent[dim] // shards_of).reshape([-1 if axis == dim else 1 for axis in range(len(extent))])
    return gain


def setup_inputs(seed: int = 0, part: int = 0) -> dict:
    streams_of = jax.random.split(jax.random.key(seed), 14)
    own_keys = jax.random.split(jax.random.fold_in(streams_of[13], part), 14)
    volt_mag = jnp.clip(0.94 + 0.119999945 * jax.random.uniform(own_keys[0], (BUSES, S), jnp.float32) ** block_scale(own_keys[0], (BUSES, S), ((0, 8),), -0.2, 0.2), 0.94, 1.06)
    volt_ang = jnp.clip(jax.random.uniform(own_keys[1], (BUSES, S), jnp.float32, -0.5, 0.5) * block_scale(own_keys[1], (BUSES, S), ((0, 8),), -0.4, 0.0), -0.5, 0.5)
    gradient = draw_gradient(jax.random.fold_in(jax.random.fold_in(streams_of[13], part), 71), part)
    branch_from = draw_branch_from(jax.random.fold_in(streams_of[13], 71), part)
    branch_to = draw_branch_to(jax.random.fold_in(streams_of[13], 71), part)
    branch_count = draw_branch_count(jax.random.fold_in(streams_of[13], 71), part)
    boundary = draw_boundary(jax.random.fold_in(streams_of[13], 71), part)
    conductance = jnp.clip(jnp.exp(math.log(2.0) - 2.3025851 * jax.random.uniform(streams_of[7], (BRANCHES,), jnp.float32) ** block_scale(streams_of[7], (BRANCHES,), ((0, 8),), -0.2, 0.2)), 0.2, 2.0)
    susceptance = jnp.clip(jnp.exp(math.log(10.0) - 2.3025851 * jax.random.uniform(streams_of[8], (BRANCHES,), jnp.float32) ** block_scale(streams_of[8], (BRANCHES,), ((0, 8),), -0.2, 0.2)), 1.0, 10.0)
    duals = jnp.clip(jnp.exp(math.log(0.2) - 2.3025851 * jax.random.uniform(own_keys[9], (2, BRANCHES, S), jnp.float32) ** block_scale(own_keys[9], (2, BRANCHES, S), ((1, 8),), -0.2, 0.2)), 0.02, 0.2)
    slacks = jnp.clip(jnp.exp(math.log(2.0) - 2.3025851 * jax.random.uniform(own_keys[10], (2, BRANCHES, S), jnp.float32) ** block_scale(own_keys[10], (2, BRANCHES, S), ((1, 8),), -0.2, 0.2)), 0.2, 2.0)
    gen_bus = place_ends(jax.random.randint(streams_of[11], (GENS,), 0, B_DEV), jax.random.fold_in(streams_of[11], 1), 0, B_DEV - 1).astype(jnp.int32)
    gen_curvature = jnp.clip(jnp.exp(math.log(10.0) - 2.3025851 * jax.random.uniform(streams_of[12], (GENS,), jnp.float32) ** block_scale(streams_of[12], (GENS,), ((0, 8),), -0.2, 0.2)), 1.0, 10.0)
    return {"volt_mag": volt_mag, "volt_ang": volt_ang, "gradient": gradient, "branch_from": branch_from, "branch_to": branch_to, "branch_count": branch_count, "boundary": boundary, "conductance": conductance, "susceptance": susceptance, "duals": duals, "slacks": slacks, "gen_bus": gen_bus, "gen_curvature": gen_curvature}


barrier_weight = 0.01
volt_low = 0.9
volt_high = 1.1
angle_reg = 0.5


def branch_blocks(magnitude_from, angle_from, magnitude_to, angle_to, conduct, suscept, weight_active, weight_reactive):
    angle_diff = angle_from - angle_to
    cosine_diff = jnp.cos(angle_diff)
    sine_diff = jnp.sin(angle_diff)
    flow_along = conduct * cosine_diff + suscept * sine_diff
    flow_across = conduct * sine_diff - suscept * cosine_diff
    cross_term = magnitude_from * magnitude_to
    active_rows = (2.0 * conduct * magnitude_from - magnitude_to * flow_along, cross_term * flow_across,
                   -magnitude_from * flow_along, -cross_term * flow_across)
    reactive_rows = (-2.0 * suscept * magnitude_from - magnitude_to * flow_across, -cross_term * flow_along,
                     -magnitude_from * flow_across, cross_term * flow_along)

    def block_entry(left_index, right_index):
        return (weight_active * active_rows[left_index] * active_rows[right_index]
                + weight_reactive * reactive_rows[left_index] * reactive_rows[right_index])

    from_block = jnp.stack([block_entry(0, 0), block_entry(0, 1), block_entry(1, 1)], axis=1)
    to_block = jnp.stack([block_entry(2, 2), block_entry(2, 3), block_entry(3, 3)], axis=1)
    cross_block = jnp.stack([block_entry(0, 2), block_entry(0, 3), block_entry(1, 2), block_entry(1, 3)], axis=1)
    return from_block, to_block, cross_block


def apply_cross(matrix_block, vector):
    return jnp.stack([matrix_block[:, 0] * vector[:, 0] + matrix_block[:, 1] * vector[:, 1],
                      matrix_block[:, 2] * vector[:, 0] + matrix_block[:, 3] * vector[:, 1]], axis=1)


def apply_cross_transposed(matrix_block, vector):
    return jnp.stack([matrix_block[:, 0] * vector[:, 0] + matrix_block[:, 2] * vector[:, 1],
                      matrix_block[:, 1] * vector[:, 0] + matrix_block[:, 3] * vector[:, 1]], axis=1)


def reference(volt_mag, volt_ang, gradient, branch_from, branch_to, branch_count, boundary, conductance, susceptance, duals, slacks, gen_bus, gen_curvature):
    slot_ids = jnp.arange(BRANCHES, dtype=jnp.int32)
    owner_dev = slot_ids // BR_DEV
    from_bus = (owner_dev * B_DEV + branch_from).astype(jnp.int32)
    bound_table = boundary.reshape(N_NET, 2 * GH)
    offset = branch_to - B_DEV
    prev_owner = jnp.clip(owner_dev - 1, 0, N_NET - 1)
    next_owner = jnp.clip(owner_dev + 1, 0, N_NET - 1)
    prev_bus = prev_owner * B_DEV + bound_table[prev_owner, jnp.clip(offset + GH, 0, 2 * GH - 1)]
    next_bus = next_owner * B_DEV + bound_table[next_owner, jnp.clip(offset - GH, 0, 2 * GH - 1)]
    to_bus = jnp.where(branch_to < B_DEV, owner_dev * B_DEV + branch_to,
                       jnp.where(offset < GH, prev_bus, next_bus)).astype(jnp.int32)
    live_mask = ((slot_ids % BR_DEV) < branch_count[owner_dev]).astype(jnp.float32)[:, None]
    weight_active = live_mask * duals[0] / slacks[0]
    weight_reactive = live_mask * duals[1] / slacks[1]
    from_block, to_block, cross_block = branch_blocks(
        volt_mag[from_bus], volt_ang[from_bus], volt_mag[to_bus], volt_ang[to_bus],
        conductance[:, None], susceptance[:, None], weight_active, weight_reactive)
    diag_sum = (jax.ops.segment_sum(from_block, from_bus, num_segments=BUSES)
                + jax.ops.segment_sum(to_block, to_bus, num_segments=BUSES))
    gen_owner = jnp.arange(GENS, dtype=jnp.int32) // GEN_DEV
    gen_sum = jax.ops.segment_sum(gen_curvature, (gen_owner * B_DEV + gen_bus).astype(jnp.int32), num_segments=BUSES)[:, None]
    barrier = barrier_weight / jnp.square(volt_mag - volt_low) + barrier_weight / jnp.square(volt_high - volt_mag)
    diag_vv = diag_sum[:, 0] + barrier + gen_sum
    diag_va = diag_sum[:, 1]
    diag_aa = diag_sum[:, 2] + angle_reg + gen_sum
    determinant = diag_vv * diag_aa - diag_va * diag_va
    inverse_vv = diag_aa / determinant
    inverse_va = -diag_va / determinant
    inverse_aa = diag_vv / determinant

    def precondition(vector):
        return jnp.stack([inverse_vv * vector[:, 0] + inverse_va * vector[:, 1],
                          inverse_va * vector[:, 0] + inverse_aa * vector[:, 1]], axis=1)

    def apply_matrix(vector):
        result = jnp.stack([diag_vv * vector[:, 0] + diag_va * vector[:, 1],
                            diag_va * vector[:, 0] + diag_aa * vector[:, 1]], axis=1)
        from_terms = apply_cross(cross_block, vector[to_bus])
        to_terms = apply_cross_transposed(cross_block, vector[from_bus])
        return (result + jax.ops.segment_sum(from_terms, from_bus, num_segments=BUSES)
                + jax.ops.segment_sum(to_terms, to_bus, num_segments=BUSES))

    def scenario_sum(left_vec, right_vec):
        return jnp.sum(left_vec * right_vec, axis=(0, 1))

    update_field = jnp.zeros_like(gradient)
    residual = gradient
    scaled = precondition(residual)
    search = scaled
    energy = scenario_sum(residual, scaled)
    for iteration in range(ITERS):
        matrix_image = apply_matrix(search)
        step_size = energy / scenario_sum(search, matrix_image)
        update_field = update_field + step_size[None, None, :] * search
        residual = residual - step_size[None, None, :] * matrix_image
        if iteration + 1 < ITERS:
            scaled = precondition(residual)
            energy_next = scenario_sum(residual, scaled)
            search = scaled + (energy_next / energy)[None, None, :] * search
            energy = energy_next
    return update_field, residual
```

```python
import functools

import jax
import jax.numpy as jnp
from jax import lax
from jax.experimental import pallas as pl
from jax.experimental.pallas import tpu as pltpu
from jax.sharding import PartitionSpec as P

ITERS = 4


barrier_weight = 0.01
volt_low = 0.9
volt_high = 1.1
angle_reg = 0.5


def shifted(array, axis, by):
    peers = lax.axis_size(axis)
    pairs = [(i, i + by) for i in range(peers) if 0 <= i + by < peers]
    return lax.ppermute(array, axis, pairs)


def branch_blocks(
    magnitude_from,
    angle_from,
    magnitude_to,
    angle_to,
    conduct,
    suscept,
    weight_active,
    weight_reactive,
):
    angle_diff = angle_from - angle_to
    cosine_diff = jnp.cos(angle_diff)
    sine_diff = jnp.sin(angle_diff)
    flow_along = conduct * cosine_diff + suscept * sine_diff
    flow_across = conduct * sine_diff - suscept * cosine_diff
    cross_term = magnitude_from * magnitude_to
    active_rows = (
        2.0 * conduct * magnitude_from - magnitude_to * flow_along,
        cross_term * flow_across,
        -magnitude_from * flow_along,
        -cross_term * flow_across,
    )
    reactive_rows = (
        -2.0 * suscept * magnitude_from - magnitude_to * flow_across,
        -cross_term * flow_along,
        -magnitude_from * flow_across,
        cross_term * flow_along,
    )

    def block_entry(left_index, right_index):
        return (
            weight_active * active_rows[left_index] * active_rows[right_index]
            + weight_reactive * reactive_rows[left_index] * reactive_rows[right_index]
        )

    from_block = jnp.stack([block_entry(0, 0), block_entry(0, 1), block_entry(1, 1)], axis=1)
    to_block = jnp.stack([block_entry(2, 2), block_entry(2, 3), block_entry(3, 3)], axis=1)
    cross_block = jnp.stack(
        [block_entry(0, 2), block_entry(0, 3), block_entry(1, 2), block_entry(1, 3)], axis=1
    )
    return (from_block, to_block, cross_block)


def apply_cross(matrix_block, vector):
    return jnp.stack(
        [
            matrix_block[:, 0] * vector[:, 0] + matrix_block[:, 1] * vector[:, 1],
            matrix_block[:, 2] * vector[:, 0] + matrix_block[:, 3] * vector[:, 1],
        ],
        axis=1,
    )


def apply_cross_transposed(matrix_block, vector):
    return jnp.stack(
        [
            matrix_block[:, 0] * vector[:, 0] + matrix_block[:, 2] * vector[:, 1],
            matrix_block[:, 1] * vector[:, 0] + matrix_block[:, 3] * vector[:, 1],
        ],
        axis=1,
    )


def scenario_sum(left_vec, right_vec):
    return jnp.sum(left_vec * right_vec, axis=(0, 1))


def widen(values):
    return values[None, None, :]


def body(
    volt_mag,
    volt_ang,
    gradient,
    branch_from,
    branch_to,
    branch_count,
    boundary,
    conductance,
    susceptance,
    duals,
    slacks,
    gen_bus,
    gen_curvature,
):
    bus_count = volt_mag.shape[0]
    ghost_count = boundary.shape[0] // 2
    extended_size = bus_count + 2 * ghost_count
    slot_count = branch_from.shape[0]
    left_list = boundary[:ghost_count]
    right_list = boundary[ghost_count:]
    left_ghost = slice(bus_count, bus_count + ghost_count)
    right_ghost = slice(bus_count + ghost_count, extended_size)
    return_plan = (
        (-1, left_ghost, right_list, right_ghost),
        (1, right_ghost, left_list, left_ghost),
    )

    def share_vector(values):
        pieces = [values]
        for direction in (1, -1):
            outgoing = jnp.take(values, right_list if direction == 1 else left_list, axis=0)
            pieces.append(shifted(outgoing, "net", direction))
        return jnp.concatenate(pieces, axis=0)

    bus_state = jnp.stack([volt_mag, volt_ang], axis=1)
    pieces = [bus_state]
    for share_direction in (1, -1):
        outgoing = jnp.take(bus_state, right_list if share_direction == 1 else left_list, axis=0)
        pieces.append(shifted(outgoing, "net", share_direction))
    extended_state = jnp.concatenate(pieces, axis=0)
    from_state = jnp.take(extended_state, branch_from, axis=0)
    to_state = jnp.take(extended_state, branch_to, axis=0)
    live_mask = (jnp.arange(slot_count) < branch_count[0]).astype(jnp.float32)[:, None]
    weight_active = live_mask * duals[0] / slacks[0]
    weight_reactive = live_mask * duals[1] / slacks[1]
    from_block, to_block, cross_block = branch_blocks(
        from_state[:, 0],
        from_state[:, 1],
        to_state[:, 0],
        to_state[:, 1],
        conductance[:, None],
        susceptance[:, None],
        weight_active,
        weight_reactive,
    )
    diag_extended = jax.ops.segment_sum(
        from_block, branch_from, num_segments=extended_size
    ) + jax.ops.segment_sum(to_block, branch_to, num_segments=extended_size)
    diag_local = diag_extended[:bus_count]
    for direction, ghost_rows, target_rows, source_rows in return_plan:
        arrived_diag = shifted(diag_extended[ghost_rows], "net", direction)
        diag_local = diag_local.at[target_rows].add(arrived_diag)
    gen_table = (gen_bus[None, :] == jnp.arange(bus_count)[:, None]).astype(jnp.float32)
    gen_sum = jnp.dot(gen_table, gen_curvature, precision=lax.Precision.HIGHEST)[:, None]
    barrier = barrier_weight / jnp.square(volt_mag - volt_low) + barrier_weight / jnp.square(
        volt_high - volt_mag
    )
    diag_vv = diag_local[:, 0] + barrier + gen_sum
    diag_va = diag_local[:, 1]
    diag_aa = diag_local[:, 2] + angle_reg + gen_sum
    determinant = diag_vv * diag_aa - diag_va * diag_va
    inverse_vv = diag_aa / determinant
    inverse_va = -diag_va / determinant
    inverse_aa = diag_vv / determinant

    def precondition(vector):
        return jnp.stack(
            [
                inverse_vv * vector[:, 0] + inverse_va * vector[:, 1],
                inverse_va * vector[:, 0] + inverse_aa * vector[:, 1],
            ],
            axis=1,
        )

    update_field = jnp.zeros_like(gradient)
    residual = gradient

    def energy_of(residual_now, scaled_now):
        return lax.psum(scenario_sum(residual_now, scaled_now), "net")

    scaled = precondition(residual)
    search = scaled
    energy = energy_of(residual, scaled)
    for iteration in range(ITERS):
        extended = share_vector(search)
        from_values = jnp.take(extended, branch_from, axis=0)
        to_values = jnp.take(extended, branch_to, axis=0)
        from_terms = apply_cross(cross_block, to_values)
        to_terms = apply_cross_transposed(cross_block, from_values)
        result = jnp.stack(
            [
                diag_vv * search[:, 0] + diag_va * search[:, 1],
                diag_va * search[:, 0] + diag_aa * search[:, 1],
            ],
            axis=1,
        )
        summed = jax.ops.segment_sum(
            from_terms, branch_from, num_segments=extended_size
        ) + jax.ops.segment_sum(to_terms, branch_to, num_segments=extended_size)
        local_sum = result + summed[:bus_count]
        for apply_direction, apply_ghost_rows, apply_target_rows, apply_source_rows in return_plan:
            arrived = shifted(summed[apply_ghost_rows], "net", apply_direction)
            local_sum = local_sum.at[apply_target_rows].add(arrived)
        step_size = energy / lax.psum(scenario_sum(search, local_sum), "net")
        update_field = update_field + widen(step_size) * search
        residual = residual - widen(step_size) * local_sum
        if iteration + 1 < ITERS:
            scaled = precondition(residual)
            energy_next = energy_of(residual, scaled)
            search = scaled + widen(energy_next / energy) * search
            energy = energy_next
    return (update_field, residual)


LANES = 128
ROWS = 8
TILE_A, TILE_B, TILE_C = 0, 2, 4
TILE_LOCAL = 6
TILE_INDEX = 9
PAYLOAD_ROWS = 11 * ROWS


def fits_fast_path(blocks, bus_count, ghost_count, slot_count, gen_count, scen_count):
    return (
        blocks == 8
        and scen_count == 2
        and bus_count == 2 * ghost_count
        and ghost_count <= LANES
        and 2 * LANES < slot_count < 3 * LANES
        and gen_count <= LANES
    )


def iota(shape, dim):
    return lax.broadcasted_iota(jnp.int32, shape, dim)


def lane_take(table, index):
    return jnp.take_along_axis(table, index, axis=1, mode="promise_in_bounds")


def take_chunks(tables, index):
    lane = index & (LANES - 1)
    chunk = index >> 7
    out = lane_take(tables[0], lane)
    for number in range(1, len(tables)):
        out = jnp.where(chunk == number, lane_take(tables[number], lane), out)
    return out


def tall(row):
    return jnp.broadcast_to(row, (ROWS, LANES))


def column(row):
    return jnp.transpose(jnp.broadcast_to(row, (LANES, LANES)))


def block_entries(vi, ci, si, vj, cj, sj, g, b, wp, wq):
    cosine = ci * cj + si * sj
    sine = si * cj - ci * sj
    along = g * cosine + b * sine
    across = g * sine - b * cosine
    cross = vi * vj
    p0 = 2.0 * g * vi - vj * along
    p1 = cross * across
    p2 = -vi * along
    q0 = -2.0 * b * vi - vj * across
    q1 = -cross * along
    q2 = -vi * across

    def entry(pa, pb, qa, qb):
        return wp * pa * pb + wq * qa * qb

    return (
        entry(p0, p0, q0, q0),
        entry(p0, p1, q0, q1),
        entry(p1, p1, q1, q1),
        entry(p2, p2, q2, q2),
        entry(p1, p2, q1, q2),
        entry(p0, p2, q0, q2),
    )


def prepare_kernel(
    vm_ref,
    va_ref,
    grad_ref,
    from_ref,
    to_ref,
    count_ref,
    bound_ref,
    g_ref,
    b_ref,
    duals_ref,
    slacks_ref,
    gen_bus_ref,
    gen_curv_ref,
    out_ref,
    pos_ref,
    bus_scr,
    weight_scr,
    branch_scr,
    index_scr,
):
    bus_count = vm_ref.shape[1]
    ghost_count = bus_count // 2
    slot_count = from_ref.shape[1]
    gen_count = gen_bus_ref.shape[1]
    none = 3 * LANES - 1
    live_count = count_ref[0]

    bus_scr[...] = jnp.zeros_like(bus_scr)
    weight_scr[...] = jnp.zeros_like(weight_scr)
    branch_scr[...] = jnp.zeros_like(branch_scr)
    index_scr[...] = jnp.full_like(index_scr, -9)
    for copy in range(4):
        bus_scr[2 * copy : 2 * copy + 2, :bus_count] = vm_ref[...]
        bus_scr[8 + 2 * copy : 10 + 2 * copy, :bus_count] = va_ref[...]
    for comp in range(2):
        bus_scr[16 + 2 * comp : 18 + 2 * comp, :bus_count] = grad_ref[comp]
    live = iota((2, slot_count), 1) < live_count
    for kind in range(2):
        weight = jnp.where(live, duals_ref[kind] / slacks_ref[kind], 0.0)
        for copy in range(4):
            weight_scr[8 * kind + 2 * copy : 8 * kind + 2 * copy + 2, :slot_count] = weight
        branch_scr[2 * kind : 2 * kind + 2, :slot_count] = weight
    branch_scr[4:5, :slot_count] = g_ref[...]
    branch_scr[5:6, :slot_count] = b_ref[...]
    branch_scr[6:7, :gen_count] = gen_curv_ref[...]
    index_scr[0:1, :slot_count] = from_ref[...]
    index_scr[1:2, :slot_count] = to_ref[...]
    index_scr[2:3, :bus_count] = bound_ref[...]
    index_scr[3:4, :gen_count] = gen_bus_ref[...]

    def tiles(ref, first, chunks):
        return [ref[first : first + ROWS, LANES * c : LANES * (c + 1)] for c in range(chunks)]

    def row(ref, number, chunk):
        return ref[number : number + 1, LANES * chunk : LANES * (chunk + 1)]

    lane = iota((ROWS, LANES), 1)
    sub = iota((ROWS, LANES), 0)
    lane_row = iota((1, LANES), 1)
    sub_col = iota((LANES, LANES), 0).astype(jnp.float32)
    inside = lane < ghost_count

    raw_bound = [tall(row(index_scr, 2, c)) for c in range(2)]
    bound = [jnp.where(inside, take_chunks(raw_bound, lane + h * ghost_count), -1) for h in range(2)]
    fetch = [jnp.maximum(b, 0) for b in bound]
    bound_row = [b[0:1].astype(jnp.float32) for b in bound]
    vm_raw, va_raw, grad_raw = (tiles(bus_scr, 8 * f, 2) for f in range(3))
    vm = [jnp.where(inside, take_chunks(vm_raw, f), 1.0) for f in fetch]
    va = [jnp.where(inside, take_chunks(va_raw, f), 0.0) for f in fetch]
    grad = [jnp.where(inside, take_chunks(grad_raw, f), 0.0) for f in fetch]
    cosv = [jnp.cos(a) for a in va]
    sinv = [jnp.sin(a) for a in va]

    from_key, to_key = [], []
    for c in range(3):
        slot = lane_row + LANES * c
        alive = (slot < live_count) & (slot < slot_count)
        to_raw = row(index_scr, 1, c)
        from_key.append(
            jnp.where(alive & (to_raw < bus_count), row(index_scr, 0, c), 9998).astype(jnp.float32)
        )
        to_key.append(jnp.where(alive, to_raw, 9999).astype(jnp.float32))
    from_col = [column(k) for k in from_key]
    to_col = [column(k) for k in to_key]
    bound_col = [column(b) for b in bound_row]
    gen_col = column(row(index_scr, 3, 0).astype(jnp.float32))
    curv_col = column(row(branch_scr, 6, 0))

    def lowest(masks):
        found = functools.reduce(
            jnp.minimum,
            [jnp.where(m, sub_col + float(LANES * c), float(none)) for c, m in masks],
        )
        return jnp.min(found, axis=0, keepdims=True)

    def links(keys, cols):
        heads, counts = [], []
        for h in range(2):
            equal = [cols[c] == bound_row[h] for c in range(3)]
            heads.append(lowest(list(enumerate(equal))))
            counts.append(
                jnp.sum(
                    functools.reduce(jnp.add, [jnp.where(e, 1.0, 0.0) for e in equal]),
                    axis=0,
                    keepdims=True,
                )
            )
        nexts = []
        for c in range(3):
            later = [(c, (cols[c] == keys[c]) & (sub_col > lane_row.astype(jnp.float32)))]
            later += [(d, cols[d] == keys[c]) for d in range(c + 1, 3)]
            nexts.append(lowest(later))
        return heads, nexts, jnp.maximum(counts[0], counts[1])

    head_f, next_f, count_f = links(from_key, from_col)
    head_t, next_t, count_t = links(to_key, to_col)
    degree = jnp.max(jnp.maximum(count_f, count_t))

    def position(keys):
        found = [
            jnp.where(bound_col[h] == keys, sub_col + float(LANES * h), 0.0) for h in range(2)
        ]
        return jnp.max(jnp.maximum(found[0], found[1]), axis=0, keepdims=True)

    pos_f = [position(k) for k in from_key]
    pos_t = [position(k) for k in to_key]
    for m in range(2):
        pos_ref[m : m + 1, :] = position((lane_row + LANES * m).astype(jnp.float32)).astype(jnp.int32)

    branch_tiles = tiles(branch_scr, 0, 3)
    cross = []
    for h in range(2):
        target = jnp.where(lane_row < ghost_count, bus_count + h * ghost_count + lane_row, -5)
        slot = lowest([(c, to_col[c] == target.astype(jnp.float32)) for c in range(2)])
        cross.append(take_chunks(branch_tiles, tall(slot).astype(jnp.int32)))

    gens = [
        jnp.sum(jnp.where(gen_col == bound_row[h], curv_col, 0.0), axis=0, keepdims=True)
        for h in range(2)
    ]

    pair = sub & 3
    from_table, to_table = [], []
    for c in range(3):
        at_f = tall(pos_f[c]).astype(jnp.int32)
        at_t = tall(pos_t[c]).astype(jnp.int32)
        h00, h01, h11, h22, h12, h02 = block_entries(
            *(take_chunks(t, at_f) for t in (vm, cosv, sinv)),
            *(take_chunks(t, at_t) for t in (vm, cosv, sinv)),
            tall(row(branch_scr, 4, c)),
            tall(row(branch_scr, 5, c)),
            weight_scr[0:8, LANES * c : LANES * (c + 1)],
            weight_scr[8:16, LANES * c : LANES * (c + 1)],
        )
        main = jnp.where(pair < 2, h02, -h11)
        off = jnp.where(pair < 2, -h01, h12)
        first = ROWS * (TILE_LOCAL + c)
        out_ref[first : first + ROWS, :] = jnp.where(sub < 4, main, off)
        from_table.append(jnp.where(sub < 2, h00, jnp.where(sub < 4, h01, h11)))
        to_table.append(jnp.where(sub < 2, h22, jnp.where(sub < 4, -h12, h11)))

    next_ft = [tall(n).astype(jnp.int32) for n in next_f]
    next_tt = [tall(n).astype(jnp.int32) for n in next_t]

    def add_rank(_, carry):
        acc, at_f, at_t = carry
        acc = tuple(
            acc[h] + take_chunks(from_table, at_f[h]) + take_chunks(to_table, at_t[h])
            for h in range(2)
        )
        at_f = tuple(take_chunks(next_ft, at_f[h]) for h in range(2))
        at_t = tuple(take_chunks(next_tt, at_t[h]) for h in range(2))
        return acc, at_f, at_t

    zero = jnp.zeros((ROWS, LANES), jnp.float32)
    acc, _, _ = lax.fori_loop(
        0,
        degree.astype(jnp.int32),
        add_rank,
        (
            (zero, zero),
            tuple(tall(x).astype(jnp.int32) for x in head_f),
            tuple(tall(x).astype(jnp.int32) for x in head_t),
        ),
    )

    for h in range(2):
        below = vm[h] - volt_low
        above = volt_high - vm[h]
        barrier = barrier_weight / (below * below) + barrier_weight / (above * above)
        diag_vv = pltpu.roll(acc[h], 4, 0) + barrier + gens[h]
        diag_aa = pltpu.roll(acc[h], 2, 0) + angle_reg + gens[h]
        diag_va = pltpu.roll(acc[h], 6, 0)
        first = ROWS * (TILE_A + h)
        out_ref[first : first + ROWS, :] = jnp.where(
            sub < 4, grad[h], jnp.where(sub < 6, diag_vv, diag_aa)
        )
        first = ROWS * (TILE_B + h)
        out_ref[first : first + ROWS, :] = jnp.where(
            sub < 2, diag_va, jnp.where(sub < 4, vm[h], jnp.where(sub < 6, cosv[h], sinv[h]))
        )
        first = ROWS * (TILE_C + h)
        out_ref[first : first + ROWS, :] = jnp.where(sub == 6, degree, cross[h])
    first = ROWS * TILE_INDEX
    for offset, value in enumerate(pos_f + pos_t + head_f + head_t + next_f + next_t):
        out_ref[first + offset : first + offset + 1, :] = value


def solve_kernel(me_ref, pos_ref, all_ref, step_ref, residual_ref, chain_scr, step_scr, residual_scr):
    blocks = all_ref.shape[0]
    half = blocks // 2
    bus_count = step_ref.shape[2]
    lane_pairs = [(j, h) for j in range(half) for h in range(2)]
    sub = iota((ROWS, LANES), 0)
    low = sub < 4
    even = (sub & 3) < 2

    def swap_component(x):
        return jnp.where(even, pltpu.roll(x, 6, 0), pltpu.roll(x, 2, 0))

    def swap_block(x):
        return pltpu.roll(x, 4, 0)

    def halves(tile, j):
        first = all_ref[j, ROWS * tile : ROWS * (tile + 1), :]
        second = all_ref[j + half, ROWS * tile : ROWS * (tile + 1), :]
        return (
            jnp.where(low, first, swap_block(second)),
            jnp.where(low, swap_block(first), second),
        )

    def quarters(x):
        return (
            jnp.where(even, x, pltpu.roll(x, 2, 0)),
            jnp.where(even, pltpu.roll(x, 6, 0), x),
        )

    def single(number, j):
        return jnp.where(
            low,
            tall(all_ref[j, number : number + 1, :]),
            tall(all_ref[j + half, number : number + 1, :]),
        )

    def single_index(number, j):
        return single(number, j).astype(jnp.int32)

    def across(field):
        out = {}
        for j in range(half):
            out[j, 1] = field[j + 1, 0] if j + 1 < half else swap_block(field[0, 0])
            out[j, 0] = field[j - 1, 1] if j > 0 else swap_block(field[half - 1, 1])
        return out

    gradient, diag, diag_off = {}, {}, {}
    vm, cosv, sinv, wp, wq, g, b = ({} for _ in range(7))
    for j, h in lane_pairs:
        key = (j, h)
        gradient[key], diag[key] = halves(TILE_A + h, j)
        first, second = halves(TILE_B + h, j)
        diag_off[key], vm[key] = quarters(first)
        cosv[key], sinv[key] = quarters(second)
        first, _ = halves(TILE_C + h, j)
        wp[key], wq[key] = quarters(first)
        g[key] = single(ROWS * (TILE_C + h) + 4, j)
        b[key] = single(ROWS * (TILE_C + h) + 5, j)

    vm_to, cos_to, sin_to = across(vm), across(cosv), across(sinv)
    to_diag, to_off, main, off = {}, {}, {}, {}
    for key in lane_pairs:
        h00, h01, h11, h22, h12, h02 = block_entries(
            vm[key],
            cosv[key],
            sinv[key],
            vm_to[key],
            cos_to[key],
            sin_to[key],
            g[key],
            b[key],
            wp[key],
            wq[key],
        )
        diag[key] = diag[key] + jnp.where(even, h00, h11)
        diag_off[key] = diag_off[key] + h01
        to_diag[key] = jnp.where(even, h22, h11)
        to_off[key] = -h12
        main[key] = jnp.where(even, h02, -h11)
        off[key] = jnp.where(even, -h01, h12)
    to_diag, to_off = across(to_diag), across(to_off)
    main_to = across(main)
    off_to = across({key: swap_component(off[key]) for key in lane_pairs})
    inverse, inverse_off = {}, {}
    for key in lane_pairs:
        diag[key] = diag[key] + to_diag[key]
        diag_off[key] = diag_off[key] + to_off[key]
        main[key] = main[key] + main_to[key]
        off[key] = off[key] + off_to[key]
        flipped = swap_component(diag[key])
        determinant = diag[key] * flipped - diag_off[key] * diag_off[key]
        inverse[key] = flipped / determinant
        inverse_off[key] = -diag_off[key] / determinant

    local_main, local_off, at_from, at_to = {}, {}, {}, {}
    next_f, next_t, head_f, head_t = {}, {}, {}, {}
    base = ROWS * TILE_INDEX
    for j in range(half):
        for c in range(3):
            local_main[j, c], local_off[j, c] = halves(TILE_LOCAL + c, j)
            at_from[j, c] = single_index(base + c, j)
            at_to[j, c] = single_index(base + 3 + c, j)
            next_f[j, c] = single_index(base + 10 + c, j)
            next_t[j, c] = single_index(base + 13 + c, j)
        for h in range(2):
            head_f[j, h] = single_index(base + 6 + h, j)
            head_t[j, h] = single_index(base + 8 + h, j)
    number = ROWS * TILE_C + 6
    degrees = functools.reduce(
        jnp.maximum, [all_ref[p, number : number + 1, :] for p in range(blocks)]
    )
    degree = jnp.max(degrees).astype(jnp.int32)

    def follow(rank, carry):
        ends_f, ends_t = carry
        new_f, new_t = [], []
        for number, (j, h) in enumerate(lane_pairs):
            chain_scr[rank, 2 * number] = ends_f[number]
            chain_scr[rank, 2 * number + 1] = ends_t[number]
            new_f.append(take_chunks([next_f[j, c] for c in range(3)], ends_f[number]))
            new_t.append(take_chunks([next_t[j, c] for c in range(3)], ends_t[number]))
        return tuple(new_f), tuple(new_t)

    lax.fori_loop(
        0,
        degree,
        follow,
        (tuple(head_f[key] for key in lane_pairs), tuple(head_t[key] for key in lane_pairs)),
    )

    def operator(v):
        flipped = {key: swap_component(v[key]) for key in lane_pairs}
        v_to, flipped_to = across(v), across(flipped)
        out = {
            key: diag[key] * v[key]
            + diag_off[key] * flipped[key]
            + main[key] * v_to[key]
            + off[key] * flipped_to[key]
            for key in lane_pairs
        }
        to_from, to_to = {}, {}
        for j in range(half):
            table = [v[j, 0], v[j, 1]]
            for c in range(3):
                far = take_chunks(table, at_to[j, c])
                near = take_chunks(table, at_from[j, c])
                to_from[j, c] = local_main[j, c] * far + local_off[j, c] * swap_component(far)
                to_to[j, c] = local_main[j, c] * near + swap_component(local_off[j, c] * near)

        def add_rank(rank, sums):
            new = []
            for number, (j, h) in enumerate(lane_pairs):
                new.append(
                    sums[number]
                    + take_chunks([to_from[j, c] for c in range(3)], chain_scr[rank, 2 * number])
                    + take_chunks([to_to[j, c] for c in range(3)], chain_scr[rank, 2 * number + 1])
                )
            return tuple(new)

        sums = lax.fori_loop(0, degree, add_rank, tuple(out[key] for key in lane_pairs))
        return dict(zip(lane_pairs, sums))

    def scenario_total(left, right):
        total = functools.reduce(jnp.add, [left[key] * right[key] for key in lane_pairs])
        total = total + pltpu.roll(total, 2, 0)
        total = total + pltpu.roll(total, 4, 0)
        return jnp.broadcast_to(jnp.sum(total, axis=1, keepdims=True), (ROWS, LANES))

    def precondition(v):
        return {
            key: inverse[key] * v[key] + inverse_off[key] * swap_component(v[key])
            for key in lane_pairs
        }

    residual = gradient
    search = precondition(residual)
    energy = scenario_total(residual, search)
    update = None
    for iteration in range(ITERS):
        image = operator(search)
        step_size = energy / scenario_total(search, image)
        if update is None:
            update = {key: step_size * search[key] for key in lane_pairs}
        else:
            update = {key: update[key] + step_size * search[key] for key in lane_pairs}
        residual = {key: residual[key] - step_size * image[key] for key in lane_pairs}
        if iteration + 1 < ITERS:
            scaled = precondition(residual)
            energy_next = scenario_total(residual, scaled)
            ratio = energy_next / energy
            search = {key: scaled[key] + ratio * search[key] for key in lane_pairs}
            energy = energy_next

    me = me_ref[0]
    upper = me >= half
    mine = jnp.where(upper, me - half, me)
    for field, keep_scr, out_ref in (
        (update, step_scr, step_ref),
        (residual, residual_scr, residual_ref),
    ):
        for j, h in lane_pairs:
            keep_scr[j, h] = field[j, h]
        own = []
        for h in range(2):
            tile = keep_scr[mine, h]
            own.append(jnp.where(upper, swap_block(tile), tile))
        for m in range(2):
            width = min(LANES, bus_count - LANES * m)
            values = take_chunks(own, tall(pos_ref[m : m + 1, :]))
            for comp in range(2):
                out_ref[comp, :, LANES * m : LANES * m + width] = values[
                    2 * comp : 2 * comp + 2, :width
                ]


def fast_body(
    volt_mag,
    volt_ang,
    gradient,
    branch_from,
    branch_to,
    branch_count,
    boundary,
    conductance,
    susceptance,
    duals,
    slacks,
    gen_bus,
    gen_curvature,
):
    bus_count = volt_mag.shape[0]
    slot_count = branch_from.shape[0]
    blocks = lax.axis_size("net")
    vmem = pl.BlockSpec(memory_space=pltpu.VMEM)
    smem = pl.BlockSpec(memory_space=pltpu.SMEM)
    payload, position = pl.pallas_call(
        prepare_kernel,
        out_shape=(
            jax.ShapeDtypeStruct((PAYLOAD_ROWS, LANES), jnp.float32),
            jax.ShapeDtypeStruct((2, LANES), jnp.int32),
        ),
        in_specs=[vmem] * 5 + [smem] + [vmem] * 7,
        out_specs=(vmem, vmem),
        scratch_shapes=[
            pltpu.VMEM((24, 2 * LANES), jnp.float32),
            pltpu.VMEM((16, 3 * LANES), jnp.float32),
            pltpu.VMEM((8, 3 * LANES), jnp.float32),
            pltpu.VMEM((8, 3 * LANES), jnp.int32),
        ],
        name="prepare",
    )(
        volt_mag.T,
        volt_ang.T,
        jnp.transpose(gradient, (1, 2, 0)),
        branch_from[None],
        branch_to[None],
        branch_count,
        boundary[None],
        conductance[None],
        susceptance[None],
        jnp.transpose(duals, (0, 2, 1)),
        jnp.transpose(slacks, (0, 2, 1)),
        gen_bus[None],
        gen_curvature[None],
    )
    gathered = lax.all_gather(payload, "net")
    me = lax.axis_index("net").astype(jnp.int32)[None]
    field = jax.ShapeDtypeStruct((2, 2, bus_count), jnp.float32)
    tile_pairs = (blocks // 2, 2, ROWS, LANES)
    step, residual = pl.pallas_call(
        solve_kernel,
        out_shape=(field, field),
        in_specs=[smem, vmem, vmem],
        out_specs=(vmem, vmem),
        scratch_shapes=[
            pltpu.VMEM((slot_count, 2 * blocks, ROWS, LANES), jnp.int32),
            pltpu.VMEM(tile_pairs, jnp.float32),
            pltpu.VMEM(tile_pairs, jnp.float32),
        ],
        compiler_params=pltpu.CompilerParams(vmem_limit_bytes=40 * 2**20),
        name="solve",
    )(me, position, gathered)
    return jnp.transpose(step, (2, 0, 1)), jnp.transpose(residual, (2, 0, 1))


def any_body(*arrays):
    volt_mag, boundary, branch_from, gen_bus = arrays[0], arrays[6], arrays[3], arrays[11]
    fast = fits_fast_path(
        lax.axis_size("net"),
        volt_mag.shape[0],
        boundary.shape[0] // 2,
        branch_from.shape[0],
        gen_bus.shape[0],
        volt_mag.shape[1],
    )
    return fast_body(*arrays) if fast else body(*arrays)


def solution(mesh):
    placed = (
        P("net", "scen"),
        P("net", "scen"),
        P("net", None, "scen"),
        P("net"),
        P("net"),
        P("net"),
        P("net"),
        P("net"),
        P("net"),
        P(None, "net", "scen"),
        P(None, "net", "scen"),
        P("net"),
        P("net"),
    )
    return jax.shard_map(
        any_body,
        mesh=mesh,
        in_specs=placed,
        out_specs=(P("net", None, "scen"), P("net", None, "scen")),
        check_vma=False,
    )
```

```python
import functools

import jax
import jax.numpy as jnp
from jax import lax
from jax.experimental import pallas as pl
from jax.experimental.pallas import tpu as pltpu
from jax.sharding import PartitionSpec as P

ITERS = 4


barrier_weight = 0.01
volt_low = 0.9
volt_high = 1.1
angle_reg = 0.5


def shifted(array, axis, by):
    peers = lax.axis_size(axis)
    pairs = [(i, i + by) for i in range(peers) if 0 <= i + by < peers]
    return lax.ppermute(array, axis, pairs)


def branch_blocks(
    magnitude_from,
    angle_from,
    magnitude_to,
    angle_to,
    conduct,
    suscept,
    weight_active,
    weight_reactive,
):
    angle_diff = angle_from - angle_to
    cosine_diff = jnp.cos(angle_diff)
    sine_diff = jnp.sin(angle_diff)
    flow_along = conduct * cosine_diff + suscept * sine_diff
    flow_across = conduct * sine_diff - suscept * cosine_diff
    cross_term = magnitude_from * magnitude_to
    active_rows = (
        2.0 * conduct * magnitude_from - magnitude_to * flow_along,
        cross_term * flow_across,
        -magnitude_from * flow_along,
        -cross_term * flow_across,
    )
    reactive_rows = (
        -2.0 * suscept * magnitude_from - magnitude_to * flow_across,
        -cross_term * flow_along,
        -magnitude_from * flow_across,
        cross_term * flow_along,
    )

    def block_entry(left_index, right_index):
        return (
            weight_active * active_rows[left_index] * active_rows[right_index]
            + weight_reactive * reactive_rows[left_index] * reactive_rows[right_index]
        )

    from_block = jnp.stack([block_entry(0, 0), block_entry(0, 1), block_entry(1, 1)], axis=1)
    to_block = jnp.stack([block_entry(2, 2), block_entry(2, 3), block_entry(3, 3)], axis=1)
    cross_block = jnp.stack(
        [block_entry(0, 2), block_entry(0, 3), block_entry(1, 2), block_entry(1, 3)], axis=1
    )
    return (from_block, to_block, cross_block)


def apply_cross(matrix_block, vector):
    return jnp.stack(
        [
            matrix_block[:, 0] * vector[:, 0] + matrix_block[:, 1] * vector[:, 1],
            matrix_block[:, 2] * vector[:, 0] + matrix_block[:, 3] * vector[:, 1],
        ],
        axis=1,
    )


def apply_cross_transposed(matrix_block, vector):
    return jnp.stack(
        [
            matrix_block[:, 0] * vector[:, 0] + matrix_block[:, 2] * vector[:, 1],
            matrix_block[:, 1] * vector[:, 0] + matrix_block[:, 3] * vector[:, 1],
        ],
        axis=1,
    )


def scenario_sum(left_vec, right_vec):
    return jnp.sum(left_vec * right_vec, axis=(0, 1))


def widen(values):
    return values[None, None, :]


def body(
    volt_mag,
    volt_ang,
    gradient,
    branch_from,
    branch_to,
    branch_count,
    boundary,
    conductance,
    susceptance,
    duals,
    slacks,
    gen_bus,
    gen_curvature,
):
    bus_count = volt_mag.shape[0]
    ghost_count = boundary.shape[0] // 2
    extended_size = bus_count + 2 * ghost_count
    slot_count = branch_from.shape[0]
    left_list = boundary[:ghost_count]
    right_list = boundary[ghost_count:]
    left_ghost = slice(bus_count, bus_count + ghost_count)
    right_ghost = slice(bus_count + ghost_count, extended_size)
    return_plan = (
        (-1, left_ghost, right_list, right_ghost),
        (1, right_ghost, left_list, left_ghost),
    )

    def share_vector(values):
        pieces = [values]
        for direction in (1, -1):
            outgoing = jnp.take(values, right_list if direction == 1 else left_list, axis=0)
            pieces.append(shifted(outgoing, "net", direction))
        return jnp.concatenate(pieces, axis=0)

    bus_state = jnp.stack([volt_mag, volt_ang], axis=1)
    pieces = [bus_state]
    for share_direction in (1, -1):
        outgoing = jnp.take(bus_state, right_list if share_direction == 1 else left_list, axis=0)
        pieces.append(shifted(outgoing, "net", share_direction))
    extended_state = jnp.concatenate(pieces, axis=0)
    from_state = jnp.take(extended_state, branch_from, axis=0)
    to_state = jnp.take(extended_state, branch_to, axis=0)
    live_mask = (jnp.arange(slot_count) < branch_count[0]).astype(jnp.float32)[:, None]
    weight_active = live_mask * duals[0] / slacks[0]
    weight_reactive = live_mask * duals[1] / slacks[1]
    from_block, to_block, cross_block = branch_blocks(
        from_state[:, 0],
        from_state[:, 1],
        to_state[:, 0],
        to_state[:, 1],
        conductance[:, None],
        susceptance[:, None],
        weight_active,
        weight_reactive,
    )
    diag_extended = jax.ops.segment_sum(
        from_block, branch_from, num_segments=extended_size
    ) + jax.ops.segment_sum(to_block, branch_to, num_segments=extended_size)
    diag_local = diag_extended[:bus_count]
    for direction, ghost_rows, target_rows, source_rows in return_plan:
        arrived_diag = shifted(diag_extended[ghost_rows], "net", direction)
        diag_local = diag_local.at[target_rows].add(arrived_diag)
    gen_table = (gen_bus[None, :] == jnp.arange(bus_count)[:, None]).astype(jnp.float32)
    gen_sum = jnp.dot(gen_table, gen_curvature, precision=lax.Precision.HIGHEST)[:, None]
    barrier = barrier_weight / jnp.square(volt_mag - volt_low) + barrier_weight / jnp.square(
        volt_high - volt_mag
    )
    diag_vv = diag_local[:, 0] + barrier + gen_sum
    diag_va = diag_local[:, 1]
    diag_aa = diag_local[:, 2] + angle_reg + gen_sum
    determinant = diag_vv * diag_aa - diag_va * diag_va
    inverse_vv = diag_aa / determinant
    inverse_va = -diag_va / determinant
    inverse_aa = diag_vv / determinant

    def precondition(vector):
        return jnp.stack(
            [
                inverse_vv * vector[:, 0] + inverse_va * vector[:, 1],
                inverse_va * vector[:, 0] + inverse_aa * vector[:, 1],
            ],
            axis=1,
        )

    update_field = jnp.zeros_like(gradient)
    residual = gradient

    def energy_of(residual_now, scaled_now):
        return lax.psum(scenario_sum(residual_now, scaled_now), "net")

    scaled = precondition(residual)
    search = scaled
    energy = energy_of(residual, scaled)
    for iteration in range(ITERS):
        extended = share_vector(search)
        from_values = jnp.take(extended, branch_from, axis=0)
        to_values = jnp.take(extended, branch_to, axis=0)
        from_terms = apply_cross(cross_block, to_values)
        to_terms = apply_cross_transposed(cross_block, from_values)
        result = jnp.stack(
            [
                diag_vv * search[:, 0] + diag_va * search[:, 1],
                diag_va * search[:, 0] + diag_aa * search[:, 1],
            ],
            axis=1,
        )
        summed = jax.ops.segment_sum(
            from_terms, branch_from, num_segments=extended_size
        ) + jax.ops.segment_sum(to_terms, branch_to, num_segments=extended_size)
        local_sum = result + summed[:bus_count]
        for apply_direction, apply_ghost_rows, apply_target_rows, apply_source_rows in return_plan:
            arrived = shifted(summed[apply_ghost_rows], "net", apply_direction)
            local_sum = local_sum.at[apply_target_rows].add(arrived)
        step_size = energy / lax.psum(scenario_sum(search, local_sum), "net")
        update_field = update_field + widen(step_size) * search
        residual = residual - widen(step_size) * local_sum
        if iteration + 1 < ITERS:
            scaled = precondition(residual)
            energy_next = energy_of(residual, scaled)
            search = scaled + widen(energy_next / energy) * search
            energy = energy_next
    return (update_field, residual)


LANES = 128
ROWS = 8
TILE_A, TILE_B, TILE_C = 0, 2, 4
TILE_LOCAL = 6
TILE_INDEX = 9
PAYLOAD_ROWS = 11 * ROWS


def fits_fast_path(blocks, bus_count, ghost_count, slot_count, gen_count, scen_count):
    return (
        blocks == 8
        and scen_count == 2
        and bus_count == 2 * ghost_count
        and ghost_count <= LANES
        and 2 * LANES < slot_count < 3 * LANES
        and gen_count <= LANES
    )


def iota(shape, dim):
    return lax.broadcasted_iota(jnp.int32, shape, dim)


def lane_take(table, index):
    return jnp.take_along_axis(table, index, axis=1, mode="promise_in_bounds")


def take_chunks(tables, index):
    lane = index & (LANES - 1)
    chunk = index >> 7
    out = lane_take(tables[0], lane)
    for number in range(1, len(tables)):
        out = jnp.where(chunk == number, lane_take(tables[number], lane), out)
    return out


def tall(row):
    return jnp.broadcast_to(row, (ROWS, LANES))


def column(row):
    return jnp.transpose(jnp.broadcast_to(row, (LANES, LANES)))


def block_entries(vi, ci, si, vj, cj, sj, g, b, wp, wq):
    cosine = ci * cj + si * sj
    sine = si * cj - ci * sj
    along = g * cosine + b * sine
    across = g * sine - b * cosine
    cross = vi * vj
    p0 = 2.0 * g * vi - vj * along
    p1 = cross * across
    p2 = -vi * along
    q0 = -2.0 * b * vi - vj * across
    q1 = -cross * along
    q2 = -vi * across

    def entry(pa, pb, qa, qb):
        return wp * pa * pb + wq * qa * qb

    return (
        entry(p0, p0, q0, q0),
        entry(p0, p1, q0, q1),
        entry(p1, p1, q1, q1),
        entry(p2, p2, q2, q2),
        entry(p1, p2, q1, q2),
        entry(p0, p2, q0, q2),
    )


def prepare_kernel(
    vm_ref,
    va_ref,
    grad_ref,
    from_ref,
    to_ref,
    count_ref,
    bound_ref,
    g_ref,
    b_ref,
    duals_ref,
    slacks_ref,
    gen_bus_ref,
    gen_curv_ref,
    out_ref,
    pos_ref,
    bus_scr,
    weight_scr,
    branch_scr,
    index_scr,
):
    bus_count = vm_ref.shape[1]
    ghost_count = bus_count // 2
    slot_count = from_ref.shape[0]
    gen_count = gen_bus_ref.shape[0]
    none = 3 * LANES - 1
    live_count = count_ref[0]

    bus_scr[...] = jnp.zeros_like(bus_scr)
    weight_scr[...] = jnp.zeros_like(weight_scr)
    branch_scr[...] = jnp.zeros_like(branch_scr)
    index_scr[...] = jnp.full_like(index_scr, -9)
    for copy in range(4):
        bus_scr[2 * copy : 2 * copy + 2, :bus_count] = vm_ref[...]
        bus_scr[8 + 2 * copy : 10 + 2 * copy, :bus_count] = va_ref[...]
    for comp in range(2):
        bus_scr[16 + 2 * comp : 18 + 2 * comp, :bus_count] = grad_ref[comp]
    live = iota((2, slot_count), 1) < live_count
    for kind in range(2):
        weight = jnp.where(live, duals_ref[kind] / slacks_ref[kind], 0.0)
        for copy in range(4):
            weight_scr[8 * kind + 2 * copy : 8 * kind + 2 * copy + 2, :slot_count] = weight
        branch_scr[2 * kind : 2 * kind + 2, :slot_count] = weight
    branch_scr[4:5, :slot_count] = g_ref[...][None]
    branch_scr[5:6, :slot_count] = b_ref[...][None]
    branch_scr[6:7, :gen_count] = gen_curv_ref[...][None]
    index_scr[0:1, :slot_count] = from_ref[...][None]
    index_scr[1:2, :slot_count] = to_ref[...][None]
    index_scr[2:3, :bus_count] = bound_ref[...][None]
    index_scr[3:4, :gen_count] = gen_bus_ref[...][None]

    def tiles(ref, first, chunks):
        return [ref[first : first + ROWS, LANES * c : LANES * (c + 1)] for c in range(chunks)]

    def row(ref, number, chunk):
        return ref[number : number + 1, LANES * chunk : LANES * (chunk + 1)]

    lane = iota((ROWS, LANES), 1)
    sub = iota((ROWS, LANES), 0)
    lane_row = iota((1, LANES), 1)
    sub_col = iota((LANES, LANES), 0).astype(jnp.float32)
    inside = lane < ghost_count

    raw_bound = [tall(row(index_scr, 2, c)) for c in range(2)]
    bound = [jnp.where(inside, take_chunks(raw_bound, lane + h * ghost_count), -1) for h in range(2)]
    fetch = [jnp.maximum(b, 0) for b in bound]
    bound_row = [b[0:1].astype(jnp.float32) for b in bound]
    vm_raw, va_raw, grad_raw = (tiles(bus_scr, 8 * f, 2) for f in range(3))
    vm = [jnp.where(inside, take_chunks(vm_raw, f), 1.0) for f in fetch]
    va = [jnp.where(inside, take_chunks(va_raw, f), 0.0) for f in fetch]
    grad = [jnp.where(inside, take_chunks(grad_raw, f), 0.0) for f in fetch]
    cosv = [jnp.cos(a) for a in va]
    sinv = [jnp.sin(a) for a in va]

    from_key, to_key = [], []
    for c in range(3):
        slot = lane_row + LANES * c
        alive = (slot < live_count) & (slot < slot_count)
        to_raw = row(index_scr, 1, c)
        from_key.append(
            jnp.where(alive & (to_raw < bus_count), row(index_scr, 0, c), 9998).astype(jnp.float32)
        )
        to_key.append(jnp.where(alive, to_raw, 9999).astype(jnp.float32))
    from_col = [column(k) for k in from_key]
    to_col = [column(k) for k in to_key]
    bound_col = [column(b) for b in bound_row]
    gen_col = column(row(index_scr, 3, 0).astype(jnp.float32))
    curv_col = column(row(branch_scr, 6, 0))

    def lowest(masks):
        found = functools.reduce(
            jnp.minimum,
            [jnp.where(m, sub_col + float(LANES * c), float(none)) for c, m in masks],
        )
        return jnp.min(found, axis=0, keepdims=True)

    def links(keys, cols):
        heads, counts = [], []
        for h in range(2):
            equal = [cols[c] == bound_row[h] for c in range(3)]
            heads.append(lowest(list(enumerate(equal))))
            counts.append(
                jnp.sum(
                    functools.reduce(jnp.add, [jnp.where(e, 1.0, 0.0) for e in equal]),
                    axis=0,
                    keepdims=True,
                )
            )
        nexts = []
        for c in range(3):
            later = [(c, (cols[c] == keys[c]) & (sub_col > lane_row.astype(jnp.float32)))]
            later += [(d, cols[d] == keys[c]) for d in range(c + 1, 3)]
            nexts.append(lowest(later))
        return heads, nexts, jnp.maximum(counts[0], counts[1])

    head_f, next_f, count_f = links(from_key, from_col)
    head_t, next_t, count_t = links(to_key, to_col)
    degree = jnp.max(jnp.maximum(count_f, count_t))

    def position(keys):
        found = [
            jnp.where(bound_col[h] == keys, sub_col + float(LANES * h), 0.0) for h in range(2)
        ]
        return jnp.max(jnp.maximum(found[0], found[1]), axis=0, keepdims=True)

    pos_f = [position(k) for k in from_key]
    pos_t = [position(k) for k in to_key]
    for m in range(2):
        pos_ref[m : m + 1, :] = position((lane_row + LANES * m).astype(jnp.float32)).astype(jnp.int32)

    branch_tiles = tiles(branch_scr, 0, 3)
    cross = []
    for h in range(2):
        target = jnp.where(lane_row < ghost_count, bus_count + h * ghost_count + lane_row, -5)
        slot = lowest([(c, to_col[c] == target.astype(jnp.float32)) for c in range(2)])
        cross.append(take_chunks(branch_tiles, tall(slot).astype(jnp.int32)))

    gens = [
        jnp.sum(jnp.where(gen_col == bound_row[h], curv_col, 0.0), axis=0, keepdims=True)
        for h in range(2)
    ]

    pair = sub & 3
    from_table, to_table = [], []
    for c in range(3):
        at_f = tall(pos_f[c]).astype(jnp.int32)
        at_t = tall(pos_t[c]).astype(jnp.int32)
        h00, h01, h11, h22, h12, h02 = block_entries(
            *(take_chunks(t, at_f) for t in (vm, cosv, sinv)),
            *(take_chunks(t, at_t) for t in (vm, cosv, sinv)),
            tall(row(branch_scr, 4, c)),
            tall(row(branch_scr, 5, c)),
            weight_scr[0:8, LANES * c : LANES * (c + 1)],
            weight_scr[8:16, LANES * c : LANES * (c + 1)],
        )
        main = jnp.where(pair < 2, h02, -h11)
        off = jnp.where(pair < 2, -h01, h12)
        first = ROWS * (TILE_LOCAL + c)
        out_ref[first : first + ROWS, :] = jnp.where(sub < 4, main, off)
        from_table.append(jnp.where(sub < 2, h00, jnp.where(sub < 4, h01, h11)))
        to_table.append(jnp.where(sub < 2, h22, jnp.where(sub < 4, -h12, h11)))

    next_ft = [tall(n).astype(jnp.int32) for n in next_f]
    next_tt = [tall(n).astype(jnp.int32) for n in next_t]

    def add_rank(_, carry):
        acc, at_f, at_t = carry
        acc = tuple(
            acc[h] + take_chunks(from_table, at_f[h]) + take_chunks(to_table, at_t[h])
            for h in range(2)
        )
        at_f = tuple(take_chunks(next_ft, at_f[h]) for h in range(2))
        at_t = tuple(take_chunks(next_tt, at_t[h]) for h in range(2))
        return acc, at_f, at_t

    zero = jnp.zeros((ROWS, LANES), jnp.float32)
    acc, _, _ = lax.fori_loop(
        0,
        degree.astype(jnp.int32),
        add_rank,
        (
            (zero, zero),
            tuple(tall(x).astype(jnp.int32) for x in head_f),
            tuple(tall(x).astype(jnp.int32) for x in head_t),
        ),
    )

    for h in range(2):
        below = vm[h] - volt_low
        above = volt_high - vm[h]
        barrier = barrier_weight / (below * below) + barrier_weight / (above * above)
        diag_vv = pltpu.roll(acc[h], 4, 0) + barrier + gens[h]
        diag_aa = pltpu.roll(acc[h], 2, 0) + angle_reg + gens[h]
        diag_va = pltpu.roll(acc[h], 6, 0)
        first = ROWS * (TILE_A + h)
        out_ref[first : first + ROWS, :] = jnp.where(
            sub < 4, grad[h], jnp.where(sub < 6, diag_vv, diag_aa)
        )
        first = ROWS * (TILE_B + h)
        out_ref[first : first + ROWS, :] = jnp.where(
            sub < 2, diag_va, jnp.where(sub < 4, vm[h], jnp.where(sub < 6, cosv[h], sinv[h]))
        )
        first = ROWS * (TILE_C + h)
        out_ref[first : first + ROWS, :] = jnp.where(sub == 6, degree, cross[h])
    first = ROWS * TILE_INDEX
    for offset, value in enumerate(pos_f + pos_t + head_f + head_t + next_f + next_t):
        out_ref[first + offset : first + offset + 1, :] = value


def solve_kernel(pos_ref, *refs):
    *all_refs, step_ref, residual_ref, chain_scr = refs
    blocks = len(all_refs)
    half = blocks // 2
    bus_count = step_ref.shape[2]
    lane_pairs = [(j, h) for j in range(half) for h in range(2)]
    sub = iota((ROWS, LANES), 0)
    low = sub < 4
    even = (sub & 3) < 2

    def swap_component(x):
        return jnp.where(even, pltpu.roll(x, 6, 0), pltpu.roll(x, 2, 0))

    def swap_block(x):
        return pltpu.roll(x, 4, 0)

    def halves(tile, j):
        first = all_refs[j][ROWS * tile : ROWS * (tile + 1), :]
        second = all_refs[j + half][ROWS * tile : ROWS * (tile + 1), :]
        return (
            jnp.where(low, first, swap_block(second)),
            jnp.where(low, swap_block(first), second),
        )

    def quarters(x):
        return (
            jnp.where(even, x, pltpu.roll(x, 2, 0)),
            jnp.where(even, pltpu.roll(x, 6, 0), x),
        )

    def single(number, j):
        return jnp.where(
            low,
            tall(all_refs[j][number : number + 1, :]),
            tall(all_refs[j + half][number : number + 1, :]),
        )

    def single_index(number, j):
        return single(number, j).astype(jnp.int32)

    def across(field):
        out = {}
        for j in range(half):
            out[j, 1] = field[j + 1, 0] if j + 1 < half else swap_block(field[0, 0])
            out[j, 0] = field[j - 1, 1] if j > 0 else swap_block(field[half - 1, 1])
        return out

    gradient, diag, diag_off = {}, {}, {}
    vm, cosv, sinv, wp, wq, g, b = ({} for _ in range(7))
    for j, h in lane_pairs:
        key = (j, h)
        gradient[key], diag[key] = halves(TILE_A + h, j)
        first, second = halves(TILE_B + h, j)
        diag_off[key], vm[key] = quarters(first)
        cosv[key], sinv[key] = quarters(second)
        first, _ = halves(TILE_C + h, j)
        wp[key], wq[key] = quarters(first)
        g[key] = single(ROWS * (TILE_C + h) + 4, j)
        b[key] = single(ROWS * (TILE_C + h) + 5, j)

    vm_to, cos_to, sin_to = across(vm), across(cosv), across(sinv)
    to_diag, to_off, main, off = {}, {}, {}, {}
    for key in lane_pairs:
        h00, h01, h11, h22, h12, h02 = block_entries(
            vm[key],
            cosv[key],
            sinv[key],
            vm_to[key],
            cos_to[key],
            sin_to[key],
            g[key],
            b[key],
            wp[key],
            wq[key],
        )
        diag[key] = diag[key] + jnp.where(even, h00, h11)
        diag_off[key] = diag_off[key] + h01
        to_diag[key] = jnp.where(even, h22, h11)
        to_off[key] = -h12
        main[key] = jnp.where(even, h02, -h11)
        off[key] = jnp.where(even, -h01, h12)
    to_diag, to_off = across(to_diag), across(to_off)
    main_to = across(main)
    off_to = across({key: swap_component(off[key]) for key in lane_pairs})
    inverse, inverse_off = {}, {}
    for key in lane_pairs:
        diag[key] = diag[key] + to_diag[key]
        diag_off[key] = diag_off[key] + to_off[key]
        main[key] = main[key] + main_to[key]
        off[key] = off[key] + off_to[key]
        flipped = swap_component(diag[key])
        determinant = diag[key] * flipped - diag_off[key] * diag_off[key]
        inverse[key] = flipped / determinant
        inverse_off[key] = -diag_off[key] / determinant

    local_main, local_off, at_from, at_to = {}, {}, {}, {}
    next_f, next_t, head_f, head_t = {}, {}, {}, {}
    base = ROWS * TILE_INDEX
    for j in range(half):
        for c in range(3):
            local_main[j, c], local_off[j, c] = halves(TILE_LOCAL + c, j)
            at_from[j, c] = single_index(base + c, j)
            at_to[j, c] = single_index(base + 3 + c, j)
            next_f[j, c] = single_index(base + 10 + c, j)
            next_t[j, c] = single_index(base + 13 + c, j)
        for h in range(2):
            head_f[j, h] = single_index(base + 6 + h, j)
            head_t[j, h] = single_index(base + 8 + h, j)
    number = ROWS * TILE_C + 6
    degrees = functools.reduce(
        jnp.maximum, [block[number : number + 1, :] for block in all_refs]
    )
    degree = jnp.max(degrees).astype(jnp.int32)

    def follow(rank, carry):
        ends_f, ends_t = carry
        new_f, new_t = [], []
        for number, (j, h) in enumerate(lane_pairs):
            chain_scr[rank, 2 * number] = ends_f[number]
            chain_scr[rank, 2 * number + 1] = ends_t[number]
            new_f.append(take_chunks([next_f[j, c] for c in range(3)], ends_f[number]))
            new_t.append(take_chunks([next_t[j, c] for c in range(3)], ends_t[number]))
        return tuple(new_f), tuple(new_t)

    lax.fori_loop(
        0,
        degree,
        follow,
        (tuple(head_f[key] for key in lane_pairs), tuple(head_t[key] for key in lane_pairs)),
    )

    def operator(v):
        flipped = {key: swap_component(v[key]) for key in lane_pairs}
        v_to, flipped_to = across(v), across(flipped)
        out = {
            key: diag[key] * v[key]
            + diag_off[key] * flipped[key]
            + main[key] * v_to[key]
            + off[key] * flipped_to[key]
            for key in lane_pairs
        }
        to_from, to_to = {}, {}
        for j in range(half):
            table = [v[j, 0], v[j, 1]]
            for c in range(3):
                far = take_chunks(table, at_to[j, c])
                near = take_chunks(table, at_from[j, c])
                to_from[j, c] = local_main[j, c] * far + local_off[j, c] * swap_component(far)
                to_to[j, c] = local_main[j, c] * near + swap_component(local_off[j, c] * near)

        def add_rank(rank, sums):
            new = []
            for number, (j, h) in enumerate(lane_pairs):
                new.append(
                    sums[number]
                    + take_chunks([to_from[j, c] for c in range(3)], chain_scr[rank, 2 * number])
                    + take_chunks([to_to[j, c] for c in range(3)], chain_scr[rank, 2 * number + 1])
                )
            return tuple(new)

        sums = lax.fori_loop(0, degree, add_rank, tuple(out[key] for key in lane_pairs))
        return dict(zip(lane_pairs, sums))

    def scenario_total(left, right):
        total = functools.reduce(jnp.add, [left[key] * right[key] for key in lane_pairs])
        total = total + pltpu.roll(total, 2, 0)
        total = total + pltpu.roll(total, 4, 0)
        return jnp.broadcast_to(jnp.sum(total, axis=1, keepdims=True), (ROWS, LANES))

    def precondition(v):
        return {
            key: inverse[key] * v[key] + inverse_off[key] * swap_component(v[key])
            for key in lane_pairs
        }

    residual = gradient
    search = precondition(residual)
    energy = scenario_total(residual, search)
    update = None
    for iteration in range(ITERS):
        image = operator(search)
        step_size = energy / scenario_total(search, image)
        if update is None:
            update = {key: step_size * search[key] for key in lane_pairs}
        else:
            update = {key: update[key] + step_size * search[key] for key in lane_pairs}
        residual = {key: residual[key] - step_size * image[key] for key in lane_pairs}
        if iteration + 1 < ITERS:
            scaled = precondition(residual)
            energy_next = scenario_total(residual, scaled)
            ratio = energy_next / energy
            search = {key: scaled[key] + ratio * search[key] for key in lane_pairs}
            energy = energy_next

    for field, out_ref in ((update, step_ref), (residual, residual_ref)):
        own = [field[0, h] for h in range(2)]
        for m in range(2):
            width = min(LANES, bus_count - LANES * m)
            values = take_chunks(own, tall(pos_ref[m : m + 1, :]))
            for comp in range(2):
                out_ref[comp, :, LANES * m : LANES * m + width] = values[
                    2 * comp : 2 * comp + 2, :width
                ]


def fast_body(
    volt_mag,
    volt_ang,
    gradient,
    branch_from,
    branch_to,
    branch_count,
    boundary,
    conductance,
    susceptance,
    duals,
    slacks,
    gen_bus,
    gen_curvature,
):
    bus_count = volt_mag.shape[0]
    slot_count = branch_from.shape[0]
    blocks = lax.axis_size("net")
    vmem = pl.BlockSpec(memory_space=pltpu.VMEM)
    smem = pl.BlockSpec(memory_space=pltpu.SMEM)
    payload, position = pl.pallas_call(
        prepare_kernel,
        out_shape=(
            jax.ShapeDtypeStruct((PAYLOAD_ROWS, LANES), jnp.float32),
            jax.ShapeDtypeStruct((2, LANES), jnp.int32),
        ),
        in_specs=[vmem] * 5 + [smem] + [vmem] * 7,
        out_specs=(vmem, vmem),
        scratch_shapes=[
            pltpu.VMEM((24, 2 * LANES), jnp.float32),
            pltpu.VMEM((16, 3 * LANES), jnp.float32),
            pltpu.VMEM((8, 3 * LANES), jnp.float32),
            pltpu.VMEM((8, 3 * LANES), jnp.int32),
        ],
        name="prepare",
    )(
        volt_mag.T,
        volt_ang.T,
        jnp.transpose(gradient, (1, 2, 0)),
        branch_from,
        branch_to,
        branch_count,
        boundary,
        conductance,
        susceptance,
        jnp.transpose(duals, (0, 2, 1)),
        jnp.transpose(slacks, (0, 2, 1)),
        gen_bus,
        gen_curvature,
    )
    gathered = [payload]
    for shift in range(1, blocks):
        pairs = [((i + shift) % blocks, i) for i in range(blocks)]
        gathered.append(lax.ppermute(payload, "net", pairs))
    field = jax.ShapeDtypeStruct((2, 2, bus_count), jnp.float32)
    step, residual = pl.pallas_call(
        solve_kernel,
        out_shape=(field, field),
        in_specs=[vmem] * (1 + blocks),
        out_specs=(vmem, vmem),
        scratch_shapes=[pltpu.VMEM((slot_count, 2 * blocks, ROWS, LANES), jnp.int32)],
        compiler_params=pltpu.CompilerParams(vmem_limit_bytes=40 * 2**20),
        name="solve",
    )(position, *gathered)
    return jnp.transpose(step, (2, 0, 1)), jnp.transpose(residual, (2, 0, 1))


def any_body(*arrays):
    volt_mag, boundary, branch_from, gen_bus = arrays[0], arrays[6], arrays[3], arrays[11]
    fast = fits_fast_path(
        lax.axis_size("net"),
        volt_mag.shape[0],
        boundary.shape[0] // 2,
        branch_from.shape[0],
        gen_bus.shape[0],
        volt_mag.shape[1],
    )
    return fast_body(*arrays) if fast else body(*arrays)


def solution(mesh):
    placed = (
        P("net", "scen"),
        P("net", "scen"),
        P("net", None, "scen"),
        P("net"),
        P("net"),
        P("net"),
        P("net"),
        P("net"),
        P("net"),
        P(None, "net", "scen"),
        P(None, "net", "scen"),
        P("net"),
        P("net"),
    )
    return jax.shard_map(
        any_body,
        mesh=mesh,
        in_specs=placed,
        out_specs=(P("net", None, "scen"), P("net", None, "scen")),
        check_vma=False,
    )
```

```python
import functools

import jax
import jax.numpy as jnp
from jax import lax
from jax.experimental import pallas as pl
from jax.experimental.pallas import tpu as pltpu
from jax.sharding import PartitionSpec as P

ITERS = 4


barrier_weight = 0.01
volt_low = 0.9
volt_high = 1.1
angle_reg = 0.5


def shifted(array, axis, by):
    peers = lax.axis_size(axis)
    pairs = [(i, i + by) for i in range(peers) if 0 <= i + by < peers]
    return lax.ppermute(array, axis, pairs)


def branch_blocks(
    magnitude_from,
    angle_from,
    magnitude_to,
    angle_to,
    conduct,
    suscept,
    weight_active,
    weight_reactive,
):
    angle_diff = angle_from - angle_to
    cosine_diff = jnp.cos(angle_diff)
    sine_diff = jnp.sin(angle_diff)
    flow_along = conduct * cosine_diff + suscept * sine_diff
    flow_across = conduct * sine_diff - suscept * cosine_diff
    cross_term = magnitude_from * magnitude_to
    active_rows = (
        2.0 * conduct * magnitude_from - magnitude_to * flow_along,
        cross_term * flow_across,
        -magnitude_from * flow_along,
        -cross_term * flow_across,
    )
    reactive_rows = (
        -2.0 * suscept * magnitude_from - magnitude_to * flow_across,
        -cross_term * flow_along,
        -magnitude_from * flow_across,
        cross_term * flow_along,
    )

    def block_entry(left_index, right_index):
        return (
            weight_active * active_rows[left_index] * active_rows[right_index]
            + weight_reactive * reactive_rows[left_index] * reactive_rows[right_index]
        )

    from_block = jnp.stack([block_entry(0, 0), block_entry(0, 1), block_entry(1, 1)], axis=1)
    to_block = jnp.stack([block_entry(2, 2), block_entry(2, 3), block_entry(3, 3)], axis=1)
    cross_block = jnp.stack(
        [block_entry(0, 2), block_entry(0, 3), block_entry(1, 2), block_entry(1, 3)], axis=1
    )
    return (from_block, to_block, cross_block)


def apply_cross(matrix_block, vector):
    return jnp.stack(
        [
            matrix_block[:, 0] * vector[:, 0] + matrix_block[:, 1] * vector[:, 1],
            matrix_block[:, 2] * vector[:, 0] + matrix_block[:, 3] * vector[:, 1],
        ],
        axis=1,
    )


def apply_cross_transposed(matrix_block, vector):
    return jnp.stack(
        [
            matrix_block[:, 0] * vector[:, 0] + matrix_block[:, 2] * vector[:, 1],
            matrix_block[:, 1] * vector[:, 0] + matrix_block[:, 3] * vector[:, 1],
        ],
        axis=1,
    )


def scenario_sum(left_vec, right_vec):
    return jnp.sum(left_vec * right_vec, axis=(0, 1))


def widen(values):
    return values[None, None, :]


def body(
    volt_mag,
    volt_ang,
    gradient,
    branch_from,
    branch_to,
    branch_count,
    boundary,
    conductance,
    susceptance,
    duals,
    slacks,
    gen_bus,
    gen_curvature,
):
    bus_count = volt_mag.shape[0]
    ghost_count = boundary.shape[0] // 2
    extended_size = bus_count + 2 * ghost_count
    slot_count = branch_from.shape[0]
    left_list = boundary[:ghost_count]
    right_list = boundary[ghost_count:]
    left_ghost = slice(bus_count, bus_count + ghost_count)
    right_ghost = slice(bus_count + ghost_count, extended_size)
    return_plan = (
        (-1, left_ghost, right_list, right_ghost),
        (1, right_ghost, left_list, left_ghost),
    )

    def share_vector(values):
        pieces = [values]
        for direction in (1, -1):
            outgoing = jnp.take(values, right_list if direction == 1 else left_list, axis=0)
            pieces.append(shifted(outgoing, "net", direction))
        return jnp.concatenate(pieces, axis=0)

    bus_state = jnp.stack([volt_mag, volt_ang], axis=1)
    pieces = [bus_state]
    for share_direction in (1, -1):
        outgoing = jnp.take(bus_state, right_list if share_direction == 1 else left_list, axis=0)
        pieces.append(shifted(outgoing, "net", share_direction))
    extended_state = jnp.concatenate(pieces, axis=0)
    from_state = jnp.take(extended_state, branch_from, axis=0)
    to_state = jnp.take(extended_state, branch_to, axis=0)
    live_mask = (jnp.arange(slot_count) < branch_count[0]).astype(jnp.float32)[:, None]
    weight_active = live_mask * duals[0] / slacks[0]
    weight_reactive = live_mask * duals[1] / slacks[1]
    from_block, to_block, cross_block = branch_blocks(
        from_state[:, 0],
        from_state[:, 1],
        to_state[:, 0],
        to_state[:, 1],
        conductance[:, None],
        susceptance[:, None],
        weight_active,
        weight_reactive,
    )
    diag_extended = jax.ops.segment_sum(
        from_block, branch_from, num_segments=extended_size
    ) + jax.ops.segment_sum(to_block, branch_to, num_segments=extended_size)
    diag_local = diag_extended[:bus_count]
    for direction, ghost_rows, target_rows, source_rows in return_plan:
        arrived_diag = shifted(diag_extended[ghost_rows], "net", direction)
        diag_local = diag_local.at[target_rows].add(arrived_diag)
    gen_table = (gen_bus[None, :] == jnp.arange(bus_count)[:, None]).astype(jnp.float32)
    gen_sum = jnp.dot(gen_table, gen_curvature, precision=lax.Precision.HIGHEST)[:, None]
    barrier = barrier_weight / jnp.square(volt_mag - volt_low) + barrier_weight / jnp.square(
        volt_high - volt_mag
    )
    diag_vv = diag_local[:, 0] + barrier + gen_sum
    diag_va = diag_local[:, 1]
    diag_aa = diag_local[:, 2] + angle_reg + gen_sum
    determinant = diag_vv * diag_aa - diag_va * diag_va
    inverse_vv = diag_aa / determinant
    inverse_va = -diag_va / determinant
    inverse_aa = diag_vv / determinant

    def precondition(vector):
        return jnp.stack(
            [
                inverse_vv * vector[:, 0] + inverse_va * vector[:, 1],
                inverse_va * vector[:, 0] + inverse_aa * vector[:, 1],
            ],
            axis=1,
        )

    update_field = jnp.zeros_like(gradient)
    residual = gradient

    def energy_of(residual_now, scaled_now):
        return lax.psum(scenario_sum(residual_now, scaled_now), "net")

    scaled = precondition(residual)
    search = scaled
    energy = energy_of(residual, scaled)
    for iteration in range(ITERS):
        extended = share_vector(search)
        from_values = jnp.take(extended, branch_from, axis=0)
        to_values = jnp.take(extended, branch_to, axis=0)
        from_terms = apply_cross(cross_block, to_values)
        to_terms = apply_cross_transposed(cross_block, from_values)
        result = jnp.stack(
            [
                diag_vv * search[:, 0] + diag_va * search[:, 1],
                diag_va * search[:, 0] + diag_aa * search[:, 1],
            ],
            axis=1,
        )
        summed = jax.ops.segment_sum(
            from_terms, branch_from, num_segments=extended_size
        ) + jax.ops.segment_sum(to_terms, branch_to, num_segments=extended_size)
        local_sum = result + summed[:bus_count]
        for apply_direction, apply_ghost_rows, apply_target_rows, apply_source_rows in return_plan:
            arrived = shifted(summed[apply_ghost_rows], "net", apply_direction)
            local_sum = local_sum.at[apply_target_rows].add(arrived)
        step_size = energy / lax.psum(scenario_sum(search, local_sum), "net")
        update_field = update_field + widen(step_size) * search
        residual = residual - widen(step_size) * local_sum
        if iteration + 1 < ITERS:
            scaled = precondition(residual)
            energy_next = energy_of(residual, scaled)
            search = scaled + widen(energy_next / energy) * search
            energy = energy_next
    return (update_field, residual)


LANES = 128
ROWS = 8
TILE_A, TILE_B, TILE_C = 0, 2, 4
TILE_LOCAL = 6
TILE_INDEX = 9
PAYLOAD_ROWS = 11 * ROWS


def fits_fast_path(blocks, bus_count, ghost_count, slot_count, gen_count, scen_count):
    return (
        blocks == 8
        and scen_count == 2
        and bus_count == 2 * ghost_count
        and ghost_count <= LANES
        and 2 * LANES < slot_count < 3 * LANES
        and gen_count <= LANES
    )


def iota(shape, dim):
    return lax.broadcasted_iota(jnp.int32, shape, dim)


def lane_take(table, index):
    return jnp.take_along_axis(table, index, axis=1, mode="promise_in_bounds")


def take_chunks(tables, index):
    lane = index & (LANES - 1)
    chunk = index >> 7
    out = lane_take(tables[0], lane)
    for number in range(1, len(tables)):
        out = jnp.where(chunk == number, lane_take(tables[number], lane), out)
    return out


def tall(row):
    return jnp.broadcast_to(row, (ROWS, LANES))


def column(row):
    return jnp.transpose(jnp.broadcast_to(row, (LANES, LANES)))


def block_entries(vi, ci, si, vj, cj, sj, g, b, wp, wq):
    cosine = ci * cj + si * sj
    sine = si * cj - ci * sj
    along = g * cosine + b * sine
    across = g * sine - b * cosine
    cross = vi * vj
    p0 = 2.0 * g * vi - vj * along
    p1 = cross * across
    p2 = -vi * along
    q0 = -2.0 * b * vi - vj * across
    q1 = -cross * along
    q2 = -vi * across

    def entry(pa, pb, qa, qb):
        return wp * pa * pb + wq * qa * qb

    return (
        entry(p0, p0, q0, q0),
        entry(p0, p1, q0, q1),
        entry(p1, p1, q1, q1),
        entry(p2, p2, q2, q2),
        entry(p1, p2, q1, q2),
        entry(p0, p2, q0, q2),
    )


def prepare_kernel(
    vm_ref,
    va_ref,
    grad_ref,
    from_ref,
    to_ref,
    count_ref,
    bound_ref,
    g_ref,
    b_ref,
    duals_ref,
    slacks_ref,
    gen_bus_ref,
    gen_curv_ref,
    copies_ref,
    pos_ref,
    bus_scr,
    weight_scr,
    branch_scr,
    index_scr,
):
    bus_count = vm_ref.shape[1]
    ghost_count = bus_count // 2
    slot_count = from_ref.shape[0]
    gen_count = gen_bus_ref.shape[0]
    none = 3 * LANES - 1
    out_ref = copies_ref.at[0]
    live_count = count_ref[0]

    bus_scr[...] = jnp.zeros_like(bus_scr)
    weight_scr[...] = jnp.zeros_like(weight_scr)
    branch_scr[...] = jnp.zeros_like(branch_scr)
    index_scr[...] = jnp.full_like(index_scr, -9)
    for copy in range(4):
        bus_scr[2 * copy : 2 * copy + 2, :bus_count] = vm_ref[...]
        bus_scr[8 + 2 * copy : 10 + 2 * copy, :bus_count] = va_ref[...]
    for comp in range(2):
        bus_scr[16 + 2 * comp : 18 + 2 * comp, :bus_count] = grad_ref[comp]
    live = iota((2, slot_count), 1) < live_count
    for kind in range(2):
        weight = jnp.where(live, duals_ref[kind] / slacks_ref[kind], 0.0)
        for copy in range(4):
            weight_scr[8 * kind + 2 * copy : 8 * kind + 2 * copy + 2, :slot_count] = weight
        branch_scr[2 * kind : 2 * kind + 2, :slot_count] = weight
    branch_scr[4:5, :slot_count] = g_ref[...][None]
    branch_scr[5:6, :slot_count] = b_ref[...][None]
    branch_scr[6:7, :gen_count] = gen_curv_ref[...][None]
    index_scr[0:1, :slot_count] = from_ref[...][None]
    index_scr[1:2, :slot_count] = to_ref[...][None]
    index_scr[2:3, :bus_count] = bound_ref[...][None]
    index_scr[3:4, :gen_count] = gen_bus_ref[...][None]

    def tiles(ref, first, chunks):
        return [ref[first : first + ROWS, LANES * c : LANES * (c + 1)] for c in range(chunks)]

    def row(ref, number, chunk):
        return ref[number : number + 1, LANES * chunk : LANES * (chunk + 1)]

    lane = iota((ROWS, LANES), 1)
    sub = iota((ROWS, LANES), 0)
    lane_row = iota((1, LANES), 1)
    sub_col = iota((LANES, LANES), 0).astype(jnp.float32)
    inside = lane < ghost_count

    raw_bound = [tall(row(index_scr, 2, c)) for c in range(2)]
    bound = [jnp.where(inside, take_chunks(raw_bound, lane + h * ghost_count), -1) for h in range(2)]
    fetch = [jnp.maximum(b, 0) for b in bound]
    bound_row = [b[0:1].astype(jnp.float32) for b in bound]
    vm_raw, va_raw, grad_raw = (tiles(bus_scr, 8 * f, 2) for f in range(3))
    vm = [jnp.where(inside, take_chunks(vm_raw, f), 1.0) for f in fetch]
    va = [jnp.where(inside, take_chunks(va_raw, f), 0.0) for f in fetch]
    grad = [jnp.where(inside, take_chunks(grad_raw, f), 0.0) for f in fetch]
    cosv = [jnp.cos(a) for a in va]
    sinv = [jnp.sin(a) for a in va]

    from_key, to_key = [], []
    for c in range(3):
        slot = lane_row + LANES * c
        alive = (slot < live_count) & (slot < slot_count)
        to_raw = row(index_scr, 1, c)
        from_key.append(
            jnp.where(alive & (to_raw < bus_count), row(index_scr, 0, c), 9998).astype(jnp.float32)
        )
        to_key.append(jnp.where(alive, to_raw, 9999).astype(jnp.float32))
    from_col = [column(k) for k in from_key]
    to_col = [column(k) for k in to_key]
    bound_col = [column(b) for b in bound_row]
    gen_col = column(row(index_scr, 3, 0).astype(jnp.float32))
    curv_col = column(row(branch_scr, 6, 0))

    def lowest(masks):
        found = functools.reduce(
            jnp.minimum,
            [jnp.where(m, sub_col + float(LANES * c), float(none)) for c, m in masks],
        )
        return jnp.min(found, axis=0, keepdims=True)

    def links(keys, cols):
        heads, counts = [], []
        for h in range(2):
            equal = [cols[c] == bound_row[h] for c in range(3)]
            heads.append(lowest(list(enumerate(equal))))
            counts.append(
                jnp.sum(
                    functools.reduce(jnp.add, [jnp.where(e, 1.0, 0.0) for e in equal]),
                    axis=0,
                    keepdims=True,
                )
            )
        nexts = []
        for c in range(3):
            later = [(c, (cols[c] == keys[c]) & (sub_col > lane_row.astype(jnp.float32)))]
            later += [(d, cols[d] == keys[c]) for d in range(c + 1, 3)]
            nexts.append(lowest(later))
        return heads, nexts, jnp.maximum(counts[0], counts[1])

    head_f, next_f, count_f = links(from_key, from_col)
    head_t, next_t, count_t = links(to_key, to_col)
    degree = jnp.max(jnp.maximum(count_f, count_t))

    def position(keys):
        found = [
            jnp.where(bound_col[h] == keys, sub_col + float(LANES * h), 0.0) for h in range(2)
        ]
        return jnp.max(jnp.maximum(found[0], found[1]), axis=0, keepdims=True)

    pos_f = [position(k) for k in from_key]
    pos_t = [position(k) for k in to_key]
    for m in range(2):
        pos_ref[m : m + 1, :] = position((lane_row + LANES * m).astype(jnp.float32)).astype(jnp.int32)

    branch_tiles = tiles(branch_scr, 0, 3)
    cross = []
    for h in range(2):
        target = jnp.where(lane_row < ghost_count, bus_count + h * ghost_count + lane_row, -5)
        slot = lowest([(c, to_col[c] == target.astype(jnp.float32)) for c in range(2)])
        cross.append(take_chunks(branch_tiles, tall(slot).astype(jnp.int32)))

    gens = [
        jnp.sum(jnp.where(gen_col == bound_row[h], curv_col, 0.0), axis=0, keepdims=True)
        for h in range(2)
    ]

    pair = sub & 3
    from_table, to_table = [], []
    for c in range(3):
        at_f = tall(pos_f[c]).astype(jnp.int32)
        at_t = tall(pos_t[c]).astype(jnp.int32)
        h00, h01, h11, h22, h12, h02 = block_entries(
            *(take_chunks(t, at_f) for t in (vm, cosv, sinv)),
            *(take_chunks(t, at_t) for t in (vm, cosv, sinv)),
            tall(row(branch_scr, 4, c)),
            tall(row(branch_scr, 5, c)),
            weight_scr[0:8, LANES * c : LANES * (c + 1)],
            weight_scr[8:16, LANES * c : LANES * (c + 1)],
        )
        main = jnp.where(pair < 2, h02, -h11)
        off = jnp.where(pair < 2, -h01, h12)
        first = ROWS * (TILE_LOCAL + c)
        out_ref[first : first + ROWS, :] = jnp.where(sub < 4, main, off)
        from_table.append(jnp.where(sub < 2, h00, jnp.where(sub < 4, h01, h11)))
        to_table.append(jnp.where(sub < 2, h22, jnp.where(sub < 4, -h12, h11)))

    next_ft = [tall(n).astype(jnp.int32) for n in next_f]
    next_tt = [tall(n).astype(jnp.int32) for n in next_t]

    def add_rank(_, carry):
        acc, at_f, at_t = carry
        acc = tuple(
            acc[h] + take_chunks(from_table, at_f[h]) + take_chunks(to_table, at_t[h])
            for h in range(2)
        )
        at_f = tuple(take_chunks(next_ft, at_f[h]) for h in range(2))
        at_t = tuple(take_chunks(next_tt, at_t[h]) for h in range(2))
        return acc, at_f, at_t

    zero = jnp.zeros((ROWS, LANES), jnp.float32)
    acc, _, _ = lax.fori_loop(
        0,
        degree.astype(jnp.int32),
        add_rank,
        (
            (zero, zero),
            tuple(tall(x).astype(jnp.int32) for x in head_f),
            tuple(tall(x).astype(jnp.int32) for x in head_t),
        ),
    )

    for h in range(2):
        below = vm[h] - volt_low
        above = volt_high - vm[h]
        barrier = barrier_weight / (below * below) + barrier_weight / (above * above)
        diag_vv = pltpu.roll(acc[h], 4, 0) + barrier + gens[h]
        diag_aa = pltpu.roll(acc[h], 2, 0) + angle_reg + gens[h]
        diag_va = pltpu.roll(acc[h], 6, 0)
        first = ROWS * (TILE_A + h)
        out_ref[first : first + ROWS, :] = jnp.where(
            sub < 4, grad[h], jnp.where(sub < 6, diag_vv, diag_aa)
        )
        first = ROWS * (TILE_B + h)
        out_ref[first : first + ROWS, :] = jnp.where(
            sub < 2, diag_va, jnp.where(sub < 4, vm[h], jnp.where(sub < 6, cosv[h], sinv[h]))
        )
        first = ROWS * (TILE_C + h)
        out_ref[first : first + ROWS, :] = jnp.where(sub == 6, degree, cross[h])
    first = ROWS * TILE_INDEX
    for offset, value in enumerate(pos_f + pos_t + head_f + head_t + next_f + next_t):
        out_ref[first + offset : first + offset + 1, :] = value
    for peer in range(1, copies_ref.shape[0]):
        copies_ref[peer] = copies_ref[0]


def solve_kernel(me_ref, pos_ref, all_ref, step_ref, residual_ref, chain_scr, step_scr, residual_scr):
    blocks = all_ref.shape[0]
    all_refs = [all_ref.at[p] for p in range(blocks)]
    half = blocks // 2
    bus_count = step_ref.shape[2]
    lane_pairs = [(j, h) for j in range(half) for h in range(2)]
    sub = iota((ROWS, LANES), 0)
    low = sub < 4
    even = (sub & 3) < 2

    def swap_component(x):
        return jnp.where(even, pltpu.roll(x, 6, 0), pltpu.roll(x, 2, 0))

    def swap_block(x):
        return pltpu.roll(x, 4, 0)

    def halves(tile, j):
        first = all_refs[j][ROWS * tile : ROWS * (tile + 1), :]
        second = all_refs[j + half][ROWS * tile : ROWS * (tile + 1), :]
        return (
            jnp.where(low, first, swap_block(second)),
            jnp.where(low, swap_block(first), second),
        )

    def quarters(x):
        return (
            jnp.where(even, x, pltpu.roll(x, 2, 0)),
            jnp.where(even, pltpu.roll(x, 6, 0), x),
        )

    def single(number, j):
        return jnp.where(
            low,
            tall(all_refs[j][number : number + 1, :]),
            tall(all_refs[j + half][number : number + 1, :]),
        )

    def single_index(number, j):
        return single(number, j).astype(jnp.int32)

    def across(field):
        out = {}
        for j in range(half):
            out[j, 1] = field[j + 1, 0] if j + 1 < half else swap_block(field[0, 0])
            out[j, 0] = field[j - 1, 1] if j > 0 else swap_block(field[half - 1, 1])
        return out

    gradient, diag, diag_off = {}, {}, {}
    vm, cosv, sinv, wp, wq, g, b = ({} for _ in range(7))
    for j, h in lane_pairs:
        key = (j, h)
        gradient[key], diag[key] = halves(TILE_A + h, j)
        first, second = halves(TILE_B + h, j)
        diag_off[key], vm[key] = quarters(first)
        cosv[key], sinv[key] = quarters(second)
        first, _ = halves(TILE_C + h, j)
        wp[key], wq[key] = quarters(first)
        g[key] = single(ROWS * (TILE_C + h) + 4, j)
        b[key] = single(ROWS * (TILE_C + h) + 5, j)

    vm_to, cos_to, sin_to = across(vm), across(cosv), across(sinv)
    to_diag, to_off, main, off = {}, {}, {}, {}
    for key in lane_pairs:
        h00, h01, h11, h22, h12, h02 = block_entries(
            vm[key],
            cosv[key],
            sinv[key],
            vm_to[key],
            cos_to[key],
            sin_to[key],
            g[key],
            b[key],
            wp[key],
            wq[key],
        )
        diag[key] = diag[key] + jnp.where(even, h00, h11)
        diag_off[key] = diag_off[key] + h01
        to_diag[key] = jnp.where(even, h22, h11)
        to_off[key] = -h12
        main[key] = jnp.where(even, h02, -h11)
        off[key] = jnp.where(even, -h01, h12)
    to_diag, to_off = across(to_diag), across(to_off)
    main_to = across(main)
    off_to = across({key: swap_component(off[key]) for key in lane_pairs})
    inverse, inverse_off = {}, {}
    for key in lane_pairs:
        diag[key] = diag[key] + to_diag[key]
        diag_off[key] = diag_off[key] + to_off[key]
        main[key] = main[key] + main_to[key]
        off[key] = off[key] + off_to[key]
        flipped = swap_component(diag[key])
        determinant = diag[key] * flipped - diag_off[key] * diag_off[key]
        inverse[key] = flipped / determinant
        inverse_off[key] = -diag_off[key] / determinant

    local_main, local_off, at_from, at_to = {}, {}, {}, {}
    next_f, next_t, head_f, head_t = {}, {}, {}, {}
    base = ROWS * TILE_INDEX
    for j in range(half):
        for c in range(3):
            local_main[j, c], local_off[j, c] = halves(TILE_LOCAL + c, j)
            at_from[j, c] = single_index(base + c, j)
            at_to[j, c] = single_index(base + 3 + c, j)
            next_f[j, c] = single_index(base + 10 + c, j)
            next_t[j, c] = single_index(base + 13 + c, j)
        for h in range(2):
            head_f[j, h] = single_index(base + 6 + h, j)
            head_t[j, h] = single_index(base + 8 + h, j)
    number = ROWS * TILE_C + 6
    degrees = functools.reduce(
        jnp.maximum, [block[number : number + 1, :] for block in all_refs]
    )
    degree = jnp.max(degrees).astype(jnp.int32)

    def follow(rank, carry):
        ends_f, ends_t = carry
        new_f, new_t = [], []
        for number, (j, h) in enumerate(lane_pairs):
            chain_scr[rank, 2 * number] = ends_f[number]
            chain_scr[rank, 2 * number + 1] = ends_t[number]
            new_f.append(take_chunks([next_f[j, c] for c in range(3)], ends_f[number]))
            new_t.append(take_chunks([next_t[j, c] for c in range(3)], ends_t[number]))
        return tuple(new_f), tuple(new_t)

    lax.fori_loop(
        0,
        degree,
        follow,
        (tuple(head_f[key] for key in lane_pairs), tuple(head_t[key] for key in lane_pairs)),
    )

    def operator(v):
        flipped = {key: swap_component(v[key]) for key in lane_pairs}
        v_to, flipped_to = across(v), across(flipped)
        out = {
            key: diag[key] * v[key]
            + diag_off[key] * flipped[key]
            + main[key] * v_to[key]
            + off[key] * flipped_to[key]
            for key in lane_pairs
        }
        to_from, to_to = {}, {}
        for j in range(half):
            table = [v[j, 0], v[j, 1]]
            for c in range(3):
                far = take_chunks(table, at_to[j, c])
                near = take_chunks(table, at_from[j, c])
                to_from[j, c] = local_main[j, c] * far + local_off[j, c] * swap_component(far)
                to_to[j, c] = local_main[j, c] * near + swap_component(local_off[j, c] * near)

        def add_rank(rank, sums):
            new = []
            for number, (j, h) in enumerate(lane_pairs):
                new.append(
                    sums[number]
                    + take_chunks([to_from[j, c] for c in range(3)], chain_scr[rank, 2 * number])
                    + take_chunks([to_to[j, c] for c in range(3)], chain_scr[rank, 2 * number + 1])
                )
            return tuple(new)

        sums = lax.fori_loop(0, degree, add_rank, tuple(out[key] for key in lane_pairs))
        return dict(zip(lane_pairs, sums))

    def scenario_total(left, right):
        total = functools.reduce(jnp.add, [left[key] * right[key] for key in lane_pairs])
        total = total + pltpu.roll(total, 2, 0)
        total = total + pltpu.roll(total, 4, 0)
        return jnp.broadcast_to(jnp.sum(total, axis=1, keepdims=True), (ROWS, LANES))

    def precondition(v):
        return {
            key: inverse[key] * v[key] + inverse_off[key] * swap_component(v[key])
            for key in lane_pairs
        }

    residual = gradient
    search = precondition(residual)
    energy = scenario_total(residual, search)
    update = None
    for iteration in range(ITERS):
        image = operator(search)
        step_size = energy / scenario_total(search, image)
        if update is None:
            update = {key: step_size * search[key] for key in lane_pairs}
        else:
            update = {key: update[key] + step_size * search[key] for key in lane_pairs}
        residual = {key: residual[key] - step_size * image[key] for key in lane_pairs}
        if iteration + 1 < ITERS:
            scaled = precondition(residual)
            energy_next = scenario_total(residual, scaled)
            ratio = energy_next / energy
            search = {key: scaled[key] + ratio * search[key] for key in lane_pairs}
            energy = energy_next

    me = me_ref[0]
    upper = me >= half
    mine = jnp.where(upper, me - half, me)
    for field, keep_scr, out_ref in (
        (update, step_scr, step_ref),
        (residual, residual_scr, residual_ref),
    ):
        for j, h in lane_pairs:
            keep_scr[j, h] = field[j, h]
        own = []
        for h in range(2):
            tile = keep_scr[mine, h]
            own.append(jnp.where(upper, swap_block(tile), tile))
        for m in range(2):
            width = min(LANES, bus_count - LANES * m)
            values = take_chunks(own, tall(pos_ref[m : m + 1, :]))
            for comp in range(2):
                out_ref[comp, :, LANES * m : LANES * m + width] = values[
                    2 * comp : 2 * comp + 2, :width
                ]


def fast_body(
    volt_mag,
    volt_ang,
    gradient,
    branch_from,
    branch_to,
    branch_count,
    boundary,
    conductance,
    susceptance,
    duals,
    slacks,
    gen_bus,
    gen_curvature,
):
    bus_count = volt_mag.shape[0]
    slot_count = branch_from.shape[0]
    blocks = lax.axis_size("net")
    vmem = pl.BlockSpec(memory_space=pltpu.VMEM)
    smem = pl.BlockSpec(memory_space=pltpu.SMEM)
    payload, position = pl.pallas_call(
        prepare_kernel,
        out_shape=(
            jax.ShapeDtypeStruct((blocks, PAYLOAD_ROWS, LANES), jnp.float32),
            jax.ShapeDtypeStruct((2, LANES), jnp.int32),
        ),
        in_specs=[vmem] * 5 + [smem] + [vmem] * 7,
        out_specs=(vmem, vmem),
        scratch_shapes=[
            pltpu.VMEM((24, 2 * LANES), jnp.float32),
            pltpu.VMEM((16, 3 * LANES), jnp.float32),
            pltpu.VMEM((8, 3 * LANES), jnp.float32),
            pltpu.VMEM((8, 3 * LANES), jnp.int32),
        ],
        name="prepare",
    )(
        volt_mag.T,
        volt_ang.T,
        jnp.transpose(gradient, (1, 2, 0)),
        branch_from,
        branch_to,
        branch_count,
        boundary,
        conductance,
        susceptance,
        jnp.transpose(duals, (0, 2, 1)),
        jnp.transpose(slacks, (0, 2, 1)),
        gen_bus,
        gen_curvature,
    )
    gathered = lax.all_to_all(payload, "net", 0, 0)
    me = lax.axis_index("net").astype(jnp.int32)[None]
    tile_pairs = (blocks // 2, 2, ROWS, LANES)
    field = jax.ShapeDtypeStruct((2, 2, bus_count), jnp.float32)
    step, residual = pl.pallas_call(
        solve_kernel,
        out_shape=(field, field),
        in_specs=[smem, vmem, vmem],
        out_specs=(vmem, vmem),
        scratch_shapes=[
            pltpu.VMEM((slot_count, 2 * blocks, ROWS, LANES), jnp.int32),
            pltpu.VMEM(tile_pairs, jnp.float32),
            pltpu.VMEM(tile_pairs, jnp.float32),
        ],
        compiler_params=pltpu.CompilerParams(vmem_limit_bytes=40 * 2**20),
        name="solve",
    )(me, position, gathered)
    return jnp.transpose(step, (2, 0, 1)), jnp.transpose(residual, (2, 0, 1))


def any_body(*arrays):
    volt_mag, boundary, branch_from, gen_bus = arrays[0], arrays[6], arrays[3], arrays[11]
    fast = fits_fast_path(
        lax.axis_size("net"),
        volt_mag.shape[0],
        boundary.shape[0] // 2,
        branch_from.shape[0],
        gen_bus.shape[0],
        volt_mag.shape[1],
    )
    return fast_body(*arrays) if fast else body(*arrays)


def solution(mesh):
    placed = (
        P("net", "scen"),
        P("net", "scen"),
        P("net", None, "scen"),
        P("net"),
        P("net"),
        P("net"),
        P("net"),
        P("net"),
        P("net"),
        P(None, "net", "scen"),
        P(None, "net", "scen"),
        P("net"),
        P("net"),
    )
    return jax.shard_map(
        any_body,
        mesh=mesh,
        in_specs=placed,
        out_specs=(P("net", None, "scen"), P("net", None, "scen")),
        check_vma=False,
    )
```

```python
import functools

import jax
import jax.numpy as jnp
from jax import lax
from jax.experimental import pallas as pl
from jax.experimental.pallas import tpu as pltpu
from jax.sharding import PartitionSpec as P

ITERS = 4


barrier_weight = 0.01
volt_low = 0.9
volt_high = 1.1
angle_reg = 0.5


def shifted(array, axis, by):
    peers = lax.axis_size(axis)
    pairs = [(i, i + by) for i in range(peers) if 0 <= i + by < peers]
    return lax.ppermute(array, axis, pairs)


def branch_blocks(
    magnitude_from,
    angle_from,
    magnitude_to,
    angle_to,
    conduct,
    suscept,
    weight_active,
    weight_reactive,
):
    angle_diff = angle_from - angle_to
    cosine_diff = jnp.cos(angle_diff)
    sine_diff = jnp.sin(angle_diff)
    flow_along = conduct * cosine_diff + suscept * sine_diff
    flow_across = conduct * sine_diff - suscept * cosine_diff
    cross_term = magnitude_from * magnitude_to
    active_rows = (
        2.0 * conduct * magnitude_from - magnitude_to * flow_along,
        cross_term * flow_across,
        -magnitude_from * flow_along,
        -cross_term * flow_across,
    )
    reactive_rows = (
        -2.0 * suscept * magnitude_from - magnitude_to * flow_across,
        -cross_term * flow_along,
        -magnitude_from * flow_across,
        cross_term * flow_along,
    )

    def block_entry(left_index, right_index):
        return (
            weight_active * active_rows[left_index] * active_rows[right_index]
            + weight_reactive * reactive_rows[left_index] * reactive_rows[right_index]
        )

    from_block = jnp.stack([block_entry(0, 0), block_entry(0, 1), block_entry(1, 1)], axis=1)
    to_block = jnp.stack([block_entry(2, 2), block_entry(2, 3), block_entry(3, 3)], axis=1)
    cross_block = jnp.stack(
        [block_entry(0, 2), block_entry(0, 3), block_entry(1, 2), block_entry(1, 3)], axis=1
    )
    return (from_block, to_block, cross_block)


def apply_cross(matrix_block, vector):
    return jnp.stack(
        [
            matrix_block[:, 0] * vector[:, 0] + matrix_block[:, 1] * vector[:, 1],
            matrix_block[:, 2] * vector[:, 0] + matrix_block[:, 3] * vector[:, 1],
        ],
        axis=1,
    )


def apply_cross_transposed(matrix_block, vector):
    return jnp.stack(
        [
            matrix_block[:, 0] * vector[:, 0] + matrix_block[:, 2] * vector[:, 1],
            matrix_block[:, 1] * vector[:, 0] + matrix_block[:, 3] * vector[:, 1],
        ],
        axis=1,
    )


def scenario_sum(left_vec, right_vec):
    return jnp.sum(left_vec * right_vec, axis=(0, 1))


def widen(values):
    return values[None, None, :]


def body(
    volt_mag,
    volt_ang,
    gradient,
    branch_from,
    branch_to,
    branch_count,
    boundary,
    conductance,
    susceptance,
    duals,
    slacks,
    gen_bus,
    gen_curvature,
):
    bus_count = volt_mag.shape[0]
    ghost_count = boundary.shape[0] // 2
    extended_size = bus_count + 2 * ghost_count
    slot_count = branch_from.shape[0]
    left_list = boundary[:ghost_count]
    right_list = boundary[ghost_count:]
    left_ghost = slice(bus_count, bus_count + ghost_count)
    right_ghost = slice(bus_count + ghost_count, extended_size)
    return_plan = (
        (-1, left_ghost, right_list, right_ghost),
        (1, right_ghost, left_list, left_ghost),
    )

    def share_vector(values):
        pieces = [values]
        for direction in (1, -1):
            outgoing = jnp.take(values, right_list if direction == 1 else left_list, axis=0)
            pieces.append(shifted(outgoing, "net", direction))
        return jnp.concatenate(pieces, axis=0)

    bus_state = jnp.stack([volt_mag, volt_ang], axis=1)
    pieces = [bus_state]
    for share_direction in (1, -1):
        outgoing = jnp.take(bus_state, right_list if share_direction == 1 else left_list, axis=0)
        pieces.append(shifted(outgoing, "net", share_direction))
    extended_state = jnp.concatenate(pieces, axis=0)
    from_state = jnp.take(extended_state, branch_from, axis=0)
    to_state = jnp.take(extended_state, branch_to, axis=0)
    live_mask = (jnp.arange(slot_count) < branch_count[0]).astype(jnp.float32)[:, None]
    weight_active = live_mask * duals[0] / slacks[0]
    weight_reactive = live_mask * duals[1] / slacks[1]
    from_block, to_block, cross_block = branch_blocks(
        from_state[:, 0],
        from_state[:, 1],
        to_state[:, 0],
        to_state[:, 1],
        conductance[:, None],
        susceptance[:, None],
        weight_active,
        weight_reactive,
    )
    diag_extended = jax.ops.segment_sum(
        from_block, branch_from, num_segments=extended_size
    ) + jax.ops.segment_sum(to_block, branch_to, num_segments=extended_size)
    diag_local = diag_extended[:bus_count]
    for direction, ghost_rows, target_rows, source_rows in return_plan:
        arrived_diag = shifted(diag_extended[ghost_rows], "net", direction)
        diag_local = diag_local.at[target_rows].add(arrived_diag)
    gen_table = (gen_bus[None, :] == jnp.arange(bus_count)[:, None]).astype(jnp.float32)
    gen_sum = jnp.dot(gen_table, gen_curvature, precision=lax.Precision.HIGHEST)[:, None]
    barrier = barrier_weight / jnp.square(volt_mag - volt_low) + barrier_weight / jnp.square(
        volt_high - volt_mag
    )
    diag_vv = diag_local[:, 0] + barrier + gen_sum
    diag_va = diag_local[:, 1]
    diag_aa = diag_local[:, 2] + angle_reg + gen_sum
    determinant = diag_vv * diag_aa - diag_va * diag_va
    inverse_vv = diag_aa / determinant
    inverse_va = -diag_va / determinant
    inverse_aa = diag_vv / determinant

    def precondition(vector):
        return jnp.stack(
            [
                inverse_vv * vector[:, 0] + inverse_va * vector[:, 1],
                inverse_va * vector[:, 0] + inverse_aa * vector[:, 1],
            ],
            axis=1,
        )

    update_field = jnp.zeros_like(gradient)
    residual = gradient

    def energy_of(residual_now, scaled_now):
        return lax.psum(scenario_sum(residual_now, scaled_now), "net")

    scaled = precondition(residual)
    search = scaled
    energy = energy_of(residual, scaled)
    for iteration in range(ITERS):
        extended = share_vector(search)
        from_values = jnp.take(extended, branch_from, axis=0)
        to_values = jnp.take(extended, branch_to, axis=0)
        from_terms = apply_cross(cross_block, to_values)
        to_terms = apply_cross_transposed(cross_block, from_values)
        result = jnp.stack(
            [
                diag_vv * search[:, 0] + diag_va * search[:, 1],
                diag_va * search[:, 0] + diag_aa * search[:, 1],
            ],
            axis=1,
        )
        summed = jax.ops.segment_sum(
            from_terms, branch_from, num_segments=extended_size
        ) + jax.ops.segment_sum(to_terms, branch_to, num_segments=extended_size)
        local_sum = result + summed[:bus_count]
        for apply_direction, apply_ghost_rows, apply_target_rows, apply_source_rows in return_plan:
            arrived = shifted(summed[apply_ghost_rows], "net", apply_direction)
            local_sum = local_sum.at[apply_target_rows].add(arrived)
        step_size = energy / lax.psum(scenario_sum(search, local_sum), "net")
        update_field = update_field + widen(step_size) * search
        residual = residual - widen(step_size) * local_sum
        if iteration + 1 < ITERS:
            scaled = precondition(residual)
            energy_next = energy_of(residual, scaled)
            search = scaled + widen(energy_next / energy) * search
            energy = energy_next
    return (update_field, residual)


LANES = 128
ROWS = 8
TILE_A, TILE_B, TILE_C = 0, 2, 4
TILE_LOCAL = 6
TILE_INDEX = 9
PAYLOAD_ROWS = 11 * ROWS
CHUNK_FIELDS = ["gradient", "diag", "diag_off", "vm", "cosv", "sinv"]
CHUNK_FIELDS += ["wp", "wq", "g", "b", "head_f", "head_t"]
SLOT_FIELDS = ["local_main", "local_off", "at_from", "at_to", "next_f", "next_t"]


def fits_fast_path(blocks, bus_count, ghost_count, slot_count, gen_count, scen_count):
    return (
        blocks == 8
        and scen_count == 2
        and bus_count == 2 * ghost_count
        and ghost_count <= LANES
        and 2 * LANES < slot_count < 3 * LANES
        and gen_count <= LANES
    )


def iota(shape, dim):
    return lax.broadcasted_iota(jnp.int32, shape, dim)


def lane_take(table, index):
    return jnp.take_along_axis(table, index, axis=1, mode="promise_in_bounds")


def take_chunks(tables, index):
    lane = index & (LANES - 1)
    chunk = index >> 7
    out = lane_take(tables[0], lane)
    for number in range(1, len(tables)):
        out = jnp.where(chunk == number, lane_take(tables[number], lane), out)
    return out


def tall(row):
    return jnp.broadcast_to(row, (ROWS, LANES))


def column(row):
    return jnp.transpose(jnp.broadcast_to(row, (LANES, LANES)))


def block_entries(vi, ci, si, vj, cj, sj, g, b, wp, wq):
    cosine = ci * cj + si * sj
    sine = si * cj - ci * sj
    along = g * cosine + b * sine
    across = g * sine - b * cosine
    cross = vi * vj
    p0 = 2.0 * g * vi - vj * along
    p1 = cross * across
    p2 = -vi * along
    q0 = -2.0 * b * vi - vj * across
    q1 = -cross * along
    q2 = -vi * across

    def entry(pa, pb, qa, qb):
        return wp * pa * pb + wq * qa * qb

    return (
        entry(p0, p0, q0, q0),
        entry(p0, p1, q0, q1),
        entry(p1, p1, q1, q1),
        entry(p2, p2, q2, q2),
        entry(p1, p2, q1, q2),
        entry(p0, p2, q0, q2),
    )


def prepare_kernel(
    vm_ref,
    va_ref,
    grad_ref,
    from_ref,
    to_ref,
    count_ref,
    bound_ref,
    g_ref,
    b_ref,
    duals_ref,
    slacks_ref,
    gen_bus_ref,
    gen_curv_ref,
    out_ref,
    pos_ref,
    bus_scr,
    weight_scr,
    branch_scr,
    index_scr,
):
    bus_count = vm_ref.shape[1]
    ghost_count = bus_count // 2
    slot_count = from_ref.shape[0]
    gen_count = gen_bus_ref.shape[0]
    none = 3 * LANES - 1
    live_count = count_ref[...][None]

    bus_scr[...] = jnp.zeros_like(bus_scr)
    weight_scr[...] = jnp.zeros_like(weight_scr)
    branch_scr[...] = jnp.zeros_like(branch_scr)
    index_scr[...] = jnp.full_like(index_scr, -9)
    for copy in range(4):
        bus_scr[2 * copy : 2 * copy + 2, :bus_count] = vm_ref[...]
        bus_scr[8 + 2 * copy : 10 + 2 * copy, :bus_count] = va_ref[...]
    for comp in range(2):
        bus_scr[16 + 2 * comp : 18 + 2 * comp, :bus_count] = grad_ref[comp]
    live = iota((2, slot_count), 1) < live_count
    for kind in range(2):
        weight = jnp.where(live, duals_ref[kind] / slacks_ref[kind], 0.0)
        for copy in range(4):
            weight_scr[8 * kind + 2 * copy : 8 * kind + 2 * copy + 2, :slot_count] = weight
        branch_scr[2 * kind : 2 * kind + 2, :slot_count] = weight
    branch_scr[4:5, :slot_count] = g_ref[...][None]
    branch_scr[5:6, :slot_count] = b_ref[...][None]
    branch_scr[6:7, :gen_count] = gen_curv_ref[...][None]
    index_scr[0:1, :slot_count] = from_ref[...][None]
    index_scr[1:2, :slot_count] = to_ref[...][None]
    index_scr[2:3, :bus_count] = bound_ref[...][None]
    index_scr[3:4, :gen_count] = gen_bus_ref[...][None]

    def tiles(ref, first, chunks):
        return [ref[first : first + ROWS, LANES * c : LANES * (c + 1)] for c in range(chunks)]

    def row(ref, number, chunk):
        return ref[number : number + 1, LANES * chunk : LANES * (chunk + 1)]

    lane = iota((ROWS, LANES), 1)
    sub = iota((ROWS, LANES), 0)
    lane_row = iota((1, LANES), 1)
    sub_col = iota((LANES, LANES), 0).astype(jnp.float32)
    inside = lane < ghost_count

    raw_bound = [tall(row(index_scr, 2, c)) for c in range(2)]
    bound = [jnp.where(inside, take_chunks(raw_bound, lane + h * ghost_count), -1) for h in range(2)]
    fetch = [jnp.maximum(b, 0) for b in bound]
    bound_row = [b[0:1].astype(jnp.float32) for b in bound]
    vm_raw, va_raw, grad_raw = (tiles(bus_scr, 8 * f, 2) for f in range(3))
    vm = [jnp.where(inside, take_chunks(vm_raw, f), 1.0) for f in fetch]
    va = [jnp.where(inside, take_chunks(va_raw, f), 0.0) for f in fetch]
    grad = [jnp.where(inside, take_chunks(grad_raw, f), 0.0) for f in fetch]
    cosv = [jnp.cos(a) for a in va]
    sinv = [jnp.sin(a) for a in va]

    from_key, to_key = [], []
    for c in range(3):
        slot = lane_row + LANES * c
        alive = (slot < live_count) & (slot < slot_count)
        to_raw = row(index_scr, 1, c)
        from_key.append(
            jnp.where(alive & (to_raw < bus_count), row(index_scr, 0, c), 9998).astype(jnp.float32)
        )
        to_key.append(jnp.where(alive, to_raw, 9999).astype(jnp.float32))
    from_col = [column(k) for k in from_key]
    to_col = [column(k) for k in to_key]
    bound_col = [column(b) for b in bound_row]
    gen_col = column(row(index_scr, 3, 0).astype(jnp.float32))
    curv_col = column(row(branch_scr, 6, 0))

    def lowest(masks):
        found = functools.reduce(
            jnp.minimum,
            [jnp.where(m, sub_col + float(LANES * c), float(none)) for c, m in masks],
        )
        return jnp.min(found, axis=0, keepdims=True)

    def links(keys, cols):
        heads, counts = [], []
        for h in range(2):
            equal = [cols[c] == bound_row[h] for c in range(3)]
            heads.append(lowest(list(enumerate(equal))))
            counts.append(
                jnp.sum(
                    functools.reduce(jnp.add, [jnp.where(e, 1.0, 0.0) for e in equal]),
                    axis=0,
                    keepdims=True,
                )
            )
        nexts = []
        for c in range(3):
            later = [(c, (cols[c] == keys[c]) & (sub_col > lane_row.astype(jnp.float32)))]
            later += [(d, cols[d] == keys[c]) for d in range(c + 1, 3)]
            nexts.append(lowest(later))
        return heads, nexts, jnp.maximum(counts[0], counts[1])

    head_f, next_f, count_f = links(from_key, from_col)
    head_t, next_t, count_t = links(to_key, to_col)
    degree = jnp.max(jnp.maximum(count_f, count_t))

    def position(keys):
        found = [
            jnp.where(bound_col[h] == keys, sub_col + float(LANES * h), 0.0) for h in range(2)
        ]
        return jnp.max(jnp.maximum(found[0], found[1]), axis=0, keepdims=True)

    pos_f = [position(k) for k in from_key]
    pos_t = [position(k) for k in to_key]
    for m in range(2):
        pos_ref[m : m + 1, :] = position((lane_row + LANES * m).astype(jnp.float32)).astype(jnp.int32)

    branch_tiles = tiles(branch_scr, 0, 3)
    cross = []
    for h in range(2):
        target = jnp.where(lane_row < ghost_count, bus_count + h * ghost_count + lane_row, -5)
        slot = lowest([(c, to_col[c] == target.astype(jnp.float32)) for c in range(2)])
        cross.append(take_chunks(branch_tiles, tall(slot).astype(jnp.int32)))

    gens = [
        jnp.sum(jnp.where(gen_col == bound_row[h], curv_col, 0.0), axis=0, keepdims=True)
        for h in range(2)
    ]

    pair = sub & 3
    from_table, to_table = [], []
    for c in range(3):
        at_f = tall(pos_f[c]).astype(jnp.int32)
        at_t = tall(pos_t[c]).astype(jnp.int32)
        h00, h01, h11, h22, h12, h02 = block_entries(
            *(take_chunks(t, at_f) for t in (vm, cosv, sinv)),
            *(take_chunks(t, at_t) for t in (vm, cosv, sinv)),
            tall(row(branch_scr, 4, c)),
            tall(row(branch_scr, 5, c)),
            weight_scr[0:8, LANES * c : LANES * (c + 1)],
            weight_scr[8:16, LANES * c : LANES * (c + 1)],
        )
        main = jnp.where(pair < 2, h02, -h11)
        off = jnp.where(pair < 2, -h01, h12)
        first = ROWS * (TILE_LOCAL + c)
        out_ref[first : first + ROWS, :] = jnp.where(sub < 4, main, off)
        from_table.append(jnp.where(sub < 2, h00, jnp.where(sub < 4, h01, h11)))
        to_table.append(jnp.where(sub < 2, h22, jnp.where(sub < 4, -h12, h11)))

    next_ft = [tall(n).astype(jnp.int32) for n in next_f]
    next_tt = [tall(n).astype(jnp.int32) for n in next_t]

    def add_rank(_, carry):
        acc, at_f, at_t = carry
        acc = tuple(
            acc[h] + take_chunks(from_table, at_f[h]) + take_chunks(to_table, at_t[h])
            for h in range(2)
        )
        at_f = tuple(take_chunks(next_ft, at_f[h]) for h in range(2))
        at_t = tuple(take_chunks(next_tt, at_t[h]) for h in range(2))
        return acc, at_f, at_t

    zero = jnp.zeros((ROWS, LANES), jnp.float32)
    acc, _, _ = lax.fori_loop(
        0,
        degree.astype(jnp.int32),
        add_rank,
        (
            (zero, zero),
            tuple(tall(x).astype(jnp.int32) for x in head_f),
            tuple(tall(x).astype(jnp.int32) for x in head_t),
        ),
    )

    for h in range(2):
        below = vm[h] - volt_low
        above = volt_high - vm[h]
        barrier = barrier_weight / (below * below) + barrier_weight / (above * above)
        diag_vv = pltpu.roll(acc[h], 4, 0) + barrier + gens[h]
        diag_aa = pltpu.roll(acc[h], 2, 0) + angle_reg + gens[h]
        diag_va = pltpu.roll(acc[h], 6, 0)
        first = ROWS * (TILE_A + h)
        out_ref[first : first + ROWS, :] = jnp.where(
            sub < 4, grad[h], jnp.where(sub < 6, diag_vv, diag_aa)
        )
        first = ROWS * (TILE_B + h)
        out_ref[first : first + ROWS, :] = jnp.where(
            sub < 2, diag_va, jnp.where(sub < 4, vm[h], jnp.where(sub < 6, cosv[h], sinv[h]))
        )
        first = ROWS * (TILE_C + h)
        out_ref[first : first + ROWS, :] = jnp.where(sub == 6, degree, cross[h])
    first = ROWS * TILE_INDEX
    for offset, value in enumerate(pos_f + pos_t + head_f + head_t + next_f + next_t):
        out_ref[first + offset : first + offset + 1, :] = value


def solve_kernel(me_ref, pos_ref, *refs):
    *all_refs, step_ref, residual_ref, chain_scr, field_scr, step_scr, residual_scr = refs
    blocks = len(all_refs)
    me = me_ref[0]
    half = blocks // 2
    bus_count = step_ref.shape[2]
    lane_pairs = [(j, h) for j in range(half) for h in range(2)]
    sub = iota((ROWS, LANES), 0)
    low = sub < 4
    even = (sub & 3) < 2

    def swap_component(x):
        return jnp.where(even, pltpu.roll(x, 6, 0), pltpu.roll(x, 2, 0))

    def swap_block(x):
        return pltpu.roll(x, 4, 0)

    upper = me >= half
    mine = me & (half - 1)
    near = low != upper

    def halves(tile, j):
        here = all_refs[j][ROWS * tile : ROWS * (tile + 1), :]
        there = all_refs[j + half][ROWS * tile : ROWS * (tile + 1), :]
        first = jnp.where(upper, there, here)
        second = jnp.where(upper, here, there)
        return (
            jnp.where(low, first, swap_block(second)),
            jnp.where(low, swap_block(first), second),
        )

    def quarters(x):
        return (
            jnp.where(even, x, pltpu.roll(x, 2, 0)),
            jnp.where(even, pltpu.roll(x, 6, 0), x),
        )

    def single(number, j):
        return jnp.where(
            near,
            tall(all_refs[j][number : number + 1, :]),
            tall(all_refs[j + half][number : number + 1, :]),
        )

    def across(field):
        out = {}
        for j in range(half):
            out[j, 1] = field[j + 1, 0] if j + 1 < half else swap_block(field[0, 0])
            out[j, 0] = field[j - 1, 1] if j > 0 else swap_block(field[half - 1, 1])
        return out

    base = ROWS * TILE_INDEX
    names = [(name, h) for name in CHUNK_FIELDS for h in range(2)]
    names += [(name, c) for name in SLOT_FIELDS for c in range(3)]
    place = {name: number for number, name in enumerate(names)}
    for j in range(half):
        found = {}
        for h in range(2):
            found["gradient", h], found["diag", h] = halves(TILE_A + h, j)
            first, second = halves(TILE_B + h, j)
            found["diag_off", h], found["vm", h] = quarters(first)
            found["cosv", h], found["sinv", h] = quarters(second)
            first, _ = halves(TILE_C + h, j)
            found["wp", h], found["wq", h] = quarters(first)
            found["g", h] = single(ROWS * (TILE_C + h) + 4, j)
            found["b", h] = single(ROWS * (TILE_C + h) + 5, j)
            found["head_f", h] = single(base + 6 + h, j)
            found["head_t", h] = single(base + 8 + h, j)
        for c in range(3):
            found["local_main", c], found["local_off", c] = halves(TILE_LOCAL + c, j)
            found["at_from", c] = single(base + c, j)
            found["at_to", c] = single(base + 3 + c, j)
            found["next_f", c] = single(base + 10 + c, j)
            found["next_t", c] = single(base + 13 + c, j)
        for name, number in place.items():
            field_scr[number, j ^ mine] = found[name]

    def load(name, chunks):
        return {
            (j, c): field_scr[place[name, c], j] for j in range(half) for c in range(chunks)
        }

    def load_index(name, chunks):
        return {key: value.astype(jnp.int32) for key, value in load(name, chunks).items()}

    gradient, diag, diag_off, vm, cosv, sinv, wp, wq, g, b = (
        load(name, 2) for name in CHUNK_FIELDS[:10]
    )
    vm_to, cos_to, sin_to = across(vm), across(cosv), across(sinv)
    to_diag, to_off, main, off = {}, {}, {}, {}
    for key in lane_pairs:
        h00, h01, h11, h22, h12, h02 = block_entries(
            vm[key],
            cosv[key],
            sinv[key],
            vm_to[key],
            cos_to[key],
            sin_to[key],
            g[key],
            b[key],
            wp[key],
            wq[key],
        )
        diag[key] = diag[key] + jnp.where(even, h00, h11)
        diag_off[key] = diag_off[key] + h01
        to_diag[key] = jnp.where(even, h22, h11)
        to_off[key] = -h12
        main[key] = jnp.where(even, h02, -h11)
        off[key] = jnp.where(even, -h01, h12)
    to_diag, to_off = across(to_diag), across(to_off)
    main_to = across(main)
    off_to = across({key: swap_component(off[key]) for key in lane_pairs})
    inverse, inverse_off = {}, {}
    for key in lane_pairs:
        diag[key] = diag[key] + to_diag[key]
        diag_off[key] = diag_off[key] + to_off[key]
        main[key] = main[key] + main_to[key]
        off[key] = off[key] + off_to[key]
        flipped = swap_component(diag[key])
        determinant = diag[key] * flipped - diag_off[key] * diag_off[key]
        inverse[key] = flipped / determinant
        inverse_off[key] = -diag_off[key] / determinant

    head_f, head_t = (load_index(name, 2) for name in CHUNK_FIELDS[10:])
    local_main, local_off = (load(name, 3) for name in SLOT_FIELDS[:2])
    at_from, at_to, next_f, next_t = (load_index(name, 3) for name in SLOT_FIELDS[2:])
    number = ROWS * TILE_C + 6
    degrees = functools.reduce(
        jnp.maximum, [block[number : number + 1, :] for block in all_refs]
    )
    degree = jnp.max(degrees).astype(jnp.int32)

    def follow(rank, carry):
        ends_f, ends_t = carry
        new_f, new_t = [], []
        for number, (j, h) in enumerate(lane_pairs):
            chain_scr[rank, 2 * number] = ends_f[number]
            chain_scr[rank, 2 * number + 1] = ends_t[number]
            new_f.append(take_chunks([next_f[j, c] for c in range(3)], ends_f[number]))
            new_t.append(take_chunks([next_t[j, c] for c in range(3)], ends_t[number]))
        return tuple(new_f), tuple(new_t)

    lax.fori_loop(
        0,
        degree,
        follow,
        (tuple(head_f[key] for key in lane_pairs), tuple(head_t[key] for key in lane_pairs)),
    )

    def operator(v):
        flipped = {key: swap_component(v[key]) for key in lane_pairs}
        v_to, flipped_to = across(v), across(flipped)
        out = {
            key: diag[key] * v[key]
            + diag_off[key] * flipped[key]
            + main[key] * v_to[key]
            + off[key] * flipped_to[key]
            for key in lane_pairs
        }
        to_from, to_to = {}, {}
        for j in range(half):
            table = [v[j, 0], v[j, 1]]
            for c in range(3):
                far = take_chunks(table, at_to[j, c])
                near = take_chunks(table, at_from[j, c])
                to_from[j, c] = local_main[j, c] * far + local_off[j, c] * swap_component(far)
                to_to[j, c] = local_main[j, c] * near + swap_component(local_off[j, c] * near)

        def add_rank(rank, sums):
            new = []
            for number, (j, h) in enumerate(lane_pairs):
                new.append(
                    sums[number]
                    + take_chunks([to_from[j, c] for c in range(3)], chain_scr[rank, 2 * number])
                    + take_chunks([to_to[j, c] for c in range(3)], chain_scr[rank, 2 * number + 1])
                )
            return tuple(new)

        sums = lax.fori_loop(0, degree, add_rank, tuple(out[key] for key in lane_pairs))
        return dict(zip(lane_pairs, sums))

    def scenario_total(left, right):
        total = functools.reduce(jnp.add, [left[key] * right[key] for key in lane_pairs])
        total = total + pltpu.roll(total, 2, 0)
        total = total + pltpu.roll(total, 4, 0)
        return jnp.broadcast_to(jnp.sum(total, axis=1, keepdims=True), (ROWS, LANES))

    def precondition(v):
        return {
            key: inverse[key] * v[key] + inverse_off[key] * swap_component(v[key])
            for key in lane_pairs
        }

    residual = gradient
    search = precondition(residual)
    energy = scenario_total(residual, search)
    update = None
    for iteration in range(ITERS):
        image = operator(search)
        step_size = energy / scenario_total(search, image)
        if update is None:
            update = {key: step_size * search[key] for key in lane_pairs}
        else:
            update = {key: update[key] + step_size * search[key] for key in lane_pairs}
        residual = {key: residual[key] - step_size * image[key] for key in lane_pairs}
        if iteration + 1 < ITERS:
            scaled = precondition(residual)
            energy_next = scenario_total(residual, scaled)
            ratio = energy_next / energy
            search = {key: scaled[key] + ratio * search[key] for key in lane_pairs}
            energy = energy_next

    for field, keep_scr, out_ref in (
        (update, step_scr, step_ref),
        (residual, residual_scr, residual_ref),
    ):
        for j, h in lane_pairs:
            keep_scr[j, h] = field[j, h]
        own = []
        for h in range(2):
            tile = keep_scr[mine, h]
            own.append(jnp.where(upper, swap_block(tile), tile))
        for m in range(2):
            width = min(LANES, bus_count - LANES * m)
            values = take_chunks(own, tall(pos_ref[m : m + 1, :]))
            for comp in range(2):
                out_ref[comp, :, LANES * m : LANES * m + width] = values[
                    2 * comp : 2 * comp + 2, :width
                ]


def fast_body(
    volt_mag,
    volt_ang,
    gradient,
    branch_from,
    branch_to,
    branch_count,
    boundary,
    conductance,
    susceptance,
    duals,
    slacks,
    gen_bus,
    gen_curvature,
):
    bus_count = volt_mag.shape[0]
    slot_count = branch_from.shape[0]
    blocks = lax.axis_size("net")
    vmem = pl.BlockSpec(memory_space=pltpu.VMEM)
    smem = pl.BlockSpec(memory_space=pltpu.SMEM)
    payload, position = pl.pallas_call(
        prepare_kernel,
        out_shape=(
            pltpu.VMEM((PAYLOAD_ROWS, LANES), jnp.float32),
            pltpu.VMEM((2, LANES), jnp.int32),
        ),
        in_specs=[vmem] * 13,
        out_specs=(vmem, vmem),
        scratch_shapes=[
            pltpu.VMEM((24, 2 * LANES), jnp.float32),
            pltpu.VMEM((16, 3 * LANES), jnp.float32),
            pltpu.VMEM((8, 3 * LANES), jnp.float32),
            pltpu.VMEM((8, 3 * LANES), jnp.int32),
        ],
        name="prepare",
    )(
        volt_mag.T,
        volt_ang.T,
        jnp.transpose(gradient, (1, 2, 0)),
        branch_from,
        branch_to,
        branch_count,
        boundary,
        conductance,
        susceptance,
        jnp.transpose(duals, (0, 2, 1)),
        jnp.transpose(slacks, (0, 2, 1)),
        gen_bus,
        gen_curvature,
    )
    gathered = [payload]
    for other in range(1, blocks):
        gathered.append(lax.ppermute(payload, "net", [(i, i ^ other) for i in range(blocks)]))
    me = lax.axis_index("net").astype(jnp.int32)[None]
    tile_pairs = (blocks // 2, 2, ROWS, LANES)
    field = jax.ShapeDtypeStruct((2, 2, bus_count), jnp.float32)
    step, residual = pl.pallas_call(
        solve_kernel,
        out_shape=(field, field),
        in_specs=[smem] + [vmem] * (1 + blocks),
        out_specs=(vmem, vmem),
        scratch_shapes=[
            pltpu.VMEM((slot_count, 2 * blocks, ROWS, LANES), jnp.int32),
            pltpu.VMEM(
                (2 * len(CHUNK_FIELDS) + 3 * len(SLOT_FIELDS), blocks // 2, ROWS, LANES),
                jnp.float32,
            ),
            pltpu.VMEM(tile_pairs, jnp.float32),
            pltpu.VMEM(tile_pairs, jnp.float32),
        ],
        compiler_params=pltpu.CompilerParams(vmem_limit_bytes=40 * 2**20),
        name="solve",
    )(me, position, *gathered)
    return jnp.transpose(step, (2, 0, 1)), jnp.transpose(residual, (2, 0, 1))


def any_body(*arrays):
    volt_mag, boundary, branch_from, gen_bus = arrays[0], arrays[6], arrays[3], arrays[11]
    fast = fits_fast_path(
        lax.axis_size("net"),
        volt_mag.shape[0],
        boundary.shape[0] // 2,
        branch_from.shape[0],
        gen_bus.shape[0],
        volt_mag.shape[1],
    )
    return fast_body(*arrays) if fast else body(*arrays)


def solution(mesh):
    placed = (
        P("net", "scen"),
        P("net", "scen"),
        P("net", None, "scen"),
        P("net"),
        P("net"),
        P("net"),
        P("net"),
        P("net"),
        P("net"),
        P(None, "net", "scen"),
        P(None, "net", "scen"),
        P("net"),
        P("net"),
    )
    return jax.shard_map(
        any_body,
        mesh=mesh,
        in_specs=placed,
        out_specs=(P("net", None, "scen"), P("net", None, "scen")),
        check_vma=False,
    )
```

```python
import functools

import jax
import jax.numpy as jnp
from jax import lax
from jax.experimental import pallas as pl
from jax.experimental.pallas import tpu as pltpu
from jax.sharding import PartitionSpec as P

ITERS = 4


barrier_weight = 0.01
volt_low = 0.9
volt_high = 1.1
angle_reg = 0.5


def shifted(array, axis, by):
    peers = lax.axis_size(axis)
    pairs = [(i, i + by) for i in range(peers) if 0 <= i + by < peers]
    return lax.ppermute(array, axis, pairs)


def branch_blocks(
    magnitude_from,
    angle_from,
    magnitude_to,
    angle_to,
    conduct,
    suscept,
    weight_active,
    weight_reactive,
):
    angle_diff = angle_from - angle_to
    cosine_diff = jnp.cos(angle_diff)
    sine_diff = jnp.sin(angle_diff)
    flow_along = conduct * cosine_diff + suscept * sine_diff
    flow_across = conduct * sine_diff - suscept * cosine_diff
    cross_term = magnitude_from * magnitude_to
    active_rows = (
        2.0 * conduct * magnitude_from - magnitude_to * flow_along,
        cross_term * flow_across,
        -magnitude_from * flow_along,
        -cross_term * flow_across,
    )
    reactive_rows = (
        -2.0 * suscept * magnitude_from - magnitude_to * flow_across,
        -cross_term * flow_along,
        -magnitude_from * flow_across,
        cross_term * flow_along,
    )

    def block_entry(left_index, right_index):
        return (
            weight_active * active_rows[left_index] * active_rows[right_index]
            + weight_reactive * reactive_rows[left_index] * reactive_rows[right_index]
        )

    from_block = jnp.stack([block_entry(0, 0), block_entry(0, 1), block_entry(1, 1)], axis=1)
    to_block = jnp.stack([block_entry(2, 2), block_entry(2, 3), block_entry(3, 3)], axis=1)
    cross_block = jnp.stack(
        [block_entry(0, 2), block_entry(0, 3), block_entry(1, 2), block_entry(1, 3)], axis=1
    )
    return (from_block, to_block, cross_block)


def apply_cross(matrix_block, vector):
    return jnp.stack(
        [
            matrix_block[:, 0] * vector[:, 0] + matrix_block[:, 1] * vector[:, 1],
            matrix_block[:, 2] * vector[:, 0] + matrix_block[:, 3] * vector[:, 1],
        ],
        axis=1,
    )


def apply_cross_transposed(matrix_block, vector):
    return jnp.stack(
        [
            matrix_block[:, 0] * vector[:, 0] + matrix_block[:, 2] * vector[:, 1],
            matrix_block[:, 1] * vector[:, 0] + matrix_block[:, 3] * vector[:, 1],
        ],
        axis=1,
    )


def scenario_sum(left_vec, right_vec):
    return jnp.sum(left_vec * right_vec, axis=(0, 1))


def widen(values):
    return values[None, None, :]


def body(
    volt_mag,
    volt_ang,
    gradient,
    branch_from,
    branch_to,
    branch_count,
    boundary,
    conductance,
    susceptance,
    duals,
    slacks,
    gen_bus,
    gen_curvature,
):
    bus_count = volt_mag.shape[0]
    ghost_count = boundary.shape[0] // 2
    extended_size = bus_count + 2 * ghost_count
    slot_count = branch_from.shape[0]
    left_list = boundary[:ghost_count]
    right_list = boundary[ghost_count:]
    left_ghost = slice(bus_count, bus_count + ghost_count)
    right_ghost = slice(bus_count + ghost_count, extended_size)
    return_plan = (
        (-1, left_ghost, right_list, right_ghost),
        (1, right_ghost, left_list, left_ghost),
    )

    def share_vector(values):
        pieces = [values]
        for direction in (1, -1):
            outgoing = jnp.take(values, right_list if direction == 1 else left_list, axis=0)
            pieces.append(shifted(outgoing, "net", direction))
        return jnp.concatenate(pieces, axis=0)

    bus_state = jnp.stack([volt_mag, volt_ang], axis=1)
    pieces = [bus_state]
    for share_direction in (1, -1):
        outgoing = jnp.take(bus_state, right_list if share_direction == 1 else left_list, axis=0)
        pieces.append(shifted(outgoing, "net", share_direction))
    extended_state = jnp.concatenate(pieces, axis=0)
    from_state = jnp.take(extended_state, branch_from, axis=0)
    to_state = jnp.take(extended_state, branch_to, axis=0)
    live_mask = (jnp.arange(slot_count) < branch_count[0]).astype(jnp.float32)[:, None]
    weight_active = live_mask * duals[0] / slacks[0]
    weight_reactive = live_mask * duals[1] / slacks[1]
    from_block, to_block, cross_block = branch_blocks(
        from_state[:, 0],
        from_state[:, 1],
        to_state[:, 0],
        to_state[:, 1],
        conductance[:, None],
        susceptance[:, None],
        weight_active,
        weight_reactive,
    )
    diag_extended = jax.ops.segment_sum(
        from_block, branch_from, num_segments=extended_size
    ) + jax.ops.segment_sum(to_block, branch_to, num_segments=extended_size)
    diag_local = diag_extended[:bus_count]
    for direction, ghost_rows, target_rows, source_rows in return_plan:
        arrived_diag = shifted(diag_extended[ghost_rows], "net", direction)
        diag_local = diag_local.at[target_rows].add(arrived_diag)
    gen_table = (gen_bus[None, :] == jnp.arange(bus_count)[:, None]).astype(jnp.float32)
    gen_sum = jnp.dot(gen_table, gen_curvature, precision=lax.Precision.HIGHEST)[:, None]
    barrier = barrier_weight / jnp.square(volt_mag - volt_low) + barrier_weight / jnp.square(
        volt_high - volt_mag
    )
    diag_vv = diag_local[:, 0] + barrier + gen_sum
    diag_va = diag_local[:, 1]
    diag_aa = diag_local[:, 2] + angle_reg + gen_sum
    determinant = diag_vv * diag_aa - diag_va * diag_va
    inverse_vv = diag_aa / determinant
    inverse_va = -diag_va / determinant
    inverse_aa = diag_vv / determinant

    def precondition(vector):
        return jnp.stack(
            [
                inverse_vv * vector[:, 0] + inverse_va * vector[:, 1],
                inverse_va * vector[:, 0] + inverse_aa * vector[:, 1],
            ],
            axis=1,
        )

    update_field = jnp.zeros_like(gradient)
    residual = gradient

    def energy_of(residual_now, scaled_now):
        return lax.psum(scenario_sum(residual_now, scaled_now), "net")

    scaled = precondition(residual)
    search = scaled
    energy = energy_of(residual, scaled)
    for iteration in range(ITERS):
        extended = share_vector(search)
        from_values = jnp.take(extended, branch_from, axis=0)
        to_values = jnp.take(extended, branch_to, axis=0)
        from_terms = apply_cross(cross_block, to_values)
        to_terms = apply_cross_transposed(cross_block, from_values)
        result = jnp.stack(
            [
                diag_vv * search[:, 0] + diag_va * search[:, 1],
                diag_va * search[:, 0] + diag_aa * search[:, 1],
            ],
            axis=1,
        )
        summed = jax.ops.segment_sum(
            from_terms, branch_from, num_segments=extended_size
        ) + jax.ops.segment_sum(to_terms, branch_to, num_segments=extended_size)
        local_sum = result + summed[:bus_count]
        for apply_direction, apply_ghost_rows, apply_target_rows, apply_source_rows in return_plan:
            arrived = shifted(summed[apply_ghost_rows], "net", apply_direction)
            local_sum = local_sum.at[apply_target_rows].add(arrived)
        step_size = energy / lax.psum(scenario_sum(search, local_sum), "net")
        update_field = update_field + widen(step_size) * search
        residual = residual - widen(step_size) * local_sum
        if iteration + 1 < ITERS:
            scaled = precondition(residual)
            energy_next = energy_of(residual, scaled)
            search = scaled + widen(energy_next / energy) * search
            energy = energy_next
    return (update_field, residual)


LANES = 128
ROWS = 8
TILE_A, TILE_B, TILE_C = 0, 2, 4
TILE_LOCAL = 6
TILE_INDEX = 9
PAYLOAD_ROWS = 11 * ROWS
CHUNK_FIELDS = ["gradient", "diag", "diag_off", "vm", "cosv", "sinv"]
CHUNK_FIELDS += ["wp", "wq", "g", "b", "head_f", "head_t"]
SLOT_FIELDS = ["local_main", "local_off", "at_from", "at_to", "next_f", "next_t"]


def fits_fast_path(blocks, bus_count, ghost_count, slot_count, gen_count, scen_count):
    return (
        blocks == 8
        and scen_count == 2
        and bus_count == 2 * ghost_count
        and ghost_count <= LANES
        and 2 * LANES < slot_count < 3 * LANES
        and gen_count <= LANES
    )


def iota(shape, dim):
    return lax.broadcasted_iota(jnp.int32, shape, dim)


def lane_take(table, index):
    return jnp.take_along_axis(table, index, axis=1, mode="promise_in_bounds")


def take_chunks(tables, index):
    lane = index & (LANES - 1)
    chunk = index >> 7
    out = lane_take(tables[0], lane)
    for number in range(1, len(tables)):
        out = jnp.where(chunk == number, lane_take(tables[number], lane), out)
    return out


def tall(row):
    return jnp.broadcast_to(row, (ROWS, LANES))


def column(row):
    return jnp.transpose(jnp.broadcast_to(row, (LANES, LANES)))


def block_entries(vi, ci, si, vj, cj, sj, g, b, wp, wq):
    cosine = ci * cj + si * sj
    sine = si * cj - ci * sj
    along = g * cosine + b * sine
    across = g * sine - b * cosine
    cross = vi * vj
    p0 = 2.0 * g * vi - vj * along
    p1 = cross * across
    p2 = -vi * along
    q0 = -2.0 * b * vi - vj * across
    q1 = -cross * along
    q2 = -vi * across

    def entry(pa, pb, qa, qb):
        return wp * pa * pb + wq * qa * qb

    return (
        entry(p0, p0, q0, q0),
        entry(p0, p1, q0, q1),
        entry(p1, p1, q1, q1),
        entry(p2, p2, q2, q2),
        entry(p1, p2, q1, q2),
        entry(p0, p2, q0, q2),
    )


def prepare_kernel(
    vm_ref,
    va_ref,
    grad_ref,
    from_ref,
    to_ref,
    count_ref,
    bound_ref,
    g_ref,
    b_ref,
    duals_ref,
    slacks_ref,
    gen_bus_ref,
    gen_curv_ref,
    out_ref,
    pos_ref,
    bus_scr,
    weight_scr,
    branch_scr,
    index_scr,
):
    bus_count = vm_ref.shape[1]
    ghost_count = bus_count // 2
    slot_count = from_ref.shape[0]
    gen_count = gen_bus_ref.shape[0]
    none = 3 * LANES - 1
    live_count = count_ref[...][None]

    bus_scr[...] = jnp.zeros_like(bus_scr)
    weight_scr[...] = jnp.zeros_like(weight_scr)
    branch_scr[...] = jnp.zeros_like(branch_scr)
    index_scr[...] = jnp.full_like(index_scr, -9)
    for copy in range(4):
        bus_scr[2 * copy : 2 * copy + 2, :bus_count] = vm_ref[...]
        bus_scr[8 + 2 * copy : 10 + 2 * copy, :bus_count] = va_ref[...]
    for comp in range(2):
        bus_scr[16 + 2 * comp : 18 + 2 * comp, :bus_count] = grad_ref[comp]
    live = iota((2, slot_count), 1) < live_count
    for kind in range(2):
        weight = jnp.where(live, duals_ref[kind] / slacks_ref[kind], 0.0)
        for copy in range(4):
            weight_scr[8 * kind + 2 * copy : 8 * kind + 2 * copy + 2, :slot_count] = weight
        branch_scr[2 * kind : 2 * kind + 2, :slot_count] = weight
    branch_scr[4:5, :slot_count] = g_ref[...][None]
    branch_scr[5:6, :slot_count] = b_ref[...][None]
    branch_scr[6:7, :gen_count] = gen_curv_ref[...][None]
    index_scr[0:1, :slot_count] = from_ref[...][None]
    index_scr[1:2, :slot_count] = to_ref[...][None]
    index_scr[2:3, :bus_count] = bound_ref[...][None]
    index_scr[3:4, :gen_count] = gen_bus_ref[...][None]

    def tiles(ref, first, chunks):
        return [ref[first : first + ROWS, LANES * c : LANES * (c + 1)] for c in range(chunks)]

    def row(ref, number, chunk):
        return ref[number : number + 1, LANES * chunk : LANES * (chunk + 1)]

    lane = iota((ROWS, LANES), 1)
    sub = iota((ROWS, LANES), 0)
    lane_row = iota((1, LANES), 1)
    sub_col = iota((LANES, LANES), 0).astype(jnp.float32)
    inside = lane < ghost_count

    raw_bound = [tall(row(index_scr, 2, c)) for c in range(2)]
    bound = [jnp.where(inside, take_chunks(raw_bound, lane + h * ghost_count), -1) for h in range(2)]
    fetch = [jnp.maximum(b, 0) for b in bound]
    bound_row = [b[0:1].astype(jnp.float32) for b in bound]
    vm_raw, va_raw, grad_raw = (tiles(bus_scr, 8 * f, 2) for f in range(3))
    vm = [jnp.where(inside, take_chunks(vm_raw, f), 1.0) for f in fetch]
    va = [jnp.where(inside, take_chunks(va_raw, f), 0.0) for f in fetch]
    grad = [jnp.where(inside, take_chunks(grad_raw, f), 0.0) for f in fetch]
    cosv = [jnp.cos(a) for a in va]
    sinv = [jnp.sin(a) for a in va]

    from_key, to_key = [], []
    for c in range(3):
        slot = lane_row + LANES * c
        alive = (slot < live_count) & (slot < slot_count)
        to_raw = row(index_scr, 1, c)
        from_key.append(
            jnp.where(alive & (to_raw < bus_count), row(index_scr, 0, c), 9998).astype(jnp.float32)
        )
        to_key.append(jnp.where(alive, to_raw, 9999).astype(jnp.float32))
    from_col = [column(k) for k in from_key]
    to_col = [column(k) for k in to_key]
    bound_col = [column(b) for b in bound_row]
    gen_col = column(row(index_scr, 3, 0).astype(jnp.float32))
    curv_col = column(row(branch_scr, 6, 0))

    def lowest(masks):
        found = functools.reduce(
            jnp.minimum,
            [jnp.where(m, sub_col + float(LANES * c), float(none)) for c, m in masks],
        )
        return jnp.min(found, axis=0, keepdims=True)

    def links(keys, cols):
        heads, counts = [], []
        for h in range(2):
            equal = [cols[c] == bound_row[h] for c in range(3)]
            heads.append(lowest(list(enumerate(equal))))
            counts.append(
                jnp.sum(
                    functools.reduce(jnp.add, [jnp.where(e, 1.0, 0.0) for e in equal]),
                    axis=0,
                    keepdims=True,
                )
            )
        nexts = []
        for c in range(3):
            later = [(c, (cols[c] == keys[c]) & (sub_col > lane_row.astype(jnp.float32)))]
            later += [(d, cols[d] == keys[c]) for d in range(c + 1, 3)]
            nexts.append(lowest(later))
        return heads, nexts, jnp.maximum(counts[0], counts[1])

    head_f, next_f, count_f = links(from_key, from_col)
    head_t, next_t, count_t = links(to_key, to_col)
    degree = jnp.max(jnp.maximum(count_f, count_t))

    def position(keys):
        found = [
            jnp.where(bound_col[h] == keys, sub_col + float(LANES * h), 0.0) for h in range(2)
        ]
        return jnp.max(jnp.maximum(found[0], found[1]), axis=0, keepdims=True)

    pos_f = [position(k) for k in from_key]
    pos_t = [position(k) for k in to_key]
    for m in range(2):
        pos_ref[m : m + 1, :] = position((lane_row + LANES * m).astype(jnp.float32)).astype(jnp.int32)

    branch_tiles = tiles(branch_scr, 0, 3)
    cross = []
    for h in range(2):
        target = jnp.where(lane_row < ghost_count, bus_count + h * ghost_count + lane_row, -5)
        slot = lowest([(c, to_col[c] == target.astype(jnp.float32)) for c in range(2)])
        cross.append(take_chunks(branch_tiles, tall(slot).astype(jnp.int32)))

    gens = [
        jnp.sum(jnp.where(gen_col == bound_row[h], curv_col, 0.0), axis=0, keepdims=True)
        for h in range(2)
    ]

    pair = sub & 3
    from_table, to_table = [], []
    for c in range(3):
        at_f = tall(pos_f[c]).astype(jnp.int32)
        at_t = tall(pos_t[c]).astype(jnp.int32)
        h00, h01, h11, h22, h12, h02 = block_entries(
            *(take_chunks(t, at_f) for t in (vm, cosv, sinv)),
            *(take_chunks(t, at_t) for t in (vm, cosv, sinv)),
            tall(row(branch_scr, 4, c)),
            tall(row(branch_scr, 5, c)),
            weight_scr[0:8, LANES * c : LANES * (c + 1)],
            weight_scr[8:16, LANES * c : LANES * (c + 1)],
        )
        main = jnp.where(pair < 2, h02, -h11)
        off = jnp.where(pair < 2, -h01, h12)
        first = ROWS * (TILE_LOCAL + c)
        out_ref[first : first + ROWS, :] = jnp.where(sub < 4, main, off)
        from_table.append(jnp.where(sub < 2, h00, jnp.where(sub < 4, h01, h11)))
        to_table.append(jnp.where(sub < 2, h22, jnp.where(sub < 4, -h12, h11)))

    next_ft = [tall(n).astype(jnp.int32) for n in next_f]
    next_tt = [tall(n).astype(jnp.int32) for n in next_t]

    def add_rank(_, carry):
        acc, at_f, at_t = carry
        acc = tuple(
            acc[h] + take_chunks(from_table, at_f[h]) + take_chunks(to_table, at_t[h])
            for h in range(2)
        )
        at_f = tuple(take_chunks(next_ft, at_f[h]) for h in range(2))
        at_t = tuple(take_chunks(next_tt, at_t[h]) for h in range(2))
        return acc, at_f, at_t

    zero = jnp.zeros((ROWS, LANES), jnp.float32)
    acc, _, _ = lax.fori_loop(
        0,
        degree.astype(jnp.int32),
        add_rank,
        (
            (zero, zero),
            tuple(tall(x).astype(jnp.int32) for x in head_f),
            tuple(tall(x).astype(jnp.int32) for x in head_t),
        ),
    )

    for h in range(2):
        below = vm[h] - volt_low
        above = volt_high - vm[h]
        barrier = barrier_weight / (below * below) + barrier_weight / (above * above)
        diag_vv = pltpu.roll(acc[h], 4, 0) + barrier + gens[h]
        diag_aa = pltpu.roll(acc[h], 2, 0) + angle_reg + gens[h]
        diag_va = pltpu.roll(acc[h], 6, 0)
        first = ROWS * (TILE_A + h)
        out_ref[first : first + ROWS, :] = jnp.where(
            sub < 4, grad[h], jnp.where(sub < 6, diag_vv, diag_aa)
        )
        first = ROWS * (TILE_B + h)
        out_ref[first : first + ROWS, :] = jnp.where(
            sub < 2, diag_va, jnp.where(sub < 4, vm[h], jnp.where(sub < 6, cosv[h], sinv[h]))
        )
        first = ROWS * (TILE_C + h)
        out_ref[first : first + ROWS, :] = jnp.where(sub == 6, degree, cross[h])
    first = ROWS * TILE_INDEX
    for offset, value in enumerate(pos_f + pos_t + head_f + head_t + next_f + next_t):
        out_ref[first + offset : first + offset + 1, :] = value


def solve_kernel(me_ref, pos_ref, *refs):
    *all_refs, step_ref, residual_ref, chain_scr, field_scr, step_scr, residual_scr = refs
    blocks = len(all_refs)
    me = me_ref[0]
    half = blocks // 2
    bus_count = step_ref.shape[2]
    lane_pairs = [(j, h) for j in range(half) for h in range(2)]
    sub = iota((ROWS, LANES), 0)
    low = sub < 4
    even = (sub & 3) < 2

    def swap_component(x):
        return jnp.where(even, pltpu.roll(x, 6, 0), pltpu.roll(x, 2, 0))

    def swap_block(x):
        return pltpu.roll(x, 4, 0)

    upper = me >= half
    mine = me & (half - 1)
    near = low != upper

    def halves(tile, j):
        here = all_refs[j][ROWS * tile : ROWS * (tile + 1), :]
        there = all_refs[j + half][ROWS * tile : ROWS * (tile + 1), :]
        first = jnp.where(upper, there, here)
        second = jnp.where(upper, here, there)
        return (
            jnp.where(low, first, swap_block(second)),
            jnp.where(low, swap_block(first), second),
        )

    def quarters(x):
        return (
            jnp.where(even, x, pltpu.roll(x, 2, 0)),
            jnp.where(even, pltpu.roll(x, 6, 0), x),
        )

    def single(number, j):
        return jnp.where(
            near,
            tall(all_refs[j][number : number + 1, :]),
            tall(all_refs[j + half][number : number + 1, :]),
        )

    def across(field):
        out = {}
        for j in range(half):
            out[j, 1] = field[j + 1, 0] if j + 1 < half else swap_block(field[0, 0])
            out[j, 0] = field[j - 1, 1] if j > 0 else swap_block(field[half - 1, 1])
        return out

    base = ROWS * TILE_INDEX
    names = [(name, h) for name in CHUNK_FIELDS for h in range(2)]
    names += [(name, c) for name in SLOT_FIELDS for c in range(3)]
    place = {name: number for number, name in enumerate(names)}
    for j in range(half):
        found = {}
        for h in range(2):
            found["gradient", h], found["diag", h] = halves(TILE_A + h, j)
            first, second = halves(TILE_B + h, j)
            found["diag_off", h], found["vm", h] = quarters(first)
            found["cosv", h], found["sinv", h] = quarters(second)
            first, _ = halves(TILE_C + h, j)
            found["wp", h], found["wq", h] = quarters(first)
            found["g", h] = single(ROWS * (TILE_C + h) + 4, j)
            found["b", h] = single(ROWS * (TILE_C + h) + 5, j)
            found["head_f", h] = single(base + 6 + h, j)
            found["head_t", h] = single(base + 8 + h, j)
        for c in range(3):
            found["local_main", c], found["local_off", c] = halves(TILE_LOCAL + c, j)
            found["at_from", c] = single(base + c, j)
            found["at_to", c] = single(base + 3 + c, j)
            found["next_f", c] = single(base + 10 + c, j)
            found["next_t", c] = single(base + 13 + c, j)
        for name, number in place.items():
            field_scr[number, j ^ mine] = found[name]

    def load(name, chunks):
        return {
            (j, c): field_scr[place[name, c], j] for j in range(half) for c in range(chunks)
        }

    def load_index(name, chunks):
        return {key: value.astype(jnp.int32) for key, value in load(name, chunks).items()}

    gradient, diag, diag_off, vm, cosv, sinv, wp, wq, g, b = (
        load(name, 2) for name in CHUNK_FIELDS[:10]
    )
    vm_to, cos_to, sin_to = across(vm), across(cosv), across(sinv)
    to_diag, to_off, main, off = {}, {}, {}, {}
    for key in lane_pairs:
        h00, h01, h11, h22, h12, h02 = block_entries(
            vm[key],
            cosv[key],
            sinv[key],
            vm_to[key],
            cos_to[key],
            sin_to[key],
            g[key],
            b[key],
            wp[key],
            wq[key],
        )
        diag[key] = diag[key] + jnp.where(even, h00, h11)
        diag_off[key] = diag_off[key] + h01
        to_diag[key] = jnp.where(even, h22, h11)
        to_off[key] = -h12
        main[key] = jnp.where(even, h02, -h11)
        off[key] = jnp.where(even, -h01, h12)
    to_diag, to_off = across(to_diag), across(to_off)
    main_to = across(main)
    off_to = across({key: swap_component(off[key]) for key in lane_pairs})
    inverse, inverse_off = {}, {}
    for key in lane_pairs:
        diag[key] = diag[key] + to_diag[key]
        diag_off[key] = diag_off[key] + to_off[key]
        main[key] = main[key] + main_to[key]
        off[key] = off[key] + off_to[key]
        flipped = swap_component(diag[key])
        determinant = diag[key] * flipped - diag_off[key] * diag_off[key]
        inverse[key] = flipped / determinant
        inverse_off[key] = -diag_off[key] / determinant

    head_f, head_t = (load_index(name, 2) for name in CHUNK_FIELDS[10:])
    local_main, local_off = (load(name, 3) for name in SLOT_FIELDS[:2])
    at_from, at_to, next_f, next_t = (load_index(name, 3) for name in SLOT_FIELDS[2:])
    number = ROWS * TILE_C + 6
    degrees = functools.reduce(
        jnp.maximum, [block[number : number + 1, :] for block in all_refs]
    )
    degree = jnp.max(degrees).astype(jnp.int32)

    def follow(rank, carry):
        ends_f, ends_t = carry
        new_f, new_t = [], []
        for number, (j, h) in enumerate(lane_pairs):
            chain_scr[rank, 2 * number] = ends_f[number]
            chain_scr[rank, 2 * number + 1] = ends_t[number]
            new_f.append(take_chunks([next_f[j, c] for c in range(3)], ends_f[number]))
            new_t.append(take_chunks([next_t[j, c] for c in range(3)], ends_t[number]))
        return tuple(new_f), tuple(new_t)

    lax.fori_loop(
        0,
        degree,
        follow,
        (tuple(head_f[key] for key in lane_pairs), tuple(head_t[key] for key in lane_pairs)),
    )

    def operator(v):
        flipped = {key: swap_component(v[key]) for key in lane_pairs}
        v_to, flipped_to = across(v), across(flipped)
        out = {
            key: diag[key] * v[key]
            + diag_off[key] * flipped[key]
            + main[key] * v_to[key]
            + off[key] * flipped_to[key]
            for key in lane_pairs
        }
        to_from, to_to = {}, {}
        for j in range(half):
            table = [v[j, 0], v[j, 1]]
            for c in range(3):
                far = take_chunks(table, at_to[j, c])
                near = take_chunks(table, at_from[j, c])
                to_from[j, c] = local_main[j, c] * far + local_off[j, c] * swap_component(far)
                to_to[j, c] = local_main[j, c] * near + swap_component(local_off[j, c] * near)

        def add_rank(rank, sums):
            new = []
            for number, (j, h) in enumerate(lane_pairs):
                new.append(
                    sums[number]
                    + take_chunks([to_from[j, c] for c in range(3)], chain_scr[rank, 2 * number])
                    + take_chunks([to_to[j, c] for c in range(3)], chain_scr[rank, 2 * number + 1])
                )
            return tuple(new)

        sums = lax.fori_loop(0, degree, add_rank, tuple(out[key] for key in lane_pairs))
        return dict(zip(lane_pairs, sums))

    def scenario_total(left, right):
        total = functools.reduce(jnp.add, [left[key] * right[key] for key in lane_pairs])
        total = total + pltpu.roll(total, 2, 0)
        total = total + pltpu.roll(total, 4, 0)
        return jnp.broadcast_to(jnp.sum(total, axis=1, keepdims=True), (ROWS, LANES))

    def precondition(v):
        return {
            key: inverse[key] * v[key] + inverse_off[key] * swap_component(v[key])
            for key in lane_pairs
        }

    residual = gradient
    search = precondition(residual)
    energy = scenario_total(residual, search)
    update = None
    for iteration in range(ITERS):
        image = operator(search)
        step_size = energy / scenario_total(search, image)
        if update is None:
            update = {key: step_size * search[key] for key in lane_pairs}
        else:
            update = {key: update[key] + step_size * search[key] for key in lane_pairs}
        residual = {key: residual[key] - step_size * image[key] for key in lane_pairs}
        if iteration + 1 < ITERS:
            scaled = precondition(residual)
            energy_next = scenario_total(residual, scaled)
            ratio = energy_next / energy
            search = {key: scaled[key] + ratio * search[key] for key in lane_pairs}
            energy = energy_next

    for field, keep_scr, out_ref in (
        (update, step_scr, step_ref),
        (residual, residual_scr, residual_ref),
    ):
        for j, h in lane_pairs:
            keep_scr[j, h] = field[j, h]
        own = []
        for h in range(2):
            tile = keep_scr[mine, h]
            own.append(jnp.where(upper, swap_block(tile), tile))
        for m in range(2):
            width = min(LANES, bus_count - LANES * m)
            values = take_chunks(own, tall(pos_ref[m : m + 1, :]))
            for comp in range(2):
                out_ref[comp, :, LANES * m : LANES * m + width] = values[
                    2 * comp : 2 * comp + 2, :width
                ]


def fast_body(
    volt_mag,
    volt_ang,
    gradient,
    branch_from,
    branch_to,
    branch_count,
    boundary,
    conductance,
    susceptance,
    duals,
    slacks,
    gen_bus,
    gen_curvature,
):
    bus_count = volt_mag.shape[0]
    slot_count = branch_from.shape[0]
    blocks = lax.axis_size("net")
    vmem = pl.BlockSpec(memory_space=pltpu.VMEM)
    smem = pl.BlockSpec(memory_space=pltpu.SMEM)
    payload, position = pl.pallas_call(
        prepare_kernel,
        out_shape=(
            pltpu.VMEM((PAYLOAD_ROWS, LANES), jnp.float32),
            pltpu.VMEM((2, LANES), jnp.int32),
        ),
        in_specs=[vmem] * 13,
        out_specs=(vmem, vmem),
        scratch_shapes=[
            pltpu.VMEM((24, 2 * LANES), jnp.float32),
            pltpu.VMEM((16, 3 * LANES), jnp.float32),
            pltpu.VMEM((8, 3 * LANES), jnp.float32),
            pltpu.VMEM((8, 3 * LANES), jnp.int32),
        ],
        name="prepare",
    )(
        volt_mag.T,
        volt_ang.T,
        jnp.transpose(gradient, (1, 2, 0)),
        branch_from,
        branch_to,
        branch_count,
        boundary,
        conductance,
        susceptance,
        jnp.transpose(duals, (0, 2, 1)),
        jnp.transpose(slacks, (0, 2, 1)),
        gen_bus,
        gen_curvature,
    )
    def passed(block, other):
        return lax.ppermute(block, "net", [(i, i ^ other) for i in range(blocks)])

    gathered = {0: payload}
    for other in range(2, blocks, 2):
        gathered[other] = passed(payload, other)
    for other in range(0, blocks, 2):
        gathered[other + 1] = passed(gathered[other], 1)
    gathered = [gathered[other] for other in range(blocks)]
    me = lax.axis_index("net").astype(jnp.int32)[None]
    tile_pairs = (blocks // 2, 2, ROWS, LANES)
    field = jax.ShapeDtypeStruct((2, 2, bus_count), jnp.float32)
    step, residual = pl.pallas_call(
        solve_kernel,
        out_shape=(field, field),
        in_specs=[smem] + [vmem] * (1 + blocks),
        out_specs=(vmem, vmem),
        scratch_shapes=[
            pltpu.VMEM((slot_count, 2 * blocks, ROWS, LANES), jnp.int32),
            pltpu.VMEM(
                (2 * len(CHUNK_FIELDS) + 3 * len(SLOT_FIELDS), blocks // 2, ROWS, LANES),
                jnp.float32,
            ),
            pltpu.VMEM(tile_pairs, jnp.float32),
            pltpu.VMEM(tile_pairs, jnp.float32),
        ],
        compiler_params=pltpu.CompilerParams(vmem_limit_bytes=40 * 2**20),
        name="solve",
    )(me, position, *gathered)
    return jnp.transpose(step, (2, 0, 1)), jnp.transpose(residual, (2, 0, 1))


def any_body(*arrays):
    volt_mag, boundary, branch_from, gen_bus = arrays[0], arrays[6], arrays[3], arrays[11]
    fast = fits_fast_path(
        lax.axis_size("net"),
        volt_mag.shape[0],
        boundary.shape[0] // 2,
        branch_from.shape[0],
        gen_bus.shape[0],
        volt_mag.shape[1],
    )
    return fast_body(*arrays) if fast else body(*arrays)


def solution(mesh):
    placed = (
        P("net", "scen"),
        P("net", "scen"),
        P("net", None, "scen"),
        P("net"),
        P("net"),
        P("net"),
        P("net"),
        P("net"),
        P("net"),
        P(None, "net", "scen"),
        P(None, "net", "scen"),
        P("net"),
        P("net"),
    )
    return jax.shard_map(
        any_body,
        mesh=mesh,
        in_specs=placed,
        out_specs=(P("net", None, "scen"), P("net", None, "scen")),
        check_vma=False,
    )
```

```python
import functools

import jax
import jax.numpy as jnp
from jax import lax
from jax.experimental import pallas as pl
from jax.experimental.pallas import tpu as pltpu
from jax.sharding import PartitionSpec as P

ITERS = 4


barrier_weight = 0.01
volt_low = 0.9
volt_high = 1.1
angle_reg = 0.5


def shifted(array, axis, by):
    peers = lax.axis_size(axis)
    pairs = [(i, i + by) for i in range(peers) if 0 <= i + by < peers]
    return lax.ppermute(array, axis, pairs)


def branch_blocks(
    magnitude_from,
    angle_from,
    magnitude_to,
    angle_to,
    conduct,
    suscept,
    weight_active,
    weight_reactive,
):
    angle_diff = angle_from - angle_to
    cosine_diff = jnp.cos(angle_diff)
    sine_diff = jnp.sin(angle_diff)
    flow_along = conduct * cosine_diff + suscept * sine_diff
    flow_across = conduct * sine_diff - suscept * cosine_diff
    cross_term = magnitude_from * magnitude_to
    active_rows = (
        2.0 * conduct * magnitude_from - magnitude_to * flow_along,
        cross_term * flow_across,
        -magnitude_from * flow_along,
        -cross_term * flow_across,
    )
    reactive_rows = (
        -2.0 * suscept * magnitude_from - magnitude_to * flow_across,
        -cross_term * flow_along,
        -magnitude_from * flow_across,
        cross_term * flow_along,
    )

    def block_entry(left_index, right_index):
        return (
            weight_active * active_rows[left_index] * active_rows[right_index]
            + weight_reactive * reactive_rows[left_index] * reactive_rows[right_index]
        )

    from_block = jnp.stack([block_entry(0, 0), block_entry(0, 1), block_entry(1, 1)], axis=1)
    to_block = jnp.stack([block_entry(2, 2), block_entry(2, 3), block_entry(3, 3)], axis=1)
    cross_block = jnp.stack(
        [block_entry(0, 2), block_entry(0, 3), block_entry(1, 2), block_entry(1, 3)], axis=1
    )
    return (from_block, to_block, cross_block)


def apply_cross(matrix_block, vector):
    return jnp.stack(
        [
            matrix_block[:, 0] * vector[:, 0] + matrix_block[:, 1] * vector[:, 1],
            matrix_block[:, 2] * vector[:, 0] + matrix_block[:, 3] * vector[:, 1],
        ],
        axis=1,
    )


def apply_cross_transposed(matrix_block, vector):
    return jnp.stack(
        [
            matrix_block[:, 0] * vector[:, 0] + matrix_block[:, 2] * vector[:, 1],
            matrix_block[:, 1] * vector[:, 0] + matrix_block[:, 3] * vector[:, 1],
        ],
        axis=1,
    )


def scenario_sum(left_vec, right_vec):
    return jnp.sum(left_vec * right_vec, axis=(0, 1))


def widen(values):
    return values[None, None, :]


def body(
    volt_mag,
    volt_ang,
    gradient,
    branch_from,
    branch_to,
    branch_count,
    boundary,
    conductance,
    susceptance,
    duals,
    slacks,
    gen_bus,
    gen_curvature,
):
    bus_count = volt_mag.shape[0]
    ghost_count = boundary.shape[0] // 2
    extended_size = bus_count + 2 * ghost_count
    slot_count = branch_from.shape[0]
    left_list = boundary[:ghost_count]
    right_list = boundary[ghost_count:]
    left_ghost = slice(bus_count, bus_count + ghost_count)
    right_ghost = slice(bus_count + ghost_count, extended_size)
    return_plan = (
        (-1, left_ghost, right_list, right_ghost),
        (1, right_ghost, left_list, left_ghost),
    )

    def share_vector(values):
        pieces = [values]
        for direction in (1, -1):
            outgoing = jnp.take(values, right_list if direction == 1 else left_list, axis=0)
            pieces.append(shifted(outgoing, "net", direction))
        return jnp.concatenate(pieces, axis=0)

    bus_state = jnp.stack([volt_mag, volt_ang], axis=1)
    pieces = [bus_state]
    for share_direction in (1, -1):
        outgoing = jnp.take(bus_state, right_list if share_direction == 1 else left_list, axis=0)
        pieces.append(shifted(outgoing, "net", share_direction))
    extended_state = jnp.concatenate(pieces, axis=0)
    from_state = jnp.take(extended_state, branch_from, axis=0)
    to_state = jnp.take(extended_state, branch_to, axis=0)
    live_mask = (jnp.arange(slot_count) < branch_count[0]).astype(jnp.float32)[:, None]
    weight_active = live_mask * duals[0] / slacks[0]
    weight_reactive = live_mask * duals[1] / slacks[1]
    from_block, to_block, cross_block = branch_blocks(
        from_state[:, 0],
        from_state[:, 1],
        to_state[:, 0],
        to_state[:, 1],
        conductance[:, None],
        susceptance[:, None],
        weight_active,
        weight_reactive,
    )
    diag_extended = jax.ops.segment_sum(
        from_block, branch_from, num_segments=extended_size
    ) + jax.ops.segment_sum(to_block, branch_to, num_segments=extended_size)
    diag_local = diag_extended[:bus_count]
    for direction, ghost_rows, target_rows, source_rows in return_plan:
        arrived_diag = shifted(diag_extended[ghost_rows], "net", direction)
        diag_local = diag_local.at[target_rows].add(arrived_diag)
    gen_table = (gen_bus[None, :] == jnp.arange(bus_count)[:, None]).astype(jnp.float32)
    gen_sum = jnp.dot(gen_table, gen_curvature, precision=lax.Precision.HIGHEST)[:, None]
    barrier = barrier_weight / jnp.square(volt_mag - volt_low) + barrier_weight / jnp.square(
        volt_high - volt_mag
    )
    diag_vv = diag_local[:, 0] + barrier + gen_sum
    diag_va = diag_local[:, 1]
    diag_aa = diag_local[:, 2] + angle_reg + gen_sum
    determinant = diag_vv * diag_aa - diag_va * diag_va
    inverse_vv = diag_aa / determinant
    inverse_va = -diag_va / determinant
    inverse_aa = diag_vv / determinant

    def precondition(vector):
        return jnp.stack(
            [
                inverse_vv * vector[:, 0] + inverse_va * vector[:, 1],
                inverse_va * vector[:, 0] + inverse_aa * vector[:, 1],
            ],
            axis=1,
        )

    update_field = jnp.zeros_like(gradient)
    residual = gradient

    def energy_of(residual_now, scaled_now):
        return lax.psum(scenario_sum(residual_now, scaled_now), "net")

    scaled = precondition(residual)
    search = scaled
    energy = energy_of(residual, scaled)
    for iteration in range(ITERS):
        extended = share_vector(search)
        from_values = jnp.take(extended, branch_from, axis=0)
        to_values = jnp.take(extended, branch_to, axis=0)
        from_terms = apply_cross(cross_block, to_values)
        to_terms = apply_cross_transposed(cross_block, from_values)
        result = jnp.stack(
            [
                diag_vv * search[:, 0] + diag_va * search[:, 1],
                diag_va * search[:, 0] + diag_aa * search[:, 1],
            ],
            axis=1,
        )
        summed = jax.ops.segment_sum(
            from_terms, branch_from, num_segments=extended_size
        ) + jax.ops.segment_sum(to_terms, branch_to, num_segments=extended_size)
        local_sum = result + summed[:bus_count]
        for apply_direction, apply_ghost_rows, apply_target_rows, apply_source_rows in return_plan:
            arrived = shifted(summed[apply_ghost_rows], "net", apply_direction)
            local_sum = local_sum.at[apply_target_rows].add(arrived)
        step_size = energy / lax.psum(scenario_sum(search, local_sum), "net")
        update_field = update_field + widen(step_size) * search
        residual = residual - widen(step_size) * local_sum
        if iteration + 1 < ITERS:
            scaled = precondition(residual)
            energy_next = energy_of(residual, scaled)
            search = scaled + widen(energy_next / energy) * search
            energy = energy_next
    return (update_field, residual)


LANES = 128
ROWS = 8
TILE_A, TILE_B, TILE_C = 0, 2, 4
TILE_LOCAL = 6
TILE_INDEX = 9
PAYLOAD_ROWS = 11 * ROWS
CHUNK_FIELDS = ["gradient", "diag", "diag_off", "vm", "cosv", "sinv"]
CHUNK_FIELDS += ["wp", "wq", "g", "b", "extent"]
SLOT_FIELDS = ["local_main", "local_off", "at_from", "at_to"]
SET_RANKS = 4


def fits_fast_path(blocks, bus_count, ghost_count, slot_count, gen_count, scen_count):
    return (
        blocks == 8
        and scen_count == 2
        and bus_count == 2 * ghost_count
        and ghost_count <= LANES
        and 2 * LANES < slot_count < 3 * LANES
        and gen_count <= LANES
    )


def iota(shape, dim):
    return lax.broadcasted_iota(jnp.int32, shape, dim)


def lane_take(table, index):
    return jnp.take_along_axis(table, index, axis=1, mode="promise_in_bounds")


def take_chunks(tables, index):
    lane = index & (LANES - 1)
    chunk = index >> 7
    out = lane_take(tables[0], lane)
    for number in range(1, len(tables)):
        out = jnp.where(chunk == number, lane_take(tables[number], lane), out)
    return out


def take_listed(tables, index, default=0):
    lane = index & (LANES - 1)
    chunk = index >> 7
    out = jnp.full(index.shape, default, tables[0].dtype)
    for number, table in enumerate(tables):
        out = jnp.where(chunk == number, lane_take(table, lane), out)
    return out


def tall(row):
    return jnp.broadcast_to(row, (ROWS, LANES))


def column(row):
    return jnp.transpose(jnp.broadcast_to(row, (LANES, LANES)))


def block_entries(vi, ci, si, vj, cj, sj, g, b, wp, wq):
    cosine = ci * cj + si * sj
    sine = si * cj - ci * sj
    along = g * cosine + b * sine
    across = g * sine - b * cosine
    cross = vi * vj
    p0 = 2.0 * g * vi - vj * along
    p1 = cross * across
    p2 = -vi * along
    q0 = -2.0 * b * vi - vj * across
    q1 = -cross * along
    q2 = -vi * across

    def entry(pa, pb, qa, qb):
        return wp * pa * pb + wq * qa * qb

    return (
        entry(p0, p0, q0, q0),
        entry(p0, p1, q0, q1),
        entry(p1, p1, q1, q1),
        entry(p2, p2, q2, q2),
        entry(p1, p2, q1, q2),
        entry(p0, p2, q0, q2),
    )


def prepare_kernel(
    vm_ref,
    va_ref,
    grad_ref,
    from_ref,
    to_ref,
    count_ref,
    bound_ref,
    g_ref,
    b_ref,
    duals_ref,
    slacks_ref,
    gen_bus_ref,
    gen_curv_ref,
    out_ref,
    pos_ref,
    bus_scr,
    branch_scr,
    index_scr,
):
    bus_count = vm_ref.shape[1]
    ghost_count = bus_count // 2
    slot_count = from_ref.shape[0]
    gen_count = gen_bus_ref.shape[0]
    none = 3 * LANES - 1
    live_count = count_ref[...][None]

    bus_scr[...] = jnp.zeros_like(bus_scr)
    branch_scr[...] = jnp.zeros_like(branch_scr)
    index_scr[...] = jnp.full_like(index_scr, -9)
    for copy in range(4):
        bus_scr[2 * copy : 2 * copy + 2, :bus_count] = vm_ref[...]
        bus_scr[8 + 2 * copy : 10 + 2 * copy, :bus_count] = va_ref[...]
    for comp in range(2):
        bus_scr[16 + 2 * comp : 18 + 2 * comp, :bus_count] = grad_ref[comp]
    live = iota((2, slot_count), 1) < live_count
    for kind in range(2):
        weight = jnp.where(live, duals_ref[kind] / slacks_ref[kind], 0.0)
        branch_scr[2 * kind : 2 * kind + 2, :slot_count] = weight
    branch_scr[4:5, :slot_count] = g_ref[...][None]
    branch_scr[5:6, :slot_count] = b_ref[...][None]
    branch_scr[6:7, :slot_count] = from_ref[...][None].astype(jnp.float32)
    branch_scr[7:8, :slot_count] = to_ref[...][None].astype(jnp.float32)
    bus_scr[20:21, :gen_count] = gen_curv_ref[...][None]
    index_scr[0:1, :slot_count] = from_ref[...][None]
    index_scr[1:2, :slot_count] = to_ref[...][None]
    index_scr[2:3, :bus_count] = bound_ref[...][None]
    index_scr[3:4, :gen_count] = gen_bus_ref[...][None]

    def tiles(ref, first, chunks):
        return [ref[first : first + ROWS, LANES * c : LANES * (c + 1)] for c in range(chunks)]

    def row(ref, number, chunk):
        return ref[number : number + 1, LANES * chunk : LANES * (chunk + 1)]

    lane = iota((ROWS, LANES), 1)
    sub = iota((ROWS, LANES), 0)
    lane_row = iota((1, LANES), 1)
    sub_col = iota((LANES, LANES), 0).astype(jnp.float32)
    inside = lane < ghost_count

    raw_bound = [tall(row(index_scr, 2, c)) for c in range(2)]
    bound = [jnp.where(inside, take_chunks(raw_bound, lane + h * ghost_count), -1) for h in range(2)]
    fetch = [jnp.maximum(b, 0) for b in bound]
    bound_row = [b[0:1].astype(jnp.float32) for b in bound]
    vm_raw, va_raw, grad_raw = (tiles(bus_scr, 8 * f, 2) for f in range(3))
    vm = [jnp.where(inside, take_chunks(vm_raw, f), 1.0) for f in fetch]
    va = [jnp.where(inside, take_chunks(va_raw, f), 0.0) for f in fetch]
    grad = [jnp.where(inside, take_chunks(grad_raw, f), 0.0) for f in fetch]
    cosv = [jnp.cos(a) for a in va]
    sinv = [jnp.sin(a) for a in va]

    earlier = (iota((LANES, LANES), 0) < iota((LANES, LANES), 1)).astype(jnp.bfloat16)
    local, cross_key, place = [], [], []
    local_count = jnp.zeros((1, 1), jnp.float32)
    for c in range(3):
        slot = lane_row + LANES * c
        alive = (slot < live_count) & (slot < slot_count)
        to_raw = row(index_scr, 1, c)
        cross_key.append(jnp.where(alive, to_raw, 9999).astype(jnp.float32))
        keep = jnp.where(alive & (to_raw < bus_count), 1.0, 0.0)
        before = jnp.dot(
            tall(keep).astype(jnp.bfloat16), earlier, preferred_element_type=jnp.float32
        )
        place.append(jnp.where(keep > 0.0, before[0:1] + local_count, -1.0))
        local_count = local_count + jnp.sum(keep, axis=1, keepdims=True)
    place_col = [column(p) for p in place]
    lane_f = lane_row.astype(jnp.float32)
    branch_tiles = tiles(branch_scr, 0, 3)

    def lowest(masks):
        found = functools.reduce(
            jnp.minimum,
            [jnp.where(m, sub_col + float(LANES * c), float(none)) for c, m in masks],
        )
        return jnp.min(found, axis=0, keepdims=True)

    packed, from_key, to_key = [], [], []
    for c in range(3):
        source = lowest([(d, place_col[d] == lane_f + float(LANES * c)) for d in range(c, 3)])
        tile = take_chunks(branch_tiles, tall(source).astype(jnp.int32))
        packed.append(tile)
        empty = source == float(none)
        from_key.append(jnp.where(empty, 9998.0, tile[6:7]))
        to_key.append(jnp.where(empty, 9999.0, tile[7:8]))
    from_col = [column(k) for k in from_key]
    to_col = [column(k) for k in to_key]
    cross_col = [column(k) for k in cross_key[:2]]
    bound_col = [column(b) for b in bound_row]
    gen_col = column(row(index_scr, 3, 0).astype(jnp.float32))
    curv_col = column(row(bus_scr, 20, 0))

    def links(keys, cols):
        heads, counts = [], []
        for h in range(2):
            equal = [cols[c] == bound_row[h] for c in range(3)]
            heads.append(lowest(list(enumerate(equal))))
            counts.append(
                jnp.sum(
                    functools.reduce(jnp.add, [jnp.where(e, 1.0, 0.0) for e in equal]),
                    axis=0,
                    keepdims=True,
                )
            )
        nexts = []
        for c in range(3):
            later = [(c, (cols[c] == keys[c]) & (sub_col > lane_f))]
            later += [(d, cols[d] == keys[c]) for d in range(c + 1, 3)]
            nexts.append(lowest(later))
        return heads, nexts, jnp.maximum(counts[0], counts[1])

    head_f, next_f, count_f = links(from_key, from_col)
    head_t, next_t, count_t = links(to_key, to_col)
    degree = jnp.max(jnp.maximum(count_f, count_t))

    def position(keys):
        found = [
            jnp.where(bound_col[h] == keys, sub_col + float(LANES * h), 0.0) for h in range(2)
        ]
        return jnp.max(jnp.maximum(found[0], found[1]), axis=0, keepdims=True)

    pos_f = [position(k) for k in from_key]
    pos_t = [position(k) for k in to_key]
    for m in range(2):
        pos_ref[m : m + 1, :] = position((lane_row + LANES * m).astype(jnp.float32)).astype(jnp.int32)

    cross = []
    for h in range(2):
        target = jnp.where(lane_row < ghost_count, bus_count + h * ghost_count + lane_row, -5)
        slot = lowest([(c, cross_col[c] == target.astype(jnp.float32)) for c in range(2)])
        cross.append(take_chunks(branch_tiles, tall(slot).astype(jnp.int32)))

    gens = [
        jnp.sum(jnp.where(gen_col == bound_row[h], curv_col, 0.0), axis=0, keepdims=True)
        for h in range(2)
    ]

    pair = sub & 3

    def every_pair(x):
        x = jnp.where(sub < 2, x, pltpu.roll(x, 2, 0))
        return jnp.where(sub < 4, x, pltpu.roll(x, 4, 0))

    from_table, to_table = [], []
    for c in range(3):
        at_f = tall(pos_f[c]).astype(jnp.int32)
        at_t = tall(pos_t[c]).astype(jnp.int32)
        h00, h01, h11, h22, h12, h02 = block_entries(
            *(take_chunks(t, at_f) for t in (vm, cosv, sinv)),
            *(take_chunks(t, at_t) for t in (vm, cosv, sinv)),
            tall(packed[c][4:5]),
            tall(packed[c][5:6]),
            every_pair(packed[c]),
            every_pair(pltpu.roll(packed[c], 6, 0)),
        )
        main = jnp.where(pair < 2, h02, -h11)
        off = jnp.where(pair < 2, -h01, h12)
        first = ROWS * (TILE_LOCAL + c)
        out_ref[first : first + ROWS, :] = jnp.where(sub < 4, main, off)
        from_table.append(jnp.where(sub < 2, h00, jnp.where(sub < 4, h01, h11)))
        to_table.append(jnp.where(sub < 2, h22, jnp.where(sub < 4, -h12, h11)))

    next_ft = [tall(n).astype(jnp.int32) for n in next_f]
    next_tt = [tall(n).astype(jnp.int32) for n in next_t]

    def scattered(chunks):
        def add_rank(_, carry):
            acc, at_f, at_t = carry
            acc = tuple(
                acc[h]
                + take_listed(from_table[:chunks], at_f[h])
                + take_listed(to_table[:chunks], at_t[h])
                for h in range(2)
            )
            at_f = tuple(take_listed(next_ft[:chunks], at_f[h], none) for h in range(2))
            at_t = tuple(take_listed(next_tt[:chunks], at_t[h], none) for h in range(2))
            return acc, at_f, at_t

        zero = jnp.zeros((ROWS, LANES), jnp.float32)
        heads = (
            tuple(tall(x).astype(jnp.int32) for x in head_f),
            tuple(tall(x).astype(jnp.int32) for x in head_t),
        )
        return lax.fori_loop(0, degree.astype(jnp.int32), add_rank, ((zero, zero), *heads))[0]

    total_local = jnp.max(local_count)
    acc = lax.cond(total_local <= 2.0 * LANES, lambda: scattered(2), lambda: scattered(3))

    for h in range(2):
        below = vm[h] - volt_low
        above = volt_high - vm[h]
        barrier = barrier_weight / (below * below) + barrier_weight / (above * above)
        diag_vv = pltpu.roll(acc[h], 4, 0) + barrier + gens[h]
        diag_aa = pltpu.roll(acc[h], 2, 0) + angle_reg + gens[h]
        diag_va = pltpu.roll(acc[h], 6, 0)
        first = ROWS * (TILE_A + h)
        out_ref[first : first + ROWS, :] = jnp.where(
            sub < 4, grad[h], jnp.where(sub < 6, diag_vv, diag_aa)
        )
        first = ROWS * (TILE_B + h)
        out_ref[first : first + ROWS, :] = jnp.where(
            sub < 2, diag_va, jnp.where(sub < 4, vm[h], jnp.where(sub < 6, cosv[h], sinv[h]))
        )
        first = ROWS * (TILE_C + h)
        out_ref[first : first + ROWS, :] = jnp.where(
            sub < 6, cross[h], jnp.where(sub == 6, degree, total_local)
        )
    first = ROWS * TILE_INDEX
    for offset, value in enumerate(pos_f + pos_t + head_f + head_t + next_f + next_t):
        out_ref[first + offset : first + offset + 1, :] = value


def solve_kernel(me_ref, pos_ref, *refs):
    *all_refs, step_ref, residual_ref, chain_scr, row_scr, field_scr, step_scr, residual_scr = refs
    blocks = len(all_refs)
    me = me_ref[0]
    half = blocks // 2
    bus_count = step_ref.shape[2]
    lane_pairs = [(j, h) for j in range(half) for h in range(2)]
    sub = iota((ROWS, LANES), 0)
    low = sub < 4
    even = (sub & 3) < 2

    def swap_component(x):
        return jnp.where(even, pltpu.roll(x, 6, 0), pltpu.roll(x, 2, 0))

    def swap_block(x):
        return pltpu.roll(x, 4, 0)

    upper = me >= half
    mine = jnp.where(upper, blocks - 1 - me, me)
    near = low != upper

    def halves(tile, j):
        here = all_refs[j][ROWS * tile : ROWS * (tile + 1), :]
        there = all_refs[blocks - 1 - j][ROWS * tile : ROWS * (tile + 1), :]
        first = jnp.where(upper, there, here)
        second = jnp.where(upper, here, there)
        return (
            jnp.where(low, first, swap_block(second)),
            jnp.where(low, swap_block(first), second),
        )

    def quarters(x):
        return (
            jnp.where(even, x, pltpu.roll(x, 2, 0)),
            jnp.where(even, pltpu.roll(x, 6, 0), x),
        )

    def single(number, j):
        return jnp.where(
            near,
            tall(all_refs[j][number : number + 1, :]),
            tall(all_refs[blocks - 1 - j][number : number + 1, :]),
        )

    def across(field):
        out = {}
        for j in range(half):
            inner = [
                field[j + 1, 1 - h] if j + 1 < half else swap_block(field[j, 1 - h])
                for h in range(2)
            ]
            outer = [field[j - 1, 1 - h] if j > 0 else 0.0 for h in range(2)]
            out[j, 0] = jnp.where(low, outer[0], inner[0])
            out[j, 1] = jnp.where(low, inner[1], outer[1])
        return out

    base = ROWS * TILE_INDEX
    names = [(name, h) for name in CHUNK_FIELDS for h in range(2)]
    names += [(name, c) for name in SLOT_FIELDS for c in range(3)]
    place = {name: number for number, name in enumerate(names)}
    for j in range(half):
        found = {}
        for h in range(2):
            found["gradient", h], found["diag", h] = halves(TILE_A + h, j)
            first, second = halves(TILE_B + h, j)
            found["diag_off", h], found["vm", h] = quarters(first)
            found["cosv", h], found["sinv", h] = quarters(second)
            first, _ = halves(TILE_C + h, j)
            found["wp", h], found["wq", h] = quarters(first)
            found["g", h] = single(ROWS * (TILE_C + h) + 4, j)
            found["b", h] = single(ROWS * (TILE_C + h) + 5, j)
            found["extent", h] = single(ROWS * TILE_C + 6 + h, j)
        for c in range(3):
            found["local_main", c], found["local_off", c] = halves(TILE_LOCAL + c, j)
            found["at_from", c] = single(base + c, j)
            found["at_to", c] = single(base + 3 + c, j)
        for name, number in place.items():
            field_scr[number, j ^ mine] = found[name]

    def load(name, chunks):
        return {
            (j, c): field_scr[place[name, c], j] for j in range(half) for c in range(chunks)
        }

    def load_index(name, chunks):
        return {key: value.astype(jnp.int32) for key, value in load(name, chunks).items()}

    gradient, diag, diag_off, vm, cosv, sinv, wp, wq, g, b, extent = (
        load(name, 2) for name in CHUNK_FIELDS
    )
    vm_to, cos_to, sin_to = across(vm), across(cosv), across(sinv)
    to_diag, to_off, main, off = {}, {}, {}, {}
    for key in lane_pairs:
        h00, h01, h11, h22, h12, h02 = block_entries(
            vm[key],
            cosv[key],
            sinv[key],
            vm_to[key],
            cos_to[key],
            sin_to[key],
            g[key],
            b[key],
            wp[key],
            wq[key],
        )
        diag[key] = diag[key] + jnp.where(even, h00, h11)
        diag_off[key] = diag_off[key] + h01
        to_diag[key] = jnp.where(even, h22, h11)
        to_off[key] = -h12
        main[key] = jnp.where(even, h02, -h11)
        off[key] = jnp.where(even, -h01, h12)
    to_diag, to_off = across(to_diag), across(to_off)
    main_to = across(main)
    off_to = across({key: swap_component(off[key]) for key in lane_pairs})
    inverse, inverse_off = {}, {}
    for key in lane_pairs:
        diag[key] = diag[key] + to_diag[key]
        diag_off[key] = diag_off[key] + to_off[key]
        main[key] = main[key] + main_to[key]
        off[key] = off[key] + off_to[key]
        flipped = swap_component(diag[key])
        determinant = diag[key] * flipped - diag_off[key] * diag_off[key]
        inverse[key] = flipped / determinant
        inverse_off[key] = -diag_off[key] / determinant

    local_main, local_off = (load(name, 3) for name in SLOT_FIELDS[:2])
    at_from, at_to = (load_index(name, 3) for name in SLOT_FIELDS[2:])

    def largest(h, pairs):
        return jnp.max(functools.reduce(jnp.maximum, [extent[j, h] for j in pairs]))

    outer_rank = largest(0, [0]).astype(jnp.int32)
    inner_rank = largest(0, range(1, half)).astype(jnp.int32)
    few = (largest(1, [0]) <= 2.0 * LANES) & (largest(1, range(1, half)) <= 1.0 * LANES)

    for number in range(10):
        for s, ref in enumerate(all_refs):
            row_scr[number, s : s + 1, :] = ref[base + 6 + number : base + 7 + number, :]
    links = [row_scr[number].astype(jnp.int32) for number in range(10)]
    heads, next_f, next_t = links[:4], links[4:7], links[7:]

    def follow(rank, ends):
        for kind in range(4):
            row_scr[kind] = ends[kind].astype(jnp.float32)
            for j in range(half):
                here = tall(row_scr[kind, j : j + 1, :])
                there = tall(row_scr[kind, blocks - 1 - j : blocks - j, :])
                chain_scr[rank, kind, j ^ mine] = jnp.where(near, here, there).astype(jnp.int32)
        return tuple(
            take_chunks(next_f if kind < 2 else next_t, ends[kind]) for kind in range(4)
        )

    ends = tuple(heads)
    for rank in range(SET_RANKS):
        ends = follow(rank, ends)
    lax.fori_loop(SET_RANKS, jnp.maximum(outer_rank, inner_rank), follow, ends)

    def local_sums(v, sums, outer_chunks, inner_chunks):
        chunks = [outer_chunks] + [inner_chunks] * (half - 1)
        to_from, to_to = {}, {}
        for j in range(half):
            table = [v[j, 0], v[j, 1]]
            for c in range(chunks[j]):
                far = take_chunks(table, at_to[j, c])
                near = take_chunks(table, at_from[j, c])
                to_from[j, c] = local_main[j, c] * far + local_off[j, c] * swap_component(far)
                to_to[j, c] = local_main[j, c] * near + swap_component(local_off[j, c] * near)

        def add_rank(pairs, rank, sums):
            sums = list(sums)
            for number, (j, h) in enumerate(lane_pairs):
                if j in pairs:
                    for offset, terms in ((0, to_from), (2, to_to)):
                        sums[number] += take_listed(
                            [terms[j, c] for c in range(chunks[j])], chain_scr[rank, offset + h, j]
                        )
            return tuple(sums)

        every = functools.partial(add_rank, range(half))
        for rank in range(SET_RANKS):
            sums = every(rank, sums)
        sums = lax.fori_loop(SET_RANKS, inner_rank, every, sums)
        return lax.fori_loop(
            jnp.maximum(inner_rank, SET_RANKS), outer_rank, functools.partial(add_rank, [0]), sums
        )

    def operator(v):
        flipped = {key: swap_component(v[key]) for key in lane_pairs}
        v_to, flipped_to = across(v), across(flipped)
        out = tuple(
            diag[key] * v[key]
            + diag_off[key] * flipped[key]
            + main[key] * v_to[key]
            + off[key] * flipped_to[key]
            for key in lane_pairs
        )
        sums = lax.cond(
            few, lambda: local_sums(v, out, 2, 1), lambda: local_sums(v, out, 3, 3)
        )
        return dict(zip(lane_pairs, sums))

    def scenario_total(left, right):
        total = functools.reduce(jnp.add, [left[key] * right[key] for key in lane_pairs])
        total = total + pltpu.roll(total, 2, 0)
        total = total + pltpu.roll(total, 4, 0)
        return jnp.broadcast_to(jnp.sum(total, axis=1, keepdims=True), (ROWS, LANES))

    def precondition(v):
        return {
            key: inverse[key] * v[key] + inverse_off[key] * swap_component(v[key])
            for key in lane_pairs
        }

    residual = gradient
    search = precondition(residual)
    energy = scenario_total(residual, search)
    update = None
    for iteration in range(ITERS):
        image = operator(search)
        step_size = energy / scenario_total(search, image)
        if update is None:
            update = {key: step_size * search[key] for key in lane_pairs}
        else:
            update = {key: update[key] + step_size * search[key] for key in lane_pairs}
        residual = {key: residual[key] - step_size * image[key] for key in lane_pairs}
        if iteration + 1 < ITERS:
            scaled = precondition(residual)
            energy_next = scenario_total(residual, scaled)
            ratio = energy_next / energy
            search = {key: scaled[key] + ratio * search[key] for key in lane_pairs}
            energy = energy_next

    for field, keep_scr, out_ref in (
        (update, step_scr, step_ref),
        (residual, residual_scr, residual_ref),
    ):
        for j, h in lane_pairs:
            keep_scr[j, h] = field[j, h]
        own = []
        for h in range(2):
            tile = keep_scr[mine, h]
            own.append(jnp.where(upper, swap_block(tile), tile))
        for m in range(2):
            width = min(LANES, bus_count - LANES * m)
            values = take_chunks(own, tall(pos_ref[m : m + 1, :]))
            for comp in range(2):
                out_ref[comp, :, LANES * m : LANES * m + width] = values[
                    2 * comp : 2 * comp + 2, :width
                ]


def fast_body(
    volt_mag,
    volt_ang,
    gradient,
    branch_from,
    branch_to,
    branch_count,
    boundary,
    conductance,
    susceptance,
    duals,
    slacks,
    gen_bus,
    gen_curvature,
):
    bus_count = volt_mag.shape[0]
    slot_count = branch_from.shape[0]
    blocks = lax.axis_size("net")
    vmem = pl.BlockSpec(memory_space=pltpu.VMEM)
    smem = pl.BlockSpec(memory_space=pltpu.SMEM)
    payload, position = pl.pallas_call(
        prepare_kernel,
        out_shape=(
            pltpu.VMEM((PAYLOAD_ROWS, LANES), jnp.float32),
            pltpu.VMEM((2, LANES), jnp.int32),
        ),
        in_specs=[vmem] * 13,
        out_specs=(vmem, vmem),
        scratch_shapes=[
            pltpu.VMEM((24, 2 * LANES), jnp.float32),
            pltpu.VMEM((8, 3 * LANES), jnp.float32),
            pltpu.VMEM((8, 3 * LANES), jnp.int32),
        ],
        name="prepare",
    )(
        volt_mag.T,
        volt_ang.T,
        jnp.transpose(gradient, (1, 2, 0)),
        branch_from,
        branch_to,
        branch_count,
        boundary,
        conductance,
        susceptance,
        jnp.transpose(duals, (0, 2, 1)),
        jnp.transpose(slacks, (0, 2, 1)),
        gen_bus,
        gen_curvature,
    )
    def passed(block, other):
        return lax.ppermute(block, "net", [(i, i ^ other) for i in range(blocks)])

    gathered = {0: payload}
    for other in range(2, blocks, 2):
        gathered[other] = passed(payload, other)
    for other in range(0, blocks, 2):
        gathered[other + 1] = passed(gathered[other], 1)
    gathered = [gathered[other] for other in range(blocks)]
    me = lax.axis_index("net").astype(jnp.int32)[None]
    tile_pairs = (blocks // 2, 2, ROWS, LANES)
    field = jax.ShapeDtypeStruct((2, 2, bus_count), jnp.float32)
    step, residual = pl.pallas_call(
        solve_kernel,
        out_shape=(field, field),
        in_specs=[smem] + [vmem] * (1 + blocks),
        out_specs=(vmem, vmem),
        scratch_shapes=[
            pltpu.VMEM((slot_count, 4, blocks // 2, ROWS, LANES), jnp.int32),
            pltpu.VMEM((10, blocks, LANES), jnp.float32),
            pltpu.VMEM(
                (2 * len(CHUNK_FIELDS) + 3 * len(SLOT_FIELDS), blocks // 2, ROWS, LANES),
                jnp.float32,
            ),
            pltpu.VMEM(tile_pairs, jnp.float32),
            pltpu.VMEM(tile_pairs, jnp.float32),
        ],
        compiler_params=pltpu.CompilerParams(vmem_limit_bytes=40 * 2**20),
        name="solve",
    )(me, position, *gathered)
    return jnp.transpose(step, (2, 0, 1)), jnp.transpose(residual, (2, 0, 1))


def any_body(*arrays):
    volt_mag, boundary, branch_from, gen_bus = arrays[0], arrays[6], arrays[3], arrays[11]
    fast = fits_fast_path(
        lax.axis_size("net"),
        volt_mag.shape[0],
        boundary.shape[0] // 2,
        branch_from.shape[0],
        gen_bus.shape[0],
        volt_mag.shape[1],
    )
    return fast_body(*arrays) if fast else body(*arrays)


def solution(mesh):
    placed = (
        P("net", "scen"),
        P("net", "scen"),
        P("net", None, "scen"),
        P("net"),
        P("net"),
        P("net"),
        P("net"),
        P("net"),
        P("net"),
        P(None, "net", "scen"),
        P(None, "net", "scen"),
        P("net"),
        P("net"),
    )
    return jax.shard_map(
        any_body,
        mesh=mesh,
        in_specs=placed,
        out_specs=(P("net", None, "scen"), P("net", None, "scen")),
        check_vma=False,
    )
```

```python
import functools

import jax
import jax.numpy as jnp
from jax import lax
from jax.experimental import pallas as pl
from jax.experimental.pallas import tpu as pltpu
from jax.sharding import PartitionSpec as P

ITERS = 4


barrier_weight = 0.01
volt_low = 0.9
volt_high = 1.1
angle_reg = 0.5


def shifted(array, axis, by):
    peers = lax.axis_size(axis)
    pairs = [(i, i + by) for i in range(peers) if 0 <= i + by < peers]
    return lax.ppermute(array, axis, pairs)


def branch_blocks(
    magnitude_from,
    angle_from,
    magnitude_to,
    angle_to,
    conduct,
    suscept,
    weight_active,
    weight_reactive,
):
    angle_diff = angle_from - angle_to
    cosine_diff = jnp.cos(angle_diff)
    sine_diff = jnp.sin(angle_diff)
    flow_along = conduct * cosine_diff + suscept * sine_diff
    flow_across = conduct * sine_diff - suscept * cosine_diff
    cross_term = magnitude_from * magnitude_to
    active_rows = (
        2.0 * conduct * magnitude_from - magnitude_to * flow_along,
        cross_term * flow_across,
        -magnitude_from * flow_along,
        -cross_term * flow_across,
    )
    reactive_rows = (
        -2.0 * suscept * magnitude_from - magnitude_to * flow_across,
        -cross_term * flow_along,
        -magnitude_from * flow_across,
        cross_term * flow_along,
    )

    def block_entry(left_index, right_index):
        return (
            weight_active * active_rows[left_index] * active_rows[right_index]
            + weight_reactive * reactive_rows[left_index] * reactive_rows[right_index]
        )

    from_block = jnp.stack([block_entry(0, 0), block_entry(0, 1), block_entry(1, 1)], axis=1)
    to_block = jnp.stack([block_entry(2, 2), block_entry(2, 3), block_entry(3, 3)], axis=1)
    cross_block = jnp.stack(
        [block_entry(0, 2), block_entry(0, 3), block_entry(1, 2), block_entry(1, 3)], axis=1
    )
    return (from_block, to_block, cross_block)


def apply_cross(matrix_block, vector):
    return jnp.stack(
        [
            matrix_block[:, 0] * vector[:, 0] + matrix_block[:, 1] * vector[:, 1],
            matrix_block[:, 2] * vector[:, 0] + matrix_block[:, 3] * vector[:, 1],
        ],
        axis=1,
    )


def apply_cross_transposed(matrix_block, vector):
    return jnp.stack(
        [
            matrix_block[:, 0] * vector[:, 0] + matrix_block[:, 2] * vector[:, 1],
            matrix_block[:, 1] * vector[:, 0] + matrix_block[:, 3] * vector[:, 1],
        ],
        axis=1,
    )


def scenario_sum(left_vec, right_vec):
    return jnp.sum(left_vec * right_vec, axis=(0, 1))


def widen(values):
    return values[None, None, :]


def body(
    volt_mag,
    volt_ang,
    gradient,
    branch_from,
    branch_to,
    branch_count,
    boundary,
    conductance,
    susceptance,
    duals,
    slacks,
    gen_bus,
    gen_curvature,
):
    bus_count = volt_mag.shape[0]
    ghost_count = boundary.shape[0] // 2
    extended_size = bus_count + 2 * ghost_count
    slot_count = branch_from.shape[0]
    left_list = boundary[:ghost_count]
    right_list = boundary[ghost_count:]
    left_ghost = slice(bus_count, bus_count + ghost_count)
    right_ghost = slice(bus_count + ghost_count, extended_size)
    return_plan = (
        (-1, left_ghost, right_list, right_ghost),
        (1, right_ghost, left_list, left_ghost),
    )

    def share_vector(values):
        pieces = [values]
        for direction in (1, -1):
            outgoing = jnp.take(values, right_list if direction == 1 else left_list, axis=0)
            pieces.append(shifted(outgoing, "net", direction))
        return jnp.concatenate(pieces, axis=0)

    bus_state = jnp.stack([volt_mag, volt_ang], axis=1)
    pieces = [bus_state]
    for share_direction in (1, -1):
        outgoing = jnp.take(bus_state, right_list if share_direction == 1 else left_list, axis=0)
        pieces.append(shifted(outgoing, "net", share_direction))
    extended_state = jnp.concatenate(pieces, axis=0)
    from_state = jnp.take(extended_state, branch_from, axis=0)
    to_state = jnp.take(extended_state, branch_to, axis=0)
    live_mask = (jnp.arange(slot_count) < branch_count[0]).astype(jnp.float32)[:, None]
    weight_active = live_mask * duals[0] / slacks[0]
    weight_reactive = live_mask * duals[1] / slacks[1]
    from_block, to_block, cross_block = branch_blocks(
        from_state[:, 0],
        from_state[:, 1],
        to_state[:, 0],
        to_state[:, 1],
        conductance[:, None],
        susceptance[:, None],
        weight_active,
        weight_reactive,
    )
    diag_extended = jax.ops.segment_sum(
        from_block, branch_from, num_segments=extended_size
    ) + jax.ops.segment_sum(to_block, branch_to, num_segments=extended_size)
    diag_local = diag_extended[:bus_count]
    for direction, ghost_rows, target_rows, source_rows in return_plan:
        arrived_diag = shifted(diag_extended[ghost_rows], "net", direction)
        diag_local = diag_local.at[target_rows].add(arrived_diag)
    gen_table = (gen_bus[None, :] == jnp.arange(bus_count)[:, None]).astype(jnp.float32)
    gen_sum = jnp.dot(gen_table, gen_curvature, precision=lax.Precision.HIGHEST)[:, None]
    barrier = barrier_weight / jnp.square(volt_mag - volt_low) + barrier_weight / jnp.square(
        volt_high - volt_mag
    )
    diag_vv = diag_local[:, 0] + barrier + gen_sum
    diag_va = diag_local[:, 1]
    diag_aa = diag_local[:, 2] + angle_reg + gen_sum
    determinant = diag_vv * diag_aa - diag_va * diag_va
    inverse_vv = diag_aa / determinant
    inverse_va = -diag_va / determinant
    inverse_aa = diag_vv / determinant

    def precondition(vector):
        return jnp.stack(
            [
                inverse_vv * vector[:, 0] + inverse_va * vector[:, 1],
                inverse_va * vector[:, 0] + inverse_aa * vector[:, 1],
            ],
            axis=1,
        )

    update_field = jnp.zeros_like(gradient)
    residual = gradient

    def energy_of(residual_now, scaled_now):
        return lax.psum(scenario_sum(residual_now, scaled_now), "net")

    scaled = precondition(residual)
    search = scaled
    energy = energy_of(residual, scaled)
    for iteration in range(ITERS):
        extended = share_vector(search)
        from_values = jnp.take(extended, branch_from, axis=0)
        to_values = jnp.take(extended, branch_to, axis=0)
        from_terms = apply_cross(cross_block, to_values)
        to_terms = apply_cross_transposed(cross_block, from_values)
        result = jnp.stack(
            [
                diag_vv * search[:, 0] + diag_va * search[:, 1],
                diag_va * search[:, 0] + diag_aa * search[:, 1],
            ],
            axis=1,
        )
        summed = jax.ops.segment_sum(
            from_terms, branch_from, num_segments=extended_size
        ) + jax.ops.segment_sum(to_terms, branch_to, num_segments=extended_size)
        local_sum = result + summed[:bus_count]
        for apply_direction, apply_ghost_rows, apply_target_rows, apply_source_rows in return_plan:
            arrived = shifted(summed[apply_ghost_rows], "net", apply_direction)
            local_sum = local_sum.at[apply_target_rows].add(arrived)
        step_size = energy / lax.psum(scenario_sum(search, local_sum), "net")
        update_field = update_field + widen(step_size) * search
        residual = residual - widen(step_size) * local_sum
        if iteration + 1 < ITERS:
            scaled = precondition(residual)
            energy_next = energy_of(residual, scaled)
            search = scaled + widen(energy_next / energy) * search
            energy = energy_next
    return (update_field, residual)


LANES = 128
ROWS = 8
TILE_A, TILE_B, TILE_C = 0, 2, 4
TILE_LOCAL = 6
TILE_INDEX = 9
PAYLOAD_ROWS = 11 * ROWS
CHUNK_FIELDS = ["gradient", "diag", "diag_off", "vm", "cosv", "sinv"]
CHUNK_FIELDS += ["wp", "wq", "g", "b", "extent"]
SLOT_FIELDS = ["local_main", "local_off", "at_from", "at_to"]
SET_RANKS = 4
SET_RANKS_OUTER = 6


def fits_fast_path(blocks, bus_count, ghost_count, slot_count, gen_count, scen_count):
    return (
        blocks == 8
        and scen_count == 2
        and bus_count == 2 * ghost_count
        and ghost_count <= LANES
        and 2 * LANES < slot_count < 3 * LANES
        and gen_count <= LANES
    )


def iota(shape, dim):
    return lax.broadcasted_iota(jnp.int32, shape, dim)


def lane_take(table, index):
    return jnp.take_along_axis(table, index, axis=1, mode="promise_in_bounds")


def take_chunks(tables, index):
    lane = index & (LANES - 1)
    chunk = index >> 7
    out = lane_take(tables[0], lane)
    for number in range(1, len(tables)):
        out = jnp.where(chunk == number, lane_take(tables[number], lane), out)
    return out


def take_listed(tables, index, default=0):
    lane = index & (LANES - 1)
    chunk = index >> 7
    out = jnp.full(index.shape, default, tables[0].dtype)
    for number, table in enumerate(tables):
        out = jnp.where(chunk == number, lane_take(table, lane), out)
    return out


def tall(row):
    return jnp.broadcast_to(row, (ROWS, LANES))


def column(row):
    return jnp.transpose(jnp.broadcast_to(row, (LANES, LANES)))


def block_entries(vi, ci, si, vj, cj, sj, g, b, wp, wq):
    cosine = ci * cj + si * sj
    sine = si * cj - ci * sj
    along = g * cosine + b * sine
    across = g * sine - b * cosine
    cross = vi * vj
    p0 = 2.0 * g * vi - vj * along
    p1 = cross * across
    p2 = -vi * along
    q0 = -2.0 * b * vi - vj * across
    q1 = -cross * along
    q2 = -vi * across

    def entry(pa, pb, qa, qb):
        return wp * pa * pb + wq * qa * qb

    return (
        entry(p0, p0, q0, q0),
        entry(p0, p1, q0, q1),
        entry(p1, p1, q1, q1),
        entry(p2, p2, q2, q2),
        entry(p1, p2, q1, q2),
        entry(p0, p2, q0, q2),
    )


def prepare_kernel(
    vm_ref,
    va_ref,
    grad_ref,
    from_ref,
    to_ref,
    count_ref,
    bound_ref,
    g_ref,
    b_ref,
    duals_ref,
    slacks_ref,
    gen_bus_ref,
    gen_curv_ref,
    out_ref,
    pos_ref,
    bus_scr,
    branch_scr,
    index_scr,
):
    bus_count = vm_ref.shape[1]
    ghost_count = bus_count // 2
    slot_count = from_ref.shape[0]
    gen_count = gen_bus_ref.shape[0]
    none = 3 * LANES - 1
    live_count = count_ref[...][None]

    bus_scr[...] = jnp.zeros_like(bus_scr)
    branch_scr[...] = jnp.zeros_like(branch_scr)
    index_scr[...] = jnp.full_like(index_scr, -9)
    for copy in range(4):
        bus_scr[2 * copy : 2 * copy + 2, :bus_count] = vm_ref[...]
        bus_scr[8 + 2 * copy : 10 + 2 * copy, :bus_count] = va_ref[...]
    for comp in range(2):
        bus_scr[16 + 2 * comp : 18 + 2 * comp, :bus_count] = grad_ref[comp]
    live = iota((2, slot_count), 1) < live_count
    for kind in range(2):
        weight = jnp.where(live, duals_ref[kind] / slacks_ref[kind], 0.0)
        branch_scr[2 * kind : 2 * kind + 2, :slot_count] = weight
    branch_scr[4:5, :slot_count] = g_ref[...][None]
    branch_scr[5:6, :slot_count] = b_ref[...][None]
    branch_scr[6:7, :slot_count] = from_ref[...][None].astype(jnp.float32)
    branch_scr[7:8, :slot_count] = to_ref[...][None].astype(jnp.float32)
    bus_scr[20:21, :gen_count] = gen_curv_ref[...][None]
    index_scr[0:1, :slot_count] = from_ref[...][None]
    index_scr[1:2, :slot_count] = to_ref[...][None]
    index_scr[2:3, :bus_count] = bound_ref[...][None]
    index_scr[3:4, :gen_count] = gen_bus_ref[...][None]

    def tiles(ref, first, chunks):
        return [ref[first : first + ROWS, LANES * c : LANES * (c + 1)] for c in range(chunks)]

    def row(ref, number, chunk):
        return ref[number : number + 1, LANES * chunk : LANES * (chunk + 1)]

    lane = iota((ROWS, LANES), 1)
    sub = iota((ROWS, LANES), 0)
    lane_row = iota((1, LANES), 1)
    sub_col = iota((LANES, LANES), 0).astype(jnp.float32)
    inside = lane < ghost_count

    raw_bound = [tall(row(index_scr, 2, c)) for c in range(2)]
    bound = [jnp.where(inside, take_chunks(raw_bound, lane + h * ghost_count), -1) for h in range(2)]
    fetch = [jnp.maximum(b, 0) for b in bound]
    bound_row = [b[0:1].astype(jnp.float32) for b in bound]
    vm_raw, va_raw, grad_raw = (tiles(bus_scr, 8 * f, 2) for f in range(3))
    vm = [jnp.where(inside, take_chunks(vm_raw, f), 1.0) for f in fetch]
    va = [jnp.where(inside, take_chunks(va_raw, f), 0.0) for f in fetch]
    grad = [jnp.where(inside, take_chunks(grad_raw, f), 0.0) for f in fetch]
    cosv = [jnp.cos(a) for a in va]
    sinv = [jnp.sin(a) for a in va]

    earlier = (iota((LANES, LANES), 0) < iota((LANES, LANES), 1)).astype(jnp.bfloat16)
    local, cross_key, place = [], [], []
    local_count = jnp.zeros((1, 1), jnp.float32)
    for c in range(3):
        slot = lane_row + LANES * c
        alive = (slot < live_count) & (slot < slot_count)
        to_raw = row(index_scr, 1, c)
        cross_key.append(jnp.where(alive, to_raw, 9999).astype(jnp.float32))
        keep = jnp.where(alive & (to_raw < bus_count), 1.0, 0.0)
        before = jnp.dot(
            tall(keep).astype(jnp.bfloat16), earlier, preferred_element_type=jnp.float32
        )
        place.append(jnp.where(keep > 0.0, before[0:1] + local_count, -1.0))
        local_count = local_count + jnp.sum(keep, axis=1, keepdims=True)
    place_col = [column(p) for p in place]
    lane_f = lane_row.astype(jnp.float32)
    branch_tiles = tiles(branch_scr, 0, 3)

    def lowest(masks):
        found = functools.reduce(
            jnp.minimum,
            [jnp.where(m, sub_col + float(LANES * c), float(none)) for c, m in masks],
        )
        return jnp.min(found, axis=0, keepdims=True)

    packed, from_key, to_key = [], [], []
    for c in range(3):
        source = lowest([(d, place_col[d] == lane_f + float(LANES * c)) for d in range(c, 3)])
        tile = take_chunks(branch_tiles, tall(source).astype(jnp.int32))
        packed.append(tile)
        empty = source == float(none)
        from_key.append(jnp.where(empty, 9998.0, tile[6:7]))
        to_key.append(jnp.where(empty, 9999.0, tile[7:8]))
    from_col = [column(k) for k in from_key]
    to_col = [column(k) for k in to_key]
    cross_col = [column(k) for k in cross_key[:2]]
    bound_col = [column(b) for b in bound_row]
    gen_col = column(row(index_scr, 3, 0).astype(jnp.float32))
    curv_col = column(row(bus_scr, 20, 0))

    def links(keys, cols):
        heads, counts, matches = [], [], []
        for h in range(2):
            equal = [cols[c] == bound_row[h] for c in range(3)]
            matches.append([jnp.where(e, 1.0, 0.0).astype(jnp.bfloat16) for e in equal])
            heads.append(lowest(list(enumerate(equal))))
            counts.append(
                jnp.sum(
                    functools.reduce(jnp.add, [jnp.where(e, 1.0, 0.0) for e in equal]),
                    axis=0,
                    keepdims=True,
                )
            )
        nexts = []
        for c in range(3):
            later = [(c, (cols[c] == keys[c]) & (sub_col > lane_f))]
            later += [(d, cols[d] == keys[c]) for d in range(c + 1, 3)]
            nexts.append(lowest(later))
        return heads, nexts, jnp.maximum(counts[0], counts[1]), matches

    head_f, next_f, count_f, match_f = links(from_key, from_col)
    head_t, next_t, count_t, match_t = links(to_key, to_col)
    degree = jnp.max(jnp.maximum(count_f, count_t))

    def position(keys):
        found = [
            jnp.where(bound_col[h] == keys, sub_col + float(LANES * h), 0.0) for h in range(2)
        ]
        return jnp.max(jnp.maximum(found[0], found[1]), axis=0, keepdims=True)

    pos_f = [position(k) for k in from_key]
    pos_t = [position(k) for k in to_key]
    for m in range(2):
        pos_ref[m : m + 1, :] = position((lane_row + LANES * m).astype(jnp.float32)).astype(jnp.int32)

    cross = []
    for h in range(2):
        target = jnp.where(lane_row < ghost_count, bus_count + h * ghost_count + lane_row, -5)
        slot = lowest([(c, cross_col[c] == target.astype(jnp.float32)) for c in range(2)])
        cross.append(take_chunks(branch_tiles, tall(slot).astype(jnp.int32)))

    gens = [
        jnp.sum(jnp.where(gen_col == bound_row[h], curv_col, 0.0), axis=0, keepdims=True)
        for h in range(2)
    ]

    pair = sub & 3

    def every_pair(x):
        x = jnp.where(sub < 2, x, pltpu.roll(x, 2, 0))
        return jnp.where(sub < 4, x, pltpu.roll(x, 4, 0))

    from_table, to_table = [], []
    for c in range(3):
        at_f = tall(pos_f[c]).astype(jnp.int32)
        at_t = tall(pos_t[c]).astype(jnp.int32)
        h00, h01, h11, h22, h12, h02 = block_entries(
            *(take_chunks(t, at_f) for t in (vm, cosv, sinv)),
            *(take_chunks(t, at_t) for t in (vm, cosv, sinv)),
            tall(packed[c][4:5]),
            tall(packed[c][5:6]),
            every_pair(packed[c]),
            every_pair(pltpu.roll(packed[c], 6, 0)),
        )
        main = jnp.where(pair < 2, h02, -h11)
        off = jnp.where(pair < 2, -h01, h12)
        first = ROWS * (TILE_LOCAL + c)
        out_ref[first : first + ROWS, :] = jnp.where(sub < 4, main, off)
        from_table.append(jnp.where(sub < 2, h00, jnp.where(sub < 4, h01, h11)))
        to_table.append(jnp.where(sub < 2, h22, jnp.where(sub < 4, -h12, h11)))

    def parts(x):
        high = x.astype(jnp.bfloat16).astype(jnp.float32)
        middle = (x - high).astype(jnp.bfloat16).astype(jnp.float32)
        rest = x - high - middle
        return jnp.concatenate([high, middle, rest, jnp.zeros_like(x)], axis=0).astype(jnp.bfloat16)

    terms = [parts(t) for t in from_table + to_table]
    acc = []
    for h in range(2):
        total = functools.reduce(
            jnp.add,
            [
                jnp.dot(term, match, preferred_element_type=jnp.float32)
                for term, match in zip(terms, match_f[h] + match_t[h])
            ],
        )
        acc.append(total[0:8] + total[8:16] + total[16:24])

    total_local = jnp.max(local_count)

    for h in range(2):
        below = vm[h] - volt_low
        above = volt_high - vm[h]
        barrier = barrier_weight / (below * below) + barrier_weight / (above * above)
        diag_vv = pltpu.roll(acc[h], 4, 0) + barrier + gens[h]
        diag_aa = pltpu.roll(acc[h], 2, 0) + angle_reg + gens[h]
        diag_va = pltpu.roll(acc[h], 6, 0)
        first = ROWS * (TILE_A + h)
        out_ref[first : first + ROWS, :] = jnp.where(
            sub < 4, grad[h], jnp.where(sub < 6, diag_vv, diag_aa)
        )
        first = ROWS * (TILE_B + h)
        out_ref[first : first + ROWS, :] = jnp.where(
            sub < 2, diag_va, jnp.where(sub < 4, vm[h], jnp.where(sub < 6, cosv[h], sinv[h]))
        )
        first = ROWS * (TILE_C + h)
        out_ref[first : first + ROWS, :] = jnp.where(
            sub < 6, cross[h], jnp.where(sub == 6, degree, total_local)
        )
    first = ROWS * TILE_INDEX
    for offset, value in enumerate(pos_f + pos_t + head_f + head_t + next_f + next_t):
        out_ref[first + offset : first + offset + 1, :] = value


def solve_kernel(me_ref, pos_ref, *refs):
    *all_refs, step_ref, residual_ref, chain_scr, row_scr, field_scr, step_scr, residual_scr = refs
    blocks = len(all_refs)
    me = me_ref[0]
    half = blocks // 2
    bus_count = step_ref.shape[2]
    lane_pairs = [(j, h) for j in range(half) for h in range(2)]
    sub = iota((ROWS, LANES), 0)
    low = sub < 4
    even = (sub & 3) < 2

    def swap_component(x):
        return jnp.where(even, pltpu.roll(x, 6, 0), pltpu.roll(x, 2, 0))

    def swap_block(x):
        return pltpu.roll(x, 4, 0)

    upper = me >= half
    mine = jnp.where(upper, blocks - 1 - me, me)
    near = low != upper

    def halves(tile, j):
        here = all_refs[j][ROWS * tile : ROWS * (tile + 1), :]
        there = all_refs[blocks - 1 - j][ROWS * tile : ROWS * (tile + 1), :]
        first = jnp.where(upper, there, here)
        second = jnp.where(upper, here, there)
        return (
            jnp.where(low, first, swap_block(second)),
            jnp.where(low, swap_block(first), second),
        )

    def quarters(x):
        return (
            jnp.where(even, x, pltpu.roll(x, 2, 0)),
            jnp.where(even, pltpu.roll(x, 6, 0), x),
        )

    def single(number, j):
        return jnp.where(
            near,
            tall(all_refs[j][number : number + 1, :]),
            tall(all_refs[blocks - 1 - j][number : number + 1, :]),
        )

    def across(field):
        out = {}
        for j in range(half):
            inner = [
                field[j + 1, 1 - h] if j + 1 < half else swap_block(field[j, 1 - h])
                for h in range(2)
            ]
            outer = [field[j - 1, 1 - h] if j > 0 else 0.0 for h in range(2)]
            out[j, 0] = jnp.where(low, outer[0], inner[0])
            out[j, 1] = jnp.where(low, inner[1], outer[1])
        return out

    base = ROWS * TILE_INDEX
    names = [(name, h) for name in CHUNK_FIELDS for h in range(2)]
    names += [(name, c) for name in SLOT_FIELDS for c in range(3)]
    place = {name: number for number, name in enumerate(names)}
    for j in range(half):
        found = {}
        for h in range(2):
            found["gradient", h], found["diag", h] = halves(TILE_A + h, j)
            first, second = halves(TILE_B + h, j)
            found["diag_off", h], found["vm", h] = quarters(first)
            found["cosv", h], found["sinv", h] = quarters(second)
            first, _ = halves(TILE_C + h, j)
            found["wp", h], found["wq", h] = quarters(first)
            found["g", h] = single(ROWS * (TILE_C + h) + 4, j)
            found["b", h] = single(ROWS * (TILE_C + h) + 5, j)
            found["extent", h] = single(ROWS * TILE_C + 6 + h, j)
        for c in range(3):
            found["local_main", c], found["local_off", c] = halves(TILE_LOCAL + c, j)
            found["at_from", c] = single(base + c, j)
            found["at_to", c] = single(base + 3 + c, j)
        for name, number in place.items():
            field_scr[number, j ^ mine] = found[name]

    def load(name, chunks):
        return {
            (j, c): field_scr[place[name, c], j] for j in range(half) for c in range(chunks)
        }

    def load_index(name, chunks):
        return {key: value.astype(jnp.int32) for key, value in load(name, chunks).items()}

    gradient, diag, diag_off, vm, cosv, sinv, wp, wq, g, b, extent = (
        load(name, 2) for name in CHUNK_FIELDS
    )
    vm_to, cos_to, sin_to = across(vm), across(cosv), across(sinv)
    to_diag, to_off, main, off = {}, {}, {}, {}
    for key in lane_pairs:
        h00, h01, h11, h22, h12, h02 = block_entries(
            vm[key],
            cosv[key],
            sinv[key],
            vm_to[key],
            cos_to[key],
            sin_to[key],
            g[key],
            b[key],
            wp[key],
            wq[key],
        )
        diag[key] = diag[key] + jnp.where(even, h00, h11)
        diag_off[key] = diag_off[key] + h01
        to_diag[key] = jnp.where(even, h22, h11)
        to_off[key] = -h12
        main[key] = jnp.where(even, h02, -h11)
        off[key] = jnp.where(even, -h01, h12)
    to_diag, to_off = across(to_diag), across(to_off)
    main_to = across(main)
    off_to = across({key: swap_component(off[key]) for key in lane_pairs})
    inverse, inverse_off = {}, {}
    for key in lane_pairs:
        diag[key] = diag[key] + to_diag[key]
        diag_off[key] = diag_off[key] + to_off[key]
        main[key] = main[key] + main_to[key]
        off[key] = off[key] + off_to[key]
        flipped = swap_component(diag[key])
        determinant = diag[key] * flipped - diag_off[key] * diag_off[key]
        inverse[key] = flipped / determinant
        inverse_off[key] = -diag_off[key] / determinant

    local_main, local_off = (load(name, 3) for name in SLOT_FIELDS[:2])
    at_from, at_to = (load_index(name, 3) for name in SLOT_FIELDS[2:])

    def largest(h, pairs):
        return jnp.max(functools.reduce(jnp.maximum, [extent[j, h] for j in pairs]))

    outer_rank = largest(0, [0]).astype(jnp.int32)
    inner_rank = largest(0, range(1, half)).astype(jnp.int32)
    few = (largest(1, [0]) <= 2.0 * LANES) & (largest(1, range(1, half)) <= 1.0 * LANES)

    for number in range(10):
        for s, ref in enumerate(all_refs):
            row_scr[number, s : s + 1, :] = ref[base + 6 + number : base + 7 + number, :]
    links = [row_scr[number].astype(jnp.int32) for number in range(10)]
    heads, next_f, next_t = links[:4], links[4:7], links[7:]

    def follow(rank, ends):
        for kind in range(4):
            row_scr[kind] = ends[kind].astype(jnp.float32)
            for j in range(half):
                here = tall(row_scr[kind, j : j + 1, :])
                there = tall(row_scr[kind, blocks - 1 - j : blocks - j, :])
                chain_scr[rank, kind, j ^ mine] = jnp.where(near, here, there).astype(jnp.int32)
        return tuple(
            take_chunks(next_f if kind < 2 else next_t, ends[kind]) for kind in range(4)
        )

    ends = tuple(heads)
    for rank in range(SET_RANKS_OUTER):
        ends = follow(rank, ends)
    lax.fori_loop(SET_RANKS_OUTER, jnp.maximum(outer_rank, inner_rank), follow, ends)

    def local_sums(v, sums, outer_chunks, inner_chunks):
        chunks = [outer_chunks] + [inner_chunks] * (half - 1)
        to_from, to_to = {}, {}
        for j in range(half):
            table = [v[j, 0], v[j, 1]]
            for c in range(chunks[j]):
                far = take_chunks(table, at_to[j, c])
                near = take_chunks(table, at_from[j, c])
                to_from[j, c] = local_main[j, c] * far + local_off[j, c] * swap_component(far)
                to_to[j, c] = local_main[j, c] * near + swap_component(local_off[j, c] * near)

        def add_rank(pairs, rank, sums):
            sums = list(sums)
            for number, (j, h) in enumerate(lane_pairs):
                if j in pairs:
                    for offset, terms in ((0, to_from), (2, to_to)):
                        sums[number] += take_listed(
                            [terms[j, c] for c in range(chunks[j])], chain_scr[rank, offset + h, j]
                        )
            return tuple(sums)

        for rank in range(SET_RANKS_OUTER):
            sums = add_rank(range(half if rank < SET_RANKS else 1), rank, sums)
        inner = functools.partial(add_rank, range(1, half))
        sums = lax.fori_loop(SET_RANKS, inner_rank, inner, sums)
        return lax.fori_loop(SET_RANKS_OUTER, outer_rank, functools.partial(add_rank, [0]), sums)

    def operator(v):
        flipped = {key: swap_component(v[key]) for key in lane_pairs}
        v_to, flipped_to = across(v), across(flipped)
        out = tuple(
            diag[key] * v[key]
            + diag_off[key] * flipped[key]
            + main[key] * v_to[key]
            + off[key] * flipped_to[key]
            for key in lane_pairs
        )
        sums = lax.cond(
            few, lambda: local_sums(v, out, 2, 1), lambda: local_sums(v, out, 3, 3)
        )
        return dict(zip(lane_pairs, sums))

    def scenario_total(left, right):
        total = functools.reduce(jnp.add, [left[key] * right[key] for key in lane_pairs])
        total = total + pltpu.roll(total, 2, 0)
        total = total + pltpu.roll(total, 4, 0)
        return jnp.broadcast_to(jnp.sum(total, axis=1, keepdims=True), (ROWS, LANES))

    def precondition(v):
        return {
            key: inverse[key] * v[key] + inverse_off[key] * swap_component(v[key])
            for key in lane_pairs
        }

    residual = gradient
    search = precondition(residual)
    energy = scenario_total(residual, search)
    update = None
    for iteration in range(ITERS):
        image = operator(search)
        step_size = energy / scenario_total(search, image)
        if update is None:
            update = {key: step_size * search[key] for key in lane_pairs}
        else:
            update = {key: update[key] + step_size * search[key] for key in lane_pairs}
        residual = {key: residual[key] - step_size * image[key] for key in lane_pairs}
        if iteration + 1 < ITERS:
            scaled = precondition(residual)
            energy_next = scenario_total(residual, scaled)
            ratio = energy_next / energy
            search = {key: scaled[key] + ratio * search[key] for key in lane_pairs}
            energy = energy_next

    for field, keep_scr, out_ref in (
        (update, step_scr, step_ref),
        (residual, residual_scr, residual_ref),
    ):
        for j, h in lane_pairs:
            keep_scr[j, h] = field[j, h]
        own = []
        for h in range(2):
            tile = keep_scr[mine, h]
            own.append(jnp.where(upper, swap_block(tile), tile))
        for m in range(2):
            width = min(LANES, bus_count - LANES * m)
            values = take_chunks(own, tall(pos_ref[m : m + 1, :]))
            for comp in range(2):
                out_ref[comp, :, LANES * m : LANES * m + width] = values[
                    2 * comp : 2 * comp + 2, :width
                ]


def fast_body(
    volt_mag,
    volt_ang,
    gradient,
    branch_from,
    branch_to,
    branch_count,
    boundary,
    conductance,
    susceptance,
    duals,
    slacks,
    gen_bus,
    gen_curvature,
):
    bus_count = volt_mag.shape[0]
    slot_count = branch_from.shape[0]
    blocks = lax.axis_size("net")
    vmem = pl.BlockSpec(memory_space=pltpu.VMEM)
    smem = pl.BlockSpec(memory_space=pltpu.SMEM)
    payload, position = pl.pallas_call(
        prepare_kernel,
        out_shape=(
            pltpu.VMEM((PAYLOAD_ROWS, LANES), jnp.float32),
            pltpu.VMEM((2, LANES), jnp.int32),
        ),
        in_specs=[vmem] * 13,
        out_specs=(vmem, vmem),
        scratch_shapes=[
            pltpu.VMEM((24, 2 * LANES), jnp.float32),
            pltpu.VMEM((8, 3 * LANES), jnp.float32),
            pltpu.VMEM((8, 3 * LANES), jnp.int32),
        ],
        name="prepare",
    )(
        volt_mag.T,
        volt_ang.T,
        jnp.transpose(gradient, (1, 2, 0)),
        branch_from,
        branch_to,
        branch_count,
        boundary,
        conductance,
        susceptance,
        jnp.transpose(duals, (0, 2, 1)),
        jnp.transpose(slacks, (0, 2, 1)),
        gen_bus,
        gen_curvature,
    )
    def passed(block, other):
        return lax.ppermute(block, "net", [(i, i ^ other) for i in range(blocks)])

    gathered = {0: payload}
    for other in range(2, blocks, 2):
        gathered[other] = passed(payload, other)
    for other in range(0, blocks, 2):
        gathered[other + 1] = passed(gathered[other], 1)
    gathered = [gathered[other] for other in range(blocks)]
    me = lax.axis_index("net").astype(jnp.int32)[None]
    tile_pairs = (blocks // 2, 2, ROWS, LANES)
    field = jax.ShapeDtypeStruct((2, 2, bus_count), jnp.float32)
    step, residual = pl.pallas_call(
        solve_kernel,
        out_shape=(field, field),
        in_specs=[smem] + [vmem] * (1 + blocks),
        out_specs=(vmem, vmem),
        scratch_shapes=[
            pltpu.VMEM((slot_count, 4, blocks // 2, ROWS, LANES), jnp.int32),
            pltpu.VMEM((10, blocks, LANES), jnp.float32),
            pltpu.VMEM(
                (2 * len(CHUNK_FIELDS) + 3 * len(SLOT_FIELDS), blocks // 2, ROWS, LANES),
                jnp.float32,
            ),
            pltpu.VMEM(tile_pairs, jnp.float32),
            pltpu.VMEM(tile_pairs, jnp.float32),
        ],
        compiler_params=pltpu.CompilerParams(vmem_limit_bytes=40 * 2**20),
        name="solve",
    )(me, position, *gathered)
    return jnp.transpose(step, (2, 0, 1)), jnp.transpose(residual, (2, 0, 1))


def any_body(*arrays):
    volt_mag, boundary, branch_from, gen_bus = arrays[0], arrays[6], arrays[3], arrays[11]
    fast = fits_fast_path(
        lax.axis_size("net"),
        volt_mag.shape[0],
        boundary.shape[0] // 2,
        branch_from.shape[0],
        gen_bus.shape[0],
        volt_mag.shape[1],
    )
    return fast_body(*arrays) if fast else body(*arrays)


def solution(mesh):
    placed = (
        P("net", "scen"),
        P("net", "scen"),
        P("net", None, "scen"),
        P("net"),
        P("net"),
        P("net"),
        P("net"),
        P("net"),
        P("net"),
        P(None, "net", "scen"),
        P(None, "net", "scen"),
        P("net"),
        P("net"),
    )
    return jax.shard_map(
        any_body,
        mesh=mesh,
        in_specs=placed,
        out_specs=(P("net", None, "scen"), P("net", None, "scen")),
        check_vma=False,
    )
```

```python
import functools

import jax
import jax.numpy as jnp
from jax import lax
from jax.experimental import pallas as pl
from jax.experimental.pallas import tpu as pltpu
from jax.sharding import PartitionSpec as P

ITERS = 4


barrier_weight = 0.01
volt_low = 0.9
volt_high = 1.1
angle_reg = 0.5


def shifted(array, axis, by):
    peers = lax.axis_size(axis)
    pairs = [(i, i + by) for i in range(peers) if 0 <= i + by < peers]
    return lax.ppermute(array, axis, pairs)


def branch_blocks(
    magnitude_from,
    angle_from,
    magnitude_to,
    angle_to,
    conduct,
    suscept,
    weight_active,
    weight_reactive,
):
    angle_diff = angle_from - angle_to
    cosine_diff = jnp.cos(angle_diff)
    sine_diff = jnp.sin(angle_diff)
    flow_along = conduct * cosine_diff + suscept * sine_diff
    flow_across = conduct * sine_diff - suscept * cosine_diff
    cross_term = magnitude_from * magnitude_to
    active_rows = (
        2.0 * conduct * magnitude_from - magnitude_to * flow_along,
        cross_term * flow_across,
        -magnitude_from * flow_along,
        -cross_term * flow_across,
    )
    reactive_rows = (
        -2.0 * suscept * magnitude_from - magnitude_to * flow_across,
        -cross_term * flow_along,
        -magnitude_from * flow_across,
        cross_term * flow_along,
    )

    def block_entry(left_index, right_index):
        return (
            weight_active * active_rows[left_index] * active_rows[right_index]
            + weight_reactive * reactive_rows[left_index] * reactive_rows[right_index]
        )

    from_block = jnp.stack([block_entry(0, 0), block_entry(0, 1), block_entry(1, 1)], axis=1)
    to_block = jnp.stack([block_entry(2, 2), block_entry(2, 3), block_entry(3, 3)], axis=1)
    cross_block = jnp.stack(
        [block_entry(0, 2), block_entry(0, 3), block_entry(1, 2), block_entry(1, 3)], axis=1
    )
    return (from_block, to_block, cross_block)


def apply_cross(matrix_block, vector):
    return jnp.stack(
        [
            matrix_block[:, 0] * vector[:, 0] + matrix_block[:, 1] * vector[:, 1],
            matrix_block[:, 2] * vector[:, 0] + matrix_block[:, 3] * vector[:, 1],
        ],
        axis=1,
    )


def apply_cross_transposed(matrix_block, vector):
    return jnp.stack(
        [
            matrix_block[:, 0] * vector[:, 0] + matrix_block[:, 2] * vector[:, 1],
            matrix_block[:, 1] * vector[:, 0] + matrix_block[:, 3] * vector[:, 1],
        ],
        axis=1,
    )


def scenario_sum(left_vec, right_vec):
    return jnp.sum(left_vec * right_vec, axis=(0, 1))


def widen(values):
    return values[None, None, :]


def body(
    volt_mag,
    volt_ang,
    gradient,
    branch_from,
    branch_to,
    branch_count,
    boundary,
    conductance,
    susceptance,
    duals,
    slacks,
    gen_bus,
    gen_curvature,
):
    bus_count = volt_mag.shape[0]
    ghost_count = boundary.shape[0] // 2
    extended_size = bus_count + 2 * ghost_count
    slot_count = branch_from.shape[0]
    left_list = boundary[:ghost_count]
    right_list = boundary[ghost_count:]
    left_ghost = slice(bus_count, bus_count + ghost_count)
    right_ghost = slice(bus_count + ghost_count, extended_size)
    return_plan = (
        (-1, left_ghost, right_list, right_ghost),
        (1, right_ghost, left_list, left_ghost),
    )

    def share_vector(values):
        pieces = [values]
        for direction in (1, -1):
            outgoing = jnp.take(values, right_list if direction == 1 else left_list, axis=0)
            pieces.append(shifted(outgoing, "net", direction))
        return jnp.concatenate(pieces, axis=0)

    bus_state = jnp.stack([volt_mag, volt_ang], axis=1)
    pieces = [bus_state]
    for share_direction in (1, -1):
        outgoing = jnp.take(bus_state, right_list if share_direction == 1 else left_list, axis=0)
        pieces.append(shifted(outgoing, "net", share_direction))
    extended_state = jnp.concatenate(pieces, axis=0)
    from_state = jnp.take(extended_state, branch_from, axis=0)
    to_state = jnp.take(extended_state, branch_to, axis=0)
    live_mask = (jnp.arange(slot_count) < branch_count[0]).astype(jnp.float32)[:, None]
    weight_active = live_mask * duals[0] / slacks[0]
    weight_reactive = live_mask * duals[1] / slacks[1]
    from_block, to_block, cross_block = branch_blocks(
        from_state[:, 0],
        from_state[:, 1],
        to_state[:, 0],
        to_state[:, 1],
        conductance[:, None],
        susceptance[:, None],
        weight_active,
        weight_reactive,
    )
    diag_extended = jax.ops.segment_sum(
        from_block, branch_from, num_segments=extended_size
    ) + jax.ops.segment_sum(to_block, branch_to, num_segments=extended_size)
    diag_local = diag_extended[:bus_count]
    for direction, ghost_rows, target_rows, source_rows in return_plan:
        arrived_diag = shifted(diag_extended[ghost_rows], "net", direction)
        diag_local = diag_local.at[target_rows].add(arrived_diag)
    gen_table = (gen_bus[None, :] == jnp.arange(bus_count)[:, None]).astype(jnp.float32)
    gen_sum = jnp.dot(gen_table, gen_curvature, precision=lax.Precision.HIGHEST)[:, None]
    barrier = barrier_weight / jnp.square(volt_mag - volt_low) + barrier_weight / jnp.square(
        volt_high - volt_mag
    )
    diag_vv = diag_local[:, 0] + barrier + gen_sum
    diag_va = diag_local[:, 1]
    diag_aa = diag_local[:, 2] + angle_reg + gen_sum
    determinant = diag_vv * diag_aa - diag_va * diag_va
    inverse_vv = diag_aa / determinant
    inverse_va = -diag_va / determinant
    inverse_aa = diag_vv / determinant

    def precondition(vector):
        return jnp.stack(
            [
                inverse_vv * vector[:, 0] + inverse_va * vector[:, 1],
                inverse_va * vector[:, 0] + inverse_aa * vector[:, 1],
            ],
            axis=1,
        )

    update_field = jnp.zeros_like(gradient)
    residual = gradient

    def energy_of(residual_now, scaled_now):
        return lax.psum(scenario_sum(residual_now, scaled_now), "net")

    scaled = precondition(residual)
    search = scaled
    energy = energy_of(residual, scaled)
    for iteration in range(ITERS):
        extended = share_vector(search)
        from_values = jnp.take(extended, branch_from, axis=0)
        to_values = jnp.take(extended, branch_to, axis=0)
        from_terms = apply_cross(cross_block, to_values)
        to_terms = apply_cross_transposed(cross_block, from_values)
        result = jnp.stack(
            [
                diag_vv * search[:, 0] + diag_va * search[:, 1],
                diag_va * search[:, 0] + diag_aa * search[:, 1],
            ],
            axis=1,
        )
        summed = jax.ops.segment_sum(
            from_terms, branch_from, num_segments=extended_size
        ) + jax.ops.segment_sum(to_terms, branch_to, num_segments=extended_size)
        local_sum = result + summed[:bus_count]
        for apply_direction, apply_ghost_rows, apply_target_rows, apply_source_rows in return_plan:
            arrived = shifted(summed[apply_ghost_rows], "net", apply_direction)
            local_sum = local_sum.at[apply_target_rows].add(arrived)
        step_size = energy / lax.psum(scenario_sum(search, local_sum), "net")
        update_field = update_field + widen(step_size) * search
        residual = residual - widen(step_size) * local_sum
        if iteration + 1 < ITERS:
            scaled = precondition(residual)
            energy_next = energy_of(residual, scaled)
            search = scaled + widen(energy_next / energy) * search
            energy = energy_next
    return (update_field, residual)


LANES = 128
ROWS = 8
TILE_A, TILE_B, TILE_C = 0, 2, 4
TILE_LOCAL = 6
TILE_INDEX = 9
PAYLOAD_ROWS = 11 * ROWS
CHUNK_FIELDS = ["gradient", "diag", "diag_off", "vm", "cosv", "sinv"]
CHUNK_FIELDS += ["wp", "wq", "g", "b", "extent"]
SLOT_FIELDS = ["local_main", "local_off", "at_from", "at_to"]
SET_RANKS = 4
SET_RANKS_OUTER = 4


def fits_fast_path(blocks, bus_count, ghost_count, slot_count, gen_count, scen_count):
    return (
        blocks == 8
        and scen_count == 2
        and bus_count == 2 * ghost_count
        and ghost_count <= LANES
        and 2 * LANES < slot_count < 3 * LANES
        and gen_count <= LANES
    )


def iota(shape, dim):
    return lax.broadcasted_iota(jnp.int32, shape, dim)


def lane_take(table, index):
    return jnp.take_along_axis(table, index, axis=1, mode="promise_in_bounds")


def take_chunks(tables, index):
    lane = index & (LANES - 1)
    chunk = index >> 7
    out = lane_take(tables[0], lane)
    for number in range(1, len(tables)):
        out = jnp.where(chunk == number, lane_take(tables[number], lane), out)
    return out


def take_listed(tables, index, default=0):
    lane = index & (LANES - 1)
    chunk = index >> 7
    out = jnp.full(index.shape, default, tables[0].dtype)
    for number, table in enumerate(tables):
        out = jnp.where(chunk == number, lane_take(table, lane), out)
    return out


def tall(row):
    return jnp.broadcast_to(row, (ROWS, LANES))


def column(row):
    return jnp.transpose(jnp.broadcast_to(row, (LANES, LANES)))


def block_entries(vi, ci, si, vj, cj, sj, g, b, wp, wq):
    cosine = ci * cj + si * sj
    sine = si * cj - ci * sj
    along = g * cosine + b * sine
    across = g * sine - b * cosine
    cross = vi * vj
    p0 = 2.0 * g * vi - vj * along
    p1 = cross * across
    p2 = -vi * along
    q0 = -2.0 * b * vi - vj * across
    q1 = -cross * along
    q2 = -vi * across

    def entry(pa, pb, qa, qb):
        return wp * pa * pb + wq * qa * qb

    return (
        entry(p0, p0, q0, q0),
        entry(p0, p1, q0, q1),
        entry(p1, p1, q1, q1),
        entry(p2, p2, q2, q2),
        entry(p1, p2, q1, q2),
        entry(p0, p2, q0, q2),
    )


def prepare_kernel(
    vm_ref,
    va_ref,
    grad_ref,
    from_ref,
    to_ref,
    count_ref,
    bound_ref,
    g_ref,
    b_ref,
    duals_ref,
    slacks_ref,
    gen_bus_ref,
    gen_curv_ref,
    out_ref,
    pos_ref,
    bus_scr,
    branch_scr,
    index_scr,
):
    bus_count = vm_ref.shape[1]
    ghost_count = bus_count // 2
    slot_count = from_ref.shape[0]
    gen_count = gen_bus_ref.shape[0]
    none = 3 * LANES - 1
    live_count = count_ref[...][None]

    bus_scr[...] = jnp.zeros_like(bus_scr)
    branch_scr[...] = jnp.zeros_like(branch_scr)
    index_scr[...] = jnp.full_like(index_scr, -9)
    for copy in range(4):
        bus_scr[2 * copy : 2 * copy + 2, :bus_count] = vm_ref[...]
        bus_scr[8 + 2 * copy : 10 + 2 * copy, :bus_count] = va_ref[...]
    for comp in range(2):
        bus_scr[16 + 2 * comp : 18 + 2 * comp, :bus_count] = grad_ref[comp]
    live = iota((2, slot_count), 1) < live_count
    for kind in range(2):
        weight = jnp.where(live, duals_ref[kind] / slacks_ref[kind], 0.0)
        branch_scr[2 * kind : 2 * kind + 2, :slot_count] = weight
    branch_scr[4:5, :slot_count] = g_ref[...][None]
    branch_scr[5:6, :slot_count] = b_ref[...][None]
    branch_scr[6:7, :slot_count] = from_ref[...][None].astype(jnp.float32)
    branch_scr[7:8, :slot_count] = to_ref[...][None].astype(jnp.float32)
    bus_scr[20:21, :gen_count] = gen_curv_ref[...][None]
    index_scr[0:1, :slot_count] = from_ref[...][None]
    index_scr[1:2, :slot_count] = to_ref[...][None]
    index_scr[2:3, :bus_count] = bound_ref[...][None]
    index_scr[3:4, :gen_count] = gen_bus_ref[...][None]

    def tiles(ref, first, chunks):
        return [ref[first : first + ROWS, LANES * c : LANES * (c + 1)] for c in range(chunks)]

    def row(ref, number, chunk):
        return ref[number : number + 1, LANES * chunk : LANES * (chunk + 1)]

    lane = iota((ROWS, LANES), 1)
    sub = iota((ROWS, LANES), 0)
    lane_row = iota((1, LANES), 1)
    sub_col = iota((LANES, LANES), 0).astype(jnp.float32)
    inside = lane < ghost_count

    raw_bound = [tall(row(index_scr, 2, c)) for c in range(2)]
    bound = [jnp.where(inside, take_chunks(raw_bound, lane + h * ghost_count), -1) for h in range(2)]
    fetch = [jnp.maximum(b, 0) for b in bound]
    bound_row = [b[0:1].astype(jnp.float32) for b in bound]
    vm_raw, va_raw, grad_raw = (tiles(bus_scr, 8 * f, 2) for f in range(3))
    vm = [jnp.where(inside, take_chunks(vm_raw, f), 1.0) for f in fetch]
    va = [jnp.where(inside, take_chunks(va_raw, f), 0.0) for f in fetch]
    grad = [jnp.where(inside, take_chunks(grad_raw, f), 0.0) for f in fetch]
    cosv = [jnp.cos(a) for a in va]
    sinv = [jnp.sin(a) for a in va]

    earlier = (iota((LANES, LANES), 0) < iota((LANES, LANES), 1)).astype(jnp.bfloat16)
    local, cross_key, place = [], [], []
    local_count = jnp.zeros((1, 1), jnp.float32)
    for c in range(3):
        slot = lane_row + LANES * c
        alive = (slot < live_count) & (slot < slot_count)
        to_raw = row(index_scr, 1, c)
        cross_key.append(jnp.where(alive, to_raw, 9999).astype(jnp.float32))
        keep = jnp.where(alive & (to_raw < bus_count), 1.0, 0.0)
        before = jnp.dot(
            tall(keep).astype(jnp.bfloat16), earlier, preferred_element_type=jnp.float32
        )
        place.append(jnp.where(keep > 0.0, before[0:1] + local_count, -1.0))
        local_count = local_count + jnp.sum(keep, axis=1, keepdims=True)
    place_col = [column(p) for p in place]
    lane_f = lane_row.astype(jnp.float32)
    branch_tiles = tiles(branch_scr, 0, 3)

    def lowest(masks):
        found = functools.reduce(
            jnp.minimum,
            [jnp.where(m, sub_col + float(LANES * c), float(none)) for c, m in masks],
        )
        return jnp.min(found, axis=0, keepdims=True)

    packed, from_key, to_key = [], [], []
    for c in range(3):
        source = lowest([(d, place_col[d] == lane_f + float(LANES * c)) for d in range(c, 3)])
        tile = take_chunks(branch_tiles, tall(source).astype(jnp.int32))
        packed.append(tile)
        empty = source == float(none)
        from_key.append(jnp.where(empty, 9998.0, tile[6:7]))
        to_key.append(jnp.where(empty, 9999.0, tile[7:8]))
    from_col = [column(k) for k in from_key]
    to_col = [column(k) for k in to_key]
    cross_col = [column(k) for k in cross_key[:2]]
    bound_col = [column(b) for b in bound_row]
    gen_col = column(row(index_scr, 3, 0).astype(jnp.float32))
    curv_col = column(row(bus_scr, 20, 0))

    def links(keys, cols):
        heads, counts, matches = [], [], []
        for h in range(2):
            equal = [cols[c] == bound_row[h] for c in range(3)]
            matches.append([jnp.where(e, 1.0, 0.0).astype(jnp.bfloat16) for e in equal])
            heads.append(lowest(list(enumerate(equal))))
            counts.append(
                jnp.sum(
                    functools.reduce(jnp.add, [jnp.where(e, 1.0, 0.0) for e in equal]),
                    axis=0,
                    keepdims=True,
                )
            )
        nexts = []
        for c in range(3):
            later = [(c, (cols[c] == keys[c]) & (sub_col > lane_f))]
            later += [(d, cols[d] == keys[c]) for d in range(c + 1, 3)]
            nexts.append(lowest(later))
        return heads, nexts, jnp.maximum(counts[0], counts[1]), matches

    head_f, next_f, count_f, match_f = links(from_key, from_col)
    head_t, next_t, count_t, match_t = links(to_key, to_col)
    degree = jnp.max(jnp.maximum(count_f, count_t))

    def position(keys):
        found = [
            jnp.where(bound_col[h] == keys, sub_col + float(LANES * h), 0.0) for h in range(2)
        ]
        return jnp.max(jnp.maximum(found[0], found[1]), axis=0, keepdims=True)

    pos_f = [position(k) for k in from_key]
    pos_t = [position(k) for k in to_key]
    for m in range(2):
        pos_ref[m : m + 1, :] = position((lane_row + LANES * m).astype(jnp.float32)).astype(jnp.int32)

    cross = []
    for h in range(2):
        target = jnp.where(lane_row < ghost_count, bus_count + h * ghost_count + lane_row, -5)
        slot = lowest([(c, cross_col[c] == target.astype(jnp.float32)) for c in range(2)])
        cross.append(take_chunks(branch_tiles, tall(slot).astype(jnp.int32)))

    gens = [
        jnp.sum(jnp.where(gen_col == bound_row[h], curv_col, 0.0), axis=0, keepdims=True)
        for h in range(2)
    ]

    pair = sub & 3

    def every_pair(x):
        x = jnp.where(sub < 2, x, pltpu.roll(x, 2, 0))
        return jnp.where(sub < 4, x, pltpu.roll(x, 4, 0))

    from_table, to_table = [], []
    for c in range(3):
        at_f = tall(pos_f[c]).astype(jnp.int32)
        at_t = tall(pos_t[c]).astype(jnp.int32)
        h00, h01, h11, h22, h12, h02 = block_entries(
            *(take_chunks(t, at_f) for t in (vm, cosv, sinv)),
            *(take_chunks(t, at_t) for t in (vm, cosv, sinv)),
            tall(packed[c][4:5]),
            tall(packed[c][5:6]),
            every_pair(packed[c]),
            every_pair(pltpu.roll(packed[c], 6, 0)),
        )
        main = jnp.where(pair < 2, h02, -h11)
        off = jnp.where(pair < 2, -h01, h12)
        first = ROWS * (TILE_LOCAL + c)
        out_ref[first : first + ROWS, :] = jnp.where(sub < 4, main, off)
        from_table.append(jnp.where(sub < 2, h00, jnp.where(sub < 4, h01, h11)))
        to_table.append(jnp.where(sub < 2, h22, jnp.where(sub < 4, -h12, h11)))

    def parts(x):
        high = x.astype(jnp.bfloat16).astype(jnp.float32)
        middle = (x - high).astype(jnp.bfloat16).astype(jnp.float32)
        rest = x - high - middle
        return jnp.concatenate([high, middle, rest, jnp.zeros_like(x)], axis=0).astype(jnp.bfloat16)

    terms = [parts(t) for t in from_table + to_table]
    acc = []
    for h in range(2):
        total = functools.reduce(
            jnp.add,
            [
                jnp.dot(term, match, preferred_element_type=jnp.float32)
                for term, match in zip(terms, match_f[h] + match_t[h])
            ],
        )
        acc.append(total[0:8] + total[8:16] + total[16:24])

    total_local = jnp.max(local_count)

    for h in range(2):
        below = vm[h] - volt_low
        above = volt_high - vm[h]
        barrier = barrier_weight / (below * below) + barrier_weight / (above * above)
        diag_vv = pltpu.roll(acc[h], 4, 0) + barrier + gens[h]
        diag_aa = pltpu.roll(acc[h], 2, 0) + angle_reg + gens[h]
        diag_va = pltpu.roll(acc[h], 6, 0)
        first = ROWS * (TILE_A + h)
        out_ref[first : first + ROWS, :] = jnp.where(
            sub < 4, grad[h], jnp.where(sub < 6, diag_vv, diag_aa)
        )
        first = ROWS * (TILE_B + h)
        out_ref[first : first + ROWS, :] = jnp.where(
            sub < 2, diag_va, jnp.where(sub < 4, vm[h], jnp.where(sub < 6, cosv[h], sinv[h]))
        )
        first = ROWS * (TILE_C + h)
        out_ref[first : first + ROWS, :] = jnp.where(
            sub < 6, cross[h], jnp.where(sub == 6, degree, total_local)
        )
    first = ROWS * TILE_INDEX
    for offset, value in enumerate(pos_f + pos_t + head_f + head_t + next_f + next_t):
        out_ref[first + offset : first + offset + 1, :] = value


def solve_kernel(me_ref, pos_ref, *refs):
    *all_refs, step_ref, residual_ref = refs[:-6]
    chain_scr, end_scr, row_scr, field_scr, step_scr, residual_scr = refs[-6:]
    blocks = len(all_refs)
    me = me_ref[0]
    half = blocks // 2
    bus_count = step_ref.shape[2]
    lane_pairs = [(j, h) for j in range(half) for h in range(2)]
    sub = iota((ROWS, LANES), 0)
    low = sub < 4
    even = (sub & 3) < 2

    def swap_component(x):
        return jnp.where(even, pltpu.roll(x, 6, 0), pltpu.roll(x, 2, 0))

    def swap_block(x):
        return pltpu.roll(x, 4, 0)

    upper = me >= half
    mine = jnp.where(upper, blocks - 1 - me, me)
    near = low != upper

    def halves(tile, j):
        here = all_refs[j][ROWS * tile : ROWS * (tile + 1), :]
        there = all_refs[blocks - 1 - j][ROWS * tile : ROWS * (tile + 1), :]
        first = jnp.where(upper, there, here)
        second = jnp.where(upper, here, there)
        return (
            jnp.where(low, first, swap_block(second)),
            jnp.where(low, swap_block(first), second),
        )

    def quarters(x):
        return (
            jnp.where(even, x, pltpu.roll(x, 2, 0)),
            jnp.where(even, pltpu.roll(x, 6, 0), x),
        )

    def single(number, j):
        return jnp.where(
            near,
            tall(all_refs[j][number : number + 1, :]),
            tall(all_refs[blocks - 1 - j][number : number + 1, :]),
        )

    def across(field):
        out = {}
        for j in range(half):
            inner = [
                field[j + 1, 1 - h] if j + 1 < half else swap_block(field[j, 1 - h])
                for h in range(2)
            ]
            outer = [field[j - 1, 1 - h] if j > 0 else 0.0 for h in range(2)]
            out[j, 0] = jnp.where(low, outer[0], inner[0])
            out[j, 1] = jnp.where(low, inner[1], outer[1])
        return out

    base = ROWS * TILE_INDEX
    names = [(name, h) for name in CHUNK_FIELDS for h in range(2)]
    names += [(name, c) for name in SLOT_FIELDS for c in range(3)]
    place = {name: number for number, name in enumerate(names)}
    for j in range(half):
        found = {}
        for h in range(2):
            found["gradient", h], found["diag", h] = halves(TILE_A + h, j)
            first, second = halves(TILE_B + h, j)
            found["diag_off", h], found["vm", h] = quarters(first)
            found["cosv", h], found["sinv", h] = quarters(second)
            first, _ = halves(TILE_C + h, j)
            found["wp", h], found["wq", h] = quarters(first)
            found["g", h] = single(ROWS * (TILE_C + h) + 4, j)
            found["b", h] = single(ROWS * (TILE_C + h) + 5, j)
            found["extent", h] = single(ROWS * TILE_C + 6 + h, j)
        for c in range(3):
            found["local_main", c], found["local_off", c] = halves(TILE_LOCAL + c, j)
            found["at_from", c] = single(base + c, j)
            found["at_to", c] = single(base + 3 + c, j)
        for name, number in place.items():
            field_scr[number, j ^ mine] = found[name]

    def load(name, chunks):
        return {
            (j, c): field_scr[place[name, c], j] for j in range(half) for c in range(chunks)
        }

    def load_index(name, chunks):
        return {key: value.astype(jnp.int32) for key, value in load(name, chunks).items()}

    gradient, diag, diag_off, vm, cosv, sinv, wp, wq, g, b, extent = (
        load(name, 2) for name in CHUNK_FIELDS
    )
    vm_to, cos_to, sin_to = across(vm), across(cosv), across(sinv)
    to_diag, to_off, main, off = {}, {}, {}, {}
    for key in lane_pairs:
        h00, h01, h11, h22, h12, h02 = block_entries(
            vm[key],
            cosv[key],
            sinv[key],
            vm_to[key],
            cos_to[key],
            sin_to[key],
            g[key],
            b[key],
            wp[key],
            wq[key],
        )
        diag[key] = diag[key] + jnp.where(even, h00, h11)
        diag_off[key] = diag_off[key] + h01
        to_diag[key] = jnp.where(even, h22, h11)
        to_off[key] = -h12
        main[key] = jnp.where(even, h02, -h11)
        off[key] = jnp.where(even, -h01, h12)
    to_diag, to_off = across(to_diag), across(to_off)
    main_to = across(main)
    off_to = across({key: swap_component(off[key]) for key in lane_pairs})
    inverse, inverse_off = {}, {}
    for key in lane_pairs:
        diag[key] = diag[key] + to_diag[key]
        diag_off[key] = diag_off[key] + to_off[key]
        main[key] = main[key] + main_to[key]
        off[key] = off[key] + off_to[key]
        flipped = swap_component(diag[key])
        determinant = diag[key] * flipped - diag_off[key] * diag_off[key]
        inverse[key] = flipped / determinant
        inverse_off[key] = -diag_off[key] / determinant

    local_main, local_off = (load(name, 3) for name in SLOT_FIELDS[:2])
    at_from, at_to = (load_index(name, 3) for name in SLOT_FIELDS[2:])

    def largest(h, pairs):
        return jnp.max(functools.reduce(jnp.maximum, [extent[j, h] for j in pairs]))

    outer_rank = largest(0, [0]).astype(jnp.int32)
    inner_rank = largest(0, range(1, half)).astype(jnp.int32)
    few = (largest(1, [0]) <= 2.0 * LANES) & (largest(1, range(1, half)) <= 1.0 * LANES)

    for number in range(10):
        for s, ref in enumerate(all_refs):
            row_scr[number, s : s + 1, :] = ref[base + 6 + number : base + 7 + number, :]
    links = [row_scr[number].astype(jnp.int32) for number in range(10)]
    heads, next_f, next_t = links[:4], links[4:7], links[7:]

    def follow(rank, ends):
        for kind in range(4):
            end_scr[rank, kind] = ends[kind]
            for j in range(half):
                here = tall(end_scr[rank, kind, j : j + 1, :])
                there = tall(end_scr[rank, kind, blocks - 1 - j : blocks - j, :])
                chain_scr[rank, kind, j ^ mine] = jnp.where(near, here, there)
        return tuple(
            take_chunks(next_f if kind < 2 else next_t, ends[kind]) for kind in range(4)
        )

    ends = tuple(heads)
    for rank in range(SET_RANKS_OUTER):
        ends = follow(rank, ends)
    lax.fori_loop(SET_RANKS_OUTER, jnp.maximum(outer_rank, inner_rank), follow, ends)

    def local_sums(v, sums, outer_chunks, inner_chunks):
        chunks = [outer_chunks] + [inner_chunks] * (half - 1)
        to_from, to_to = {}, {}
        for j in range(half):
            table = [v[j, 0], v[j, 1]]
            for c in range(chunks[j]):
                far = take_chunks(table, at_to[j, c])
                near = take_chunks(table, at_from[j, c])
                to_from[j, c] = local_main[j, c] * far + local_off[j, c] * swap_component(far)
                to_to[j, c] = local_main[j, c] * near + swap_component(local_off[j, c] * near)

        def add_rank(pairs, rank, sums):
            sums = list(sums)
            for number, (j, h) in enumerate(lane_pairs):
                if j in pairs:
                    for offset, terms in ((0, to_from), (2, to_to)):
                        sums[number] += take_listed(
                            [terms[j, c] for c in range(chunks[j])], chain_scr[rank, offset + h, j]
                        )
            return tuple(sums)

        for rank in range(SET_RANKS_OUTER):
            sums = add_rank(range(half if rank < SET_RANKS else 1), rank, sums)
        inner = functools.partial(add_rank, range(1, half))
        sums = lax.fori_loop(SET_RANKS, inner_rank, inner, sums)
        return lax.fori_loop(SET_RANKS_OUTER, outer_rank, functools.partial(add_rank, [0]), sums)

    def operator(v):
        flipped = {key: swap_component(v[key]) for key in lane_pairs}
        v_to, flipped_to = across(v), across(flipped)
        out = tuple(
            diag[key] * v[key]
            + diag_off[key] * flipped[key]
            + main[key] * v_to[key]
            + off[key] * flipped_to[key]
            for key in lane_pairs
        )
        sums = lax.cond(
            few, lambda: local_sums(v, out, 2, 1), lambda: local_sums(v, out, 3, 3)
        )
        return dict(zip(lane_pairs, sums))

    def scenario_total(left, right):
        total = functools.reduce(jnp.add, [left[key] * right[key] for key in lane_pairs])
        total = total + pltpu.roll(total, 2, 0)
        total = total + pltpu.roll(total, 4, 0)
        return jnp.broadcast_to(jnp.sum(total, axis=1, keepdims=True), (ROWS, LANES))

    def precondition(v):
        return {
            key: inverse[key] * v[key] + inverse_off[key] * swap_component(v[key])
            for key in lane_pairs
        }

    residual = gradient
    search = precondition(residual)
    energy = scenario_total(residual, search)
    update = None
    for iteration in range(ITERS):
        image = operator(search)
        step_size = energy / scenario_total(search, image)
        if update is None:
            update = {key: step_size * search[key] for key in lane_pairs}
        else:
            update = {key: update[key] + step_size * search[key] for key in lane_pairs}
        residual = {key: residual[key] - step_size * image[key] for key in lane_pairs}
        if iteration + 1 < ITERS:
            scaled = precondition(residual)
            energy_next = scenario_total(residual, scaled)
            ratio = energy_next / energy
            search = {key: scaled[key] + ratio * search[key] for key in lane_pairs}
            energy = energy_next

    for field, keep_scr, out_ref in (
        (update, step_scr, step_ref),
        (residual, residual_scr, residual_ref),
    ):
        for j, h in lane_pairs:
            keep_scr[j, h] = field[j, h]
        own = []
        for h in range(2):
            tile = keep_scr[mine, h]
            own.append(jnp.where(upper, swap_block(tile), tile))
        for m in range(2):
            width = min(LANES, bus_count - LANES * m)
            values = take_chunks(own, tall(pos_ref[m : m + 1, :]))
            for comp in range(2):
                out_ref[comp, :, LANES * m : LANES * m + width] = values[
                    2 * comp : 2 * comp + 2, :width
                ]


def fast_body(
    volt_mag,
    volt_ang,
    gradient,
    branch_from,
    branch_to,
    branch_count,
    boundary,
    conductance,
    susceptance,
    duals,
    slacks,
    gen_bus,
    gen_curvature,
):
    bus_count = volt_mag.shape[0]
    slot_count = branch_from.shape[0]
    blocks = lax.axis_size("net")
    vmem = pl.BlockSpec(memory_space=pltpu.VMEM)
    smem = pl.BlockSpec(memory_space=pltpu.SMEM)
    payload, position = pl.pallas_call(
        prepare_kernel,
        out_shape=(
            pltpu.VMEM((PAYLOAD_ROWS, LANES), jnp.float32),
            pltpu.VMEM((2, LANES), jnp.int32),
        ),
        in_specs=[vmem] * 13,
        out_specs=(vmem, vmem),
        scratch_shapes=[
            pltpu.VMEM((24, 2 * LANES), jnp.float32),
            pltpu.VMEM((8, 3 * LANES), jnp.float32),
            pltpu.VMEM((8, 3 * LANES), jnp.int32),
        ],
        name="prepare",
    )(
        volt_mag.T,
        volt_ang.T,
        jnp.transpose(gradient, (1, 2, 0)),
        branch_from,
        branch_to,
        branch_count,
        boundary,
        conductance,
        susceptance,
        jnp.transpose(duals, (0, 2, 1)),
        jnp.transpose(slacks, (0, 2, 1)),
        gen_bus,
        gen_curvature,
    )
    def passed(block, other):
        return lax.ppermute(block, "net", [(i, i ^ other) for i in range(blocks)])

    gathered = {0: payload}
    for other in range(2, blocks, 2):
        gathered[other] = passed(payload, other)
    for other in range(0, blocks, 2):
        gathered[other + 1] = passed(gathered[other], 1)
    gathered = [gathered[other] for other in range(blocks)]
    me = lax.axis_index("net").astype(jnp.int32)[None]
    tile_pairs = (blocks // 2, 2, ROWS, LANES)
    field = jax.ShapeDtypeStruct((2, 2, bus_count), jnp.float32)
    step, residual = pl.pallas_call(
        solve_kernel,
        out_shape=(field, field),
        in_specs=[smem] + [vmem] * (1 + blocks),
        out_specs=(vmem, vmem),
        scratch_shapes=[
            pltpu.VMEM((slot_count, 4, blocks // 2, ROWS, LANES), jnp.int32),
            pltpu.VMEM((slot_count, 4, blocks, LANES), jnp.int32),
            pltpu.VMEM((10, blocks, LANES), jnp.float32),
            pltpu.VMEM(
                (2 * len(CHUNK_FIELDS) + 3 * len(SLOT_FIELDS), blocks // 2, ROWS, LANES),
                jnp.float32,
            ),
            pltpu.VMEM(tile_pairs, jnp.float32),
            pltpu.VMEM(tile_pairs, jnp.float32),
        ],
        compiler_params=pltpu.CompilerParams(vmem_limit_bytes=40 * 2**20),
        name="solve",
    )(me, position, *gathered)
    return jnp.transpose(step, (2, 0, 1)), jnp.transpose(residual, (2, 0, 1))


def any_body(*arrays):
    volt_mag, boundary, branch_from, gen_bus = arrays[0], arrays[6], arrays[3], arrays[11]
    fast = fits_fast_path(
        lax.axis_size("net"),
        volt_mag.shape[0],
        boundary.shape[0] // 2,
        branch_from.shape[0],
        gen_bus.shape[0],
        volt_mag.shape[1],
    )
    return fast_body(*arrays) if fast else body(*arrays)


def solution(mesh):
    placed = (
        P("net", "scen"),
        P("net", "scen"),
        P("net", None, "scen"),
        P("net"),
        P("net"),
        P("net"),
        P("net"),
        P("net"),
        P("net"),
        P(None, "net", "scen"),
        P(None, "net", "scen"),
        P("net"),
        P("net"),
    )
    return jax.shard_map(
        any_body,
        mesh=mesh,
        in_specs=placed,
        out_specs=(P("net", None, "scen"), P("net", None, "scen")),
        check_vma=False,
    )
```

```python
import functools

import jax
import jax.numpy as jnp
from jax import lax
from jax.experimental import pallas as pl
from jax.experimental.pallas import tpu as pltpu
from jax.sharding import PartitionSpec as P

ITERS = 4


barrier_weight = 0.01
volt_low = 0.9
volt_high = 1.1
angle_reg = 0.5


def shifted(array, axis, by):
    peers = lax.axis_size(axis)
    pairs = [(i, i + by) for i in range(peers) if 0 <= i + by < peers]
    return lax.ppermute(array, axis, pairs)


def branch_blocks(
    magnitude_from,
    angle_from,
    magnitude_to,
    angle_to,
    conduct,
    suscept,
    weight_active,
    weight_reactive,
):
    angle_diff = angle_from - angle_to
    cosine_diff = jnp.cos(angle_diff)
    sine_diff = jnp.sin(angle_diff)
    flow_along = conduct * cosine_diff + suscept * sine_diff
    flow_across = conduct * sine_diff - suscept * cosine_diff
    cross_term = magnitude_from * magnitude_to
    active_rows = (
        2.0 * conduct * magnitude_from - magnitude_to * flow_along,
        cross_term * flow_across,
        -magnitude_from * flow_along,
        -cross_term * flow_across,
    )
    reactive_rows = (
        -2.0 * suscept * magnitude_from - magnitude_to * flow_across,
        -cross_term * flow_along,
        -magnitude_from * flow_across,
        cross_term * flow_along,
    )

    def block_entry(left_index, right_index):
        return (
            weight_active * active_rows[left_index] * active_rows[right_index]
            + weight_reactive * reactive_rows[left_index] * reactive_rows[right_index]
        )

    from_block = jnp.stack([block_entry(0, 0), block_entry(0, 1), block_entry(1, 1)], axis=1)
    to_block = jnp.stack([block_entry(2, 2), block_entry(2, 3), block_entry(3, 3)], axis=1)
    cross_block = jnp.stack(
        [block_entry(0, 2), block_entry(0, 3), block_entry(1, 2), block_entry(1, 3)], axis=1
    )
    return (from_block, to_block, cross_block)


def apply_cross(matrix_block, vector):
    return jnp.stack(
        [
            matrix_block[:, 0] * vector[:, 0] + matrix_block[:, 1] * vector[:, 1],
            matrix_block[:, 2] * vector[:, 0] + matrix_block[:, 3] * vector[:, 1],
        ],
        axis=1,
    )


def apply_cross_transposed(matrix_block, vector):
    return jnp.stack(
        [
            matrix_block[:, 0] * vector[:, 0] + matrix_block[:, 2] * vector[:, 1],
            matrix_block[:, 1] * vector[:, 0] + matrix_block[:, 3] * vector[:, 1],
        ],
        axis=1,
    )


def scenario_sum(left_vec, right_vec):
    return jnp.sum(left_vec * right_vec, axis=(0, 1))


def widen(values):
    return values[None, None, :]


def body(
    volt_mag,
    volt_ang,
    gradient,
    branch_from,
    branch_to,
    branch_count,
    boundary,
    conductance,
    susceptance,
    duals,
    slacks,
    gen_bus,
    gen_curvature,
):
    bus_count = volt_mag.shape[0]
    ghost_count = boundary.shape[0] // 2
    extended_size = bus_count + 2 * ghost_count
    slot_count = branch_from.shape[0]
    left_list = boundary[:ghost_count]
    right_list = boundary[ghost_count:]
    left_ghost = slice(bus_count, bus_count + ghost_count)
    right_ghost = slice(bus_count + ghost_count, extended_size)
    return_plan = (
        (-1, left_ghost, right_list, right_ghost),
        (1, right_ghost, left_list, left_ghost),
    )

    def share_vector(values):
        pieces = [values]
        for direction in (1, -1):
            outgoing = jnp.take(values, right_list if direction == 1 else left_list, axis=0)
            pieces.append(shifted(outgoing, "net", direction))
        return jnp.concatenate(pieces, axis=0)

    bus_state = jnp.stack([volt_mag, volt_ang], axis=1)
    pieces = [bus_state]
    for share_direction in (1, -1):
        outgoing = jnp.take(bus_state, right_list if share_direction == 1 else left_list, axis=0)
        pieces.append(shifted(outgoing, "net", share_direction))
    extended_state = jnp.concatenate(pieces, axis=0)
    from_state = jnp.take(extended_state, branch_from, axis=0)
    to_state = jnp.take(extended_state, branch_to, axis=0)
    live_mask = (jnp.arange(slot_count) < branch_count[0]).astype(jnp.float32)[:, None]
    weight_active = live_mask * duals[0] / slacks[0]
    weight_reactive = live_mask * duals[1] / slacks[1]
    from_block, to_block, cross_block = branch_blocks(
        from_state[:, 0],
        from_state[:, 1],
        to_state[:, 0],
        to_state[:, 1],
        conductance[:, None],
        susceptance[:, None],
        weight_active,
        weight_reactive,
    )
    diag_extended = jax.ops.segment_sum(
        from_block, branch_from, num_segments=extended_size
    ) + jax.ops.segment_sum(to_block, branch_to, num_segments=extended_size)
    diag_local = diag_extended[:bus_count]
    for direction, ghost_rows, target_rows, source_rows in return_plan:
        arrived_diag = shifted(diag_extended[ghost_rows], "net", direction)
        diag_local = diag_local.at[target_rows].add(arrived_diag)
    gen_table = (gen_bus[None, :] == jnp.arange(bus_count)[:, None]).astype(jnp.float32)
    gen_sum = jnp.dot(gen_table, gen_curvature, precision=lax.Precision.HIGHEST)[:, None]
    barrier = barrier_weight / jnp.square(volt_mag - volt_low) + barrier_weight / jnp.square(
        volt_high - volt_mag
    )
    diag_vv = diag_local[:, 0] + barrier + gen_sum
    diag_va = diag_local[:, 1]
    diag_aa = diag_local[:, 2] + angle_reg + gen_sum
    determinant = diag_vv * diag_aa - diag_va * diag_va
    inverse_vv = diag_aa / determinant
    inverse_va = -diag_va / determinant
    inverse_aa = diag_vv / determinant

    def precondition(vector):
        return jnp.stack(
            [
                inverse_vv * vector[:, 0] + inverse_va * vector[:, 1],
                inverse_va * vector[:, 0] + inverse_aa * vector[:, 1],
            ],
            axis=1,
        )

    update_field = jnp.zeros_like(gradient)
    residual = gradient

    def energy_of(residual_now, scaled_now):
        return lax.psum(scenario_sum(residual_now, scaled_now), "net")

    scaled = precondition(residual)
    search = scaled
    energy = energy_of(residual, scaled)
    for iteration in range(ITERS):
        extended = share_vector(search)
        from_values = jnp.take(extended, branch_from, axis=0)
        to_values = jnp.take(extended, branch_to, axis=0)
        from_terms = apply_cross(cross_block, to_values)
        to_terms = apply_cross_transposed(cross_block, from_values)
        result = jnp.stack(
            [
                diag_vv * search[:, 0] + diag_va * search[:, 1],
                diag_va * search[:, 0] + diag_aa * search[:, 1],
            ],
            axis=1,
        )
        summed = jax.ops.segment_sum(
            from_terms, branch_from, num_segments=extended_size
        ) + jax.ops.segment_sum(to_terms, branch_to, num_segments=extended_size)
        local_sum = result + summed[:bus_count]
        for apply_direction, apply_ghost_rows, apply_target_rows, apply_source_rows in return_plan:
            arrived = shifted(summed[apply_ghost_rows], "net", apply_direction)
            local_sum = local_sum.at[apply_target_rows].add(arrived)
        step_size = energy / lax.psum(scenario_sum(search, local_sum), "net")
        update_field = update_field + widen(step_size) * search
        residual = residual - widen(step_size) * local_sum
        if iteration + 1 < ITERS:
            scaled = precondition(residual)
            energy_next = energy_of(residual, scaled)
            search = scaled + widen(energy_next / energy) * search
            energy = energy_next
    return (update_field, residual)


LANES = 128
ROWS = 8
TILE_A, TILE_B, TILE_C = 0, 2, 4
TILE_LOCAL = 6
TILE_INDEX = 9
PAYLOAD_ROWS = 11 * ROWS
CHUNK_FIELDS = ["gradient", "diag", "diag_off", "vm", "cosv", "sinv"]
CHUNK_FIELDS += ["wp", "wq", "g", "b", "extent"]
SLOT_FIELDS = ["local_main", "local_off", "at_from", "at_to"]
SET_RANKS = 4
SET_RANKS_OUTER = 4


def fits_fast_path(blocks, bus_count, ghost_count, slot_count, gen_count, scen_count):
    return (
        blocks == 8
        and scen_count == 2
        and bus_count == 2 * ghost_count
        and ghost_count <= LANES
        and 2 * LANES < slot_count < 3 * LANES
        and gen_count <= LANES
    )


def iota(shape, dim):
    return lax.broadcasted_iota(jnp.int32, shape, dim)


def lane_take(table, index):
    return jnp.take_along_axis(table, index, axis=1, mode="promise_in_bounds")


def take_chunks(tables, index):
    lane = index & (LANES - 1)
    chunk = index >> 7
    out = lane_take(tables[0], lane)
    for number in range(1, len(tables)):
        out = jnp.where(chunk == number, lane_take(tables[number], lane), out)
    return out


def take_listed(tables, index, default=0):
    lane = index & (LANES - 1)
    chunk = index >> 7
    out = jnp.full(index.shape, default, tables[0].dtype)
    for number, table in enumerate(tables):
        out = jnp.where(chunk == number, lane_take(table, lane), out)
    return out


def tall(row):
    return jnp.broadcast_to(row, (ROWS, LANES))


def column(row):
    return jnp.transpose(jnp.broadcast_to(row, (LANES, LANES)))


def block_entries(vi, ci, si, vj, cj, sj, g, b, wp, wq):
    cosine = ci * cj + si * sj
    sine = si * cj - ci * sj
    along = g * cosine + b * sine
    across = g * sine - b * cosine
    cross = vi * vj
    p0 = 2.0 * g * vi - vj * along
    p1 = cross * across
    p2 = -vi * along
    q0 = -2.0 * b * vi - vj * across
    q1 = -cross * along
    q2 = -vi * across

    def entry(pa, pb, qa, qb):
        return wp * pa * pb + wq * qa * qb

    return (
        entry(p0, p0, q0, q0),
        entry(p0, p1, q0, q1),
        entry(p1, p1, q1, q1),
        entry(p2, p2, q2, q2),
        entry(p1, p2, q1, q2),
        entry(p0, p2, q0, q2),
    )


def prepare_kernel(
    vm_ref,
    va_ref,
    grad_ref,
    from_ref,
    to_ref,
    count_ref,
    bound_ref,
    g_ref,
    b_ref,
    duals_ref,
    slacks_ref,
    gen_bus_ref,
    gen_curv_ref,
    out_ref,
    pos_ref,
    bus_scr,
    branch_scr,
    index_scr,
):
    bus_count = vm_ref.shape[1]
    ghost_count = bus_count // 2
    slot_count = from_ref.shape[0]
    gen_count = gen_bus_ref.shape[0]
    none = 3 * LANES - 1
    live_count = count_ref[...][None]

    bus_scr[...] = jnp.zeros_like(bus_scr)
    branch_scr[...] = jnp.zeros_like(branch_scr)
    index_scr[...] = jnp.full_like(index_scr, -9)
    for copy in range(4):
        bus_scr[2 * copy : 2 * copy + 2, :bus_count] = vm_ref[...]
        bus_scr[8 + 2 * copy : 10 + 2 * copy, :bus_count] = va_ref[...]
    for comp in range(2):
        bus_scr[16 + 2 * comp : 18 + 2 * comp, :bus_count] = grad_ref[comp]
    live = iota((2, slot_count), 1) < live_count
    for kind in range(2):
        weight = jnp.where(live, duals_ref[kind] / slacks_ref[kind], 0.0)
        branch_scr[2 * kind : 2 * kind + 2, :slot_count] = weight
    branch_scr[4:5, :slot_count] = g_ref[...][None]
    branch_scr[5:6, :slot_count] = b_ref[...][None]
    branch_scr[6:7, :slot_count] = from_ref[...][None].astype(jnp.float32)
    branch_scr[7:8, :slot_count] = to_ref[...][None].astype(jnp.float32)
    bus_scr[20:21, :gen_count] = gen_curv_ref[...][None]
    index_scr[0:1, :slot_count] = from_ref[...][None]
    index_scr[1:2, :slot_count] = to_ref[...][None]
    index_scr[2:3, :bus_count] = bound_ref[...][None]
    index_scr[3:4, :gen_count] = gen_bus_ref[...][None]

    def tiles(ref, first, chunks):
        return [ref[first : first + ROWS, LANES * c : LANES * (c + 1)] for c in range(chunks)]

    def row(ref, number, chunk):
        return ref[number : number + 1, LANES * chunk : LANES * (chunk + 1)]

    lane = iota((ROWS, LANES), 1)
    sub = iota((ROWS, LANES), 0)
    lane_row = iota((1, LANES), 1)
    sub_col = iota((LANES, LANES), 0).astype(jnp.float32)
    inside = lane < ghost_count

    raw_bound = [tall(row(index_scr, 2, c)) for c in range(2)]
    bound = [jnp.where(inside, take_chunks(raw_bound, lane + h * ghost_count), -1) for h in range(2)]
    fetch = [jnp.maximum(b, 0) for b in bound]
    bound_row = [b[0:1].astype(jnp.float32) for b in bound]
    vm_raw, va_raw, grad_raw = (tiles(bus_scr, 8 * f, 2) for f in range(3))
    vm = [jnp.where(inside, take_chunks(vm_raw, f), 1.0) for f in fetch]
    va = [jnp.where(inside, take_chunks(va_raw, f), 0.0) for f in fetch]
    grad = [jnp.where(inside, take_chunks(grad_raw, f), 0.0) for f in fetch]
    cosv = [jnp.cos(a) for a in va]
    sinv = [jnp.sin(a) for a in va]

    earlier = (iota((LANES, LANES), 0) < iota((LANES, LANES), 1)).astype(jnp.bfloat16)
    local, cross_key, place = [], [], []
    local_count = jnp.zeros((1, 1), jnp.float32)
    for c in range(3):
        slot = lane_row + LANES * c
        alive = (slot < live_count) & (slot < slot_count)
        to_raw = row(index_scr, 1, c)
        cross_key.append(jnp.where(alive, to_raw, 9999).astype(jnp.float32))
        keep = jnp.where(alive & (to_raw < bus_count), 1.0, 0.0)
        before = jnp.dot(
            tall(keep).astype(jnp.bfloat16), earlier, preferred_element_type=jnp.float32
        )
        place.append(jnp.where(keep > 0.0, before[0:1] + local_count, -1.0))
        local_count = local_count + jnp.sum(keep, axis=1, keepdims=True)
    place_col = [column(p) for p in place]
    lane_f = lane_row.astype(jnp.float32)
    branch_tiles = tiles(branch_scr, 0, 3)

    def lowest(masks):
        found = functools.reduce(
            jnp.minimum,
            [jnp.where(m, sub_col + float(LANES * c), float(none)) for c, m in masks],
        )
        return jnp.min(found, axis=0, keepdims=True)

    packed, from_key, to_key = [], [], []
    for c in range(3):
        source = lowest([(d, place_col[d] == lane_f + float(LANES * c)) for d in range(c, 3)])
        tile = take_chunks(branch_tiles, tall(source).astype(jnp.int32))
        packed.append(tile)
        empty = source == float(none)
        from_key.append(jnp.where(empty, 9998.0, tile[6:7]))
        to_key.append(jnp.where(empty, 9999.0, tile[7:8]))
    from_col = [column(k) for k in from_key]
    to_col = [column(k) for k in to_key]
    cross_col = [column(k) for k in cross_key[:2]]
    bound_col = [column(b) for b in bound_row]
    gen_col = column(row(index_scr, 3, 0).astype(jnp.float32))
    curv_col = column(row(bus_scr, 20, 0))

    def links(keys, cols):
        heads, counts, matches = [], [], []
        for h in range(2):
            equal = [cols[c] == bound_row[h] for c in range(3)]
            matches.append([jnp.where(e, 1.0, 0.0).astype(jnp.bfloat16) for e in equal])
            heads.append(lowest(list(enumerate(equal))))
            counts.append(
                jnp.sum(
                    functools.reduce(jnp.add, [jnp.where(e, 1.0, 0.0) for e in equal]),
                    axis=0,
                    keepdims=True,
                )
            )
        nexts = []
        for c in range(3):
            later = [(c, (cols[c] == keys[c]) & (sub_col > lane_f))]
            later += [(d, cols[d] == keys[c]) for d in range(c + 1, 3)]
            nexts.append(lowest(later))
        return heads, nexts, jnp.maximum(counts[0], counts[1]), matches

    head_f, next_f, count_f, match_f = links(from_key, from_col)
    head_t, next_t, count_t, match_t = links(to_key, to_col)
    degree = jnp.max(jnp.maximum(count_f, count_t))

    def position(keys):
        found = [
            jnp.where(bound_col[h] == keys, sub_col + float(LANES * h), 0.0) for h in range(2)
        ]
        return jnp.max(jnp.maximum(found[0], found[1]), axis=0, keepdims=True)

    pos_f = [position(k) for k in from_key]
    pos_t = [position(k) for k in to_key]
    for m in range(2):
        pos_ref[m : m + 1, :] = position((lane_row + LANES * m).astype(jnp.float32)).astype(jnp.int32)

    cross = []
    for h in range(2):
        target = jnp.where(lane_row < ghost_count, bus_count + h * ghost_count + lane_row, -5)
        slot = lowest([(c, cross_col[c] == target.astype(jnp.float32)) for c in range(2)])
        cross.append(take_chunks(branch_tiles, tall(slot).astype(jnp.int32)))

    gens = [
        jnp.sum(jnp.where(gen_col == bound_row[h], curv_col, 0.0), axis=0, keepdims=True)
        for h in range(2)
    ]

    pair = sub & 3

    def every_pair(x):
        x = jnp.where(sub < 2, x, pltpu.roll(x, 2, 0))
        return jnp.where(sub < 4, x, pltpu.roll(x, 4, 0))

    from_table, to_table = [], []
    for c in range(3):
        at_f = tall(pos_f[c]).astype(jnp.int32)
        at_t = tall(pos_t[c]).astype(jnp.int32)
        h00, h01, h11, h22, h12, h02 = block_entries(
            *(take_chunks(t, at_f) for t in (vm, cosv, sinv)),
            *(take_chunks(t, at_t) for t in (vm, cosv, sinv)),
            tall(packed[c][4:5]),
            tall(packed[c][5:6]),
            every_pair(packed[c]),
            every_pair(pltpu.roll(packed[c], 6, 0)),
        )
        main = jnp.where(pair < 2, h02, -h11)
        off = jnp.where(pair < 2, -h01, h12)
        first = ROWS * (TILE_LOCAL + c)
        out_ref[first : first + ROWS, :] = jnp.where(sub < 4, main, off)
        from_table.append(jnp.where(sub < 2, h00, jnp.where(sub < 4, h01, h11)))
        to_table.append(jnp.where(sub < 2, h22, jnp.where(sub < 4, -h12, h11)))

    def parts(x):
        high = x.astype(jnp.bfloat16).astype(jnp.float32)
        middle = (x - high).astype(jnp.bfloat16).astype(jnp.float32)
        rest = x - high - middle
        return jnp.concatenate([high, middle, rest, jnp.zeros_like(x)], axis=0).astype(jnp.bfloat16)

    terms = [parts(t) for t in from_table + to_table]
    acc = []
    for h in range(2):
        total = functools.reduce(
            jnp.add,
            [
                jnp.dot(term, match, preferred_element_type=jnp.float32)
                for term, match in zip(terms, match_f[h] + match_t[h])
            ],
        )
        acc.append(total[0:8] + total[8:16] + total[16:24])

    total_local = jnp.max(local_count)

    for h in range(2):
        below = vm[h] - volt_low
        above = volt_high - vm[h]
        barrier = barrier_weight / (below * below) + barrier_weight / (above * above)
        diag_vv = pltpu.roll(acc[h], 4, 0) + barrier + gens[h]
        diag_aa = pltpu.roll(acc[h], 2, 0) + angle_reg + gens[h]
        diag_va = pltpu.roll(acc[h], 6, 0)
        first = ROWS * (TILE_A + h)
        out_ref[first : first + ROWS, :] = jnp.where(
            sub < 4, grad[h], jnp.where(sub < 6, diag_vv, diag_aa)
        )
        first = ROWS * (TILE_B + h)
        out_ref[first : first + ROWS, :] = jnp.where(
            sub < 2, diag_va, jnp.where(sub < 4, vm[h], jnp.where(sub < 6, cosv[h], sinv[h]))
        )
        first = ROWS * (TILE_C + h)
        out_ref[first : first + ROWS, :] = jnp.where(
            sub < 6, cross[h], jnp.where(sub == 6, degree, total_local)
        )
    first = ROWS * TILE_INDEX
    for offset, value in enumerate(pos_f + pos_t + head_f + head_t + next_f + next_t):
        out_ref[first + offset : first + offset + 1, :] = value


def solve_kernel(me_ref, pos_ref, *refs):
    *all_refs, step_ref, residual_ref = refs[:-6]
    chain_scr, end_scr, row_scr, field_scr, step_scr, residual_scr = refs[-6:]
    blocks = len(all_refs)
    me = me_ref[0]
    half = blocks // 2
    bus_count = step_ref.shape[2]
    lane_pairs = [(j, h) for j in range(half) for h in range(2)]
    sub = iota((ROWS, LANES), 0)
    low = sub < 4
    even = (sub & 3) < 2

    def swap_component(x):
        return jnp.where(even, pltpu.roll(x, 6, 0), pltpu.roll(x, 2, 0))

    def swap_block(x):
        return pltpu.roll(x, 4, 0)

    upper = me >= half
    mine = jnp.where(upper, blocks - 1 - me, me)
    near = low != upper

    def halves(tile, j):
        here = all_refs[j][ROWS * tile : ROWS * (tile + 1), :]
        there = all_refs[blocks - 1 - j][ROWS * tile : ROWS * (tile + 1), :]
        first = jnp.where(upper, there, here)
        second = jnp.where(upper, here, there)
        return (
            jnp.where(low, first, swap_block(second)),
            jnp.where(low, swap_block(first), second),
        )

    def quarters(x):
        return (
            jnp.where(even, x, pltpu.roll(x, 2, 0)),
            jnp.where(even, pltpu.roll(x, 6, 0), x),
        )

    def single(number, j):
        return jnp.where(
            near,
            tall(all_refs[j][number : number + 1, :]),
            tall(all_refs[blocks - 1 - j][number : number + 1, :]),
        )

    def across(field):
        out = {}
        for j in range(half):
            inner = [
                field[j + 1, 1 - h] if j + 1 < half else swap_block(field[j, 1 - h])
                for h in range(2)
            ]
            outer = [field[j - 1, 1 - h] if j > 0 else 0.0 for h in range(2)]
            out[j, 0] = jnp.where(low, outer[0], inner[0])
            out[j, 1] = jnp.where(low, inner[1], outer[1])
        return out

    base = ROWS * TILE_INDEX
    names = [(name, h) for name in CHUNK_FIELDS for h in range(2)]
    names += [(name, c) for name in SLOT_FIELDS for c in range(3)]
    place = {name: number for number, name in enumerate(names)}
    for j in range(half):
        found = {}
        for h in range(2):
            found["gradient", h], found["diag", h] = halves(TILE_A + h, j)
            first, second = halves(TILE_B + h, j)
            found["diag_off", h], found["vm", h] = quarters(first)
            found["cosv", h], found["sinv", h] = quarters(second)
            first, _ = halves(TILE_C + h, j)
            found["wp", h], found["wq", h] = quarters(first)
            found["g", h] = single(ROWS * (TILE_C + h) + 4, j)
            found["b", h] = single(ROWS * (TILE_C + h) + 5, j)
            found["extent", h] = single(ROWS * TILE_C + 6 + h, j)
        for c in range(3):
            found["local_main", c], found["local_off", c] = halves(TILE_LOCAL + c, j)
            found["at_from", c] = single(base + c, j)
            found["at_to", c] = single(base + 3 + c, j)
        for name, number in place.items():
            field_scr[number, j ^ mine] = found[name]

    def load(name, chunks):
        return {
            (j, c): field_scr[place[name, c], j] for j in range(half) for c in range(chunks)
        }

    gradient, diag, diag_off, vm, cosv, sinv, wp, wq, g, b, extent = (
        load(name, 2) for name in CHUNK_FIELDS
    )
    vm_to, cos_to, sin_to = across(vm), across(cosv), across(sinv)
    to_diag, to_off, main, off = {}, {}, {}, {}
    for key in lane_pairs:
        h00, h01, h11, h22, h12, h02 = block_entries(
            vm[key],
            cosv[key],
            sinv[key],
            vm_to[key],
            cos_to[key],
            sin_to[key],
            g[key],
            b[key],
            wp[key],
            wq[key],
        )
        diag[key] = diag[key] + jnp.where(even, h00, h11)
        diag_off[key] = diag_off[key] + h01
        to_diag[key] = jnp.where(even, h22, h11)
        to_off[key] = -h12
        main[key] = jnp.where(even, h02, -h11)
        off[key] = jnp.where(even, -h01, h12)
    to_diag, to_off = across(to_diag), across(to_off)
    main_to = across(main)
    off_to = across({key: swap_component(off[key]) for key in lane_pairs})
    inverse, inverse_off = {}, {}
    for key in lane_pairs:
        diag[key] = diag[key] + to_diag[key]
        diag_off[key] = diag_off[key] + to_off[key]
        main[key] = main[key] + main_to[key]
        off[key] = off[key] + off_to[key]
        flipped = swap_component(diag[key])
        determinant = diag[key] * flipped - diag_off[key] * diag_off[key]
        inverse[key] = flipped / determinant
        inverse_off[key] = -diag_off[key] / determinant

    def largest(h, pairs):
        return jnp.max(functools.reduce(jnp.maximum, [extent[j, h] for j in pairs]))

    outer_rank = largest(0, [0]).astype(jnp.int32)
    inner_rank = largest(0, range(1, half)).astype(jnp.int32)
    few = (largest(1, [0]) <= 2.0 * LANES) & (largest(1, range(1, half)) <= 1.0 * LANES)

    for number in range(10):
        for s, ref in enumerate(all_refs):
            row_scr[number, s : s + 1, :] = ref[base + 6 + number : base + 7 + number, :]
    links = [row_scr[number].astype(jnp.int32) for number in range(10)]
    heads, next_f, next_t = links[:4], links[4:7], links[7:]

    def follow(rank, ends):
        for kind in range(4):
            end_scr[rank, kind] = ends[kind]
            for j in range(half):
                here = tall(end_scr[rank, kind, j : j + 1, :])
                there = tall(end_scr[rank, kind, blocks - 1 - j : blocks - j, :])
                chain_scr[rank, kind, j ^ mine] = jnp.where(near, here, there)
        return tuple(
            take_chunks(next_f if kind < 2 else next_t, ends[kind]) for kind in range(4)
        )

    ends = tuple(heads)
    for rank in range(SET_RANKS_OUTER):
        ends = follow(rank, ends)
    lax.fori_loop(SET_RANKS_OUTER, jnp.maximum(outer_rank, inner_rank), follow, ends)

    def local_sums(v, sums, outer_chunks, inner_chunks):
        chunks = [outer_chunks] + [inner_chunks] * (half - 1)
        to_from, to_to = {}, {}
        for j in range(half):
            table = [v[j, 0], v[j, 1]]
            for c in range(chunks[j]):
                main_c, off_c, at_from, at_to = (
                    field_scr[place[name, c], j] for name in SLOT_FIELDS
                )
                far = take_chunks(table, at_to.astype(jnp.int32))
                near = take_chunks(table, at_from.astype(jnp.int32))
                to_from[j, c] = main_c * far + off_c * swap_component(far)
                to_to[j, c] = main_c * near + swap_component(off_c * near)

        def add_rank(pairs, rank, sums):
            sums = list(sums)
            for number, (j, h) in enumerate(lane_pairs):
                if j in pairs:
                    for offset, terms in ((0, to_from), (2, to_to)):
                        sums[number] += take_listed(
                            [terms[j, c] for c in range(chunks[j])], chain_scr[rank, offset + h, j]
                        )
            return tuple(sums)

        for rank in range(SET_RANKS_OUTER):
            sums = add_rank(range(half if rank < SET_RANKS else 1), rank, sums)
        inner = functools.partial(add_rank, range(1, half))
        sums = lax.fori_loop(SET_RANKS, inner_rank, inner, sums)
        return lax.fori_loop(SET_RANKS_OUTER, outer_rank, functools.partial(add_rank, [0]), sums)

    def operator(v):
        flipped = {key: swap_component(v[key]) for key in lane_pairs}
        v_to, flipped_to = across(v), across(flipped)
        out = tuple(
            diag[key] * v[key]
            + diag_off[key] * flipped[key]
            + main[key] * v_to[key]
            + off[key] * flipped_to[key]
            for key in lane_pairs
        )
        sums = lax.cond(
            few, lambda: local_sums(v, out, 2, 1), lambda: local_sums(v, out, 3, 3)
        )
        return dict(zip(lane_pairs, sums))

    def scenario_total(left, right):
        total = functools.reduce(jnp.add, [left[key] * right[key] for key in lane_pairs])
        total = total + pltpu.roll(total, 2, 0)
        total = total + pltpu.roll(total, 4, 0)
        return jnp.broadcast_to(jnp.sum(total, axis=1, keepdims=True), (ROWS, LANES))

    def precondition(v):
        return {
            key: inverse[key] * v[key] + inverse_off[key] * swap_component(v[key])
            for key in lane_pairs
        }

    residual = gradient
    search = precondition(residual)
    energy = scenario_total(residual, search)
    update = None
    for iteration in range(ITERS):
        image = operator(search)
        step_size = energy / scenario_total(search, image)
        if update is None:
            update = {key: step_size * search[key] for key in lane_pairs}
        else:
            update = {key: update[key] + step_size * search[key] for key in lane_pairs}
        residual = {key: residual[key] - step_size * image[key] for key in lane_pairs}
        if iteration + 1 < ITERS:
            scaled = precondition(residual)
            energy_next = scenario_total(residual, scaled)
            ratio = energy_next / energy
            search = {key: scaled[key] + ratio * search[key] for key in lane_pairs}
            energy = energy_next

    for field, keep_scr, out_ref in (
        (update, step_scr, step_ref),
        (residual, residual_scr, residual_ref),
    ):
        for j, h in lane_pairs:
            keep_scr[j, h] = field[j, h]
        own = []
        for h in range(2):
            tile = keep_scr[mine, h]
            own.append(jnp.where(upper, swap_block(tile), tile))
        for m in range(2):
            width = min(LANES, bus_count - LANES * m)
            values = take_chunks(own, tall(pos_ref[m : m + 1, :]))
            for comp in range(2):
                out_ref[comp, :, LANES * m : LANES * m + width] = values[
                    2 * comp : 2 * comp + 2, :width
                ]


def fast_body(
    volt_mag,
    volt_ang,
    gradient,
    branch_from,
    branch_to,
    branch_count,
    boundary,
    conductance,
    susceptance,
    duals,
    slacks,
    gen_bus,
    gen_curvature,
):
    bus_count = volt_mag.shape[0]
    slot_count = branch_from.shape[0]
    blocks = lax.axis_size("net")
    vmem = pl.BlockSpec(memory_space=pltpu.VMEM)
    smem = pl.BlockSpec(memory_space=pltpu.SMEM)
    payload, position = pl.pallas_call(
        prepare_kernel,
        out_shape=(
            pltpu.VMEM((PAYLOAD_ROWS, LANES), jnp.float32),
            pltpu.VMEM((2, LANES), jnp.int32),
        ),
        in_specs=[vmem] * 13,
        out_specs=(vmem, vmem),
        scratch_shapes=[
            pltpu.VMEM((24, 2 * LANES), jnp.float32),
            pltpu.VMEM((8, 3 * LANES), jnp.float32),
            pltpu.VMEM((8, 3 * LANES), jnp.int32),
        ],
        name="prepare",
    )(
        volt_mag.T,
        volt_ang.T,
        jnp.transpose(gradient, (1, 2, 0)),
        branch_from,
        branch_to,
        branch_count,
        boundary,
        conductance,
        susceptance,
        jnp.transpose(duals, (0, 2, 1)),
        jnp.transpose(slacks, (0, 2, 1)),
        gen_bus,
        gen_curvature,
    )
    def passed(block, other):
        return lax.ppermute(block, "net", [(i, i ^ other) for i in range(blocks)])

    gathered = {0: payload}
    for other in range(2, blocks, 2):
        gathered[other] = passed(payload, other)
    for other in range(0, blocks, 2):
        gathered[other + 1] = passed(gathered[other], 1)
    gathered = [gathered[other] for other in range(blocks)]
    me = lax.axis_index("net").astype(jnp.int32)[None]
    tile_pairs = (blocks // 2, 2, ROWS, LANES)
    field = jax.ShapeDtypeStruct((2, 2, bus_count), jnp.float32)
    step, residual = pl.pallas_call(
        solve_kernel,
        out_shape=(field, field),
        in_specs=[smem] + [vmem] * (1 + blocks),
        out_specs=(vmem, vmem),
        scratch_shapes=[
            pltpu.VMEM((slot_count, 4, blocks // 2, ROWS, LANES), jnp.int32),
            pltpu.VMEM((slot_count, 4, blocks, LANES), jnp.int32),
            pltpu.VMEM((10, blocks, LANES), jnp.float32),
            pltpu.VMEM(
                (2 * len(CHUNK_FIELDS) + 3 * len(SLOT_FIELDS), blocks // 2, ROWS, LANES),
                jnp.float32,
            ),
            pltpu.VMEM(tile_pairs, jnp.float32),
            pltpu.VMEM(tile_pairs, jnp.float32),
        ],
        compiler_params=pltpu.CompilerParams(vmem_limit_bytes=40 * 2**20),
        name="solve",
    )(me, position, *gathered)
    return jnp.transpose(step, (2, 0, 1)), jnp.transpose(residual, (2, 0, 1))


def any_body(*arrays):
    volt_mag, boundary, branch_from, gen_bus = arrays[0], arrays[6], arrays[3], arrays[11]
    fast = fits_fast_path(
        lax.axis_size("net"),
        volt_mag.shape[0],
        boundary.shape[0] // 2,
        branch_from.shape[0],
        gen_bus.shape[0],
        volt_mag.shape[1],
    )
    return fast_body(*arrays) if fast else body(*arrays)


def solution(mesh):
    placed = (
        P("net", "scen"),
        P("net", "scen"),
        P("net", None, "scen"),
        P("net"),
        P("net"),
        P("net"),
        P("net"),
        P("net"),
        P("net"),
        P(None, "net", "scen"),
        P(None, "net", "scen"),
        P("net"),
        P("net"),
    )
    return jax.shard_map(
        any_body,
        mesh=mesh,
        in_specs=placed,
        out_specs=(P("net", None, "scen"), P("net", None, "scen")),
        check_vma=False,
    )
```

```python
import functools

import jax
import jax.numpy as jnp
from jax import lax
from jax.experimental import pallas as pl
from jax.experimental.pallas import tpu as pltpu
from jax.sharding import PartitionSpec as P

ITERS = 4


barrier_weight = 0.01
volt_low = 0.9
volt_high = 1.1
angle_reg = 0.5


def shifted(array, axis, by):
    peers = lax.axis_size(axis)
    pairs = [(i, i + by) for i in range(peers) if 0 <= i + by < peers]
    return lax.ppermute(array, axis, pairs)


def branch_blocks(
    magnitude_from,
    angle_from,
    magnitude_to,
    angle_to,
    conduct,
    suscept,
    weight_active,
    weight_reactive,
):
    angle_diff = angle_from - angle_to
    cosine_diff = jnp.cos(angle_diff)
    sine_diff = jnp.sin(angle_diff)
    flow_along = conduct * cosine_diff + suscept * sine_diff
    flow_across = conduct * sine_diff - suscept * cosine_diff
    cross_term = magnitude_from * magnitude_to
    active_rows = (
        2.0 * conduct * magnitude_from - magnitude_to * flow_along,
        cross_term * flow_across,
        -magnitude_from * flow_along,
        -cross_term * flow_across,
    )
    reactive_rows = (
        -2.0 * suscept * magnitude_from - magnitude_to * flow_across,
        -cross_term * flow_along,
        -magnitude_from * flow_across,
        cross_term * flow_along,
    )

    def block_entry(left_index, right_index):
        return (
            weight_active * active_rows[left_index] * active_rows[right_index]
            + weight_reactive * reactive_rows[left_index] * reactive_rows[right_index]
        )

    from_block = jnp.stack([block_entry(0, 0), block_entry(0, 1), block_entry(1, 1)], axis=1)
    to_block = jnp.stack([block_entry(2, 2), block_entry(2, 3), block_entry(3, 3)], axis=1)
    cross_block = jnp.stack(
        [block_entry(0, 2), block_entry(0, 3), block_entry(1, 2), block_entry(1, 3)], axis=1
    )
    return (from_block, to_block, cross_block)


def apply_cross(matrix_block, vector):
    return jnp.stack(
        [
            matrix_block[:, 0] * vector[:, 0] + matrix_block[:, 1] * vector[:, 1],
            matrix_block[:, 2] * vector[:, 0] + matrix_block[:, 3] * vector[:, 1],
        ],
        axis=1,
    )


def apply_cross_transposed(matrix_block, vector):
    return jnp.stack(
        [
            matrix_block[:, 0] * vector[:, 0] + matrix_block[:, 2] * vector[:, 1],
            matrix_block[:, 1] * vector[:, 0] + matrix_block[:, 3] * vector[:, 1],
        ],
        axis=1,
    )


def scenario_sum(left_vec, right_vec):
    return jnp.sum(left_vec * right_vec, axis=(0, 1))


def widen(values):
    return values[None, None, :]


def body(
    volt_mag,
    volt_ang,
    gradient,
    branch_from,
    branch_to,
    branch_count,
    boundary,
    conductance,
    susceptance,
    duals,
    slacks,
    gen_bus,
    gen_curvature,
):
    bus_count = volt_mag.shape[0]
    ghost_count = boundary.shape[0] // 2
    extended_size = bus_count + 2 * ghost_count
    slot_count = branch_from.shape[0]
    left_list = boundary[:ghost_count]
    right_list = boundary[ghost_count:]
    left_ghost = slice(bus_count, bus_count + ghost_count)
    right_ghost = slice(bus_count + ghost_count, extended_size)
    return_plan = (
        (-1, left_ghost, right_list, right_ghost),
        (1, right_ghost, left_list, left_ghost),
    )

    def share_vector(values):
        pieces = [values]
        for direction in (1, -1):
            outgoing = jnp.take(values, right_list if direction == 1 else left_list, axis=0)
            pieces.append(shifted(outgoing, "net", direction))
        return jnp.concatenate(pieces, axis=0)

    bus_state = jnp.stack([volt_mag, volt_ang], axis=1)
    pieces = [bus_state]
    for share_direction in (1, -1):
        outgoing = jnp.take(bus_state, right_list if share_direction == 1 else left_list, axis=0)
        pieces.append(shifted(outgoing, "net", share_direction))
    extended_state = jnp.concatenate(pieces, axis=0)
    from_state = jnp.take(extended_state, branch_from, axis=0)
    to_state = jnp.take(extended_state, branch_to, axis=0)
    live_mask = (jnp.arange(slot_count) < branch_count[0]).astype(jnp.float32)[:, None]
    weight_active = live_mask * duals[0] / slacks[0]
    weight_reactive = live_mask * duals[1] / slacks[1]
    from_block, to_block, cross_block = branch_blocks(
        from_state[:, 0],
        from_state[:, 1],
        to_state[:, 0],
        to_state[:, 1],
        conductance[:, None],
        susceptance[:, None],
        weight_active,
        weight_reactive,
    )
    diag_extended = jax.ops.segment_sum(
        from_block, branch_from, num_segments=extended_size
    ) + jax.ops.segment_sum(to_block, branch_to, num_segments=extended_size)
    diag_local = diag_extended[:bus_count]
    for direction, ghost_rows, target_rows, source_rows in return_plan:
        arrived_diag = shifted(diag_extended[ghost_rows], "net", direction)
        diag_local = diag_local.at[target_rows].add(arrived_diag)
    gen_table = (gen_bus[None, :] == jnp.arange(bus_count)[:, None]).astype(jnp.float32)
    gen_sum = jnp.dot(gen_table, gen_curvature, precision=lax.Precision.HIGHEST)[:, None]
    barrier = barrier_weight / jnp.square(volt_mag - volt_low) + barrier_weight / jnp.square(
        volt_high - volt_mag
    )
    diag_vv = diag_local[:, 0] + barrier + gen_sum
    diag_va = diag_local[:, 1]
    diag_aa = diag_local[:, 2] + angle_reg + gen_sum
    determinant = diag_vv * diag_aa - diag_va * diag_va
    inverse_vv = diag_aa / determinant
    inverse_va = -diag_va / determinant
    inverse_aa = diag_vv / determinant

    def precondition(vector):
        return jnp.stack(
            [
                inverse_vv * vector[:, 0] + inverse_va * vector[:, 1],
                inverse_va * vector[:, 0] + inverse_aa * vector[:, 1],
            ],
            axis=1,
        )

    update_field = jnp.zeros_like(gradient)
    residual = gradient

    def energy_of(residual_now, scaled_now):
        return lax.psum(scenario_sum(residual_now, scaled_now), "net")

    scaled = precondition(residual)
    search = scaled
    energy = energy_of(residual, scaled)
    for iteration in range(ITERS):
        extended = share_vector(search)
        from_values = jnp.take(extended, branch_from, axis=0)
        to_values = jnp.take(extended, branch_to, axis=0)
        from_terms = apply_cross(cross_block, to_values)
        to_terms = apply_cross_transposed(cross_block, from_values)
        result = jnp.stack(
            [
                diag_vv * search[:, 0] + diag_va * search[:, 1],
                diag_va * search[:, 0] + diag_aa * search[:, 1],
            ],
            axis=1,
        )
        summed = jax.ops.segment_sum(
            from_terms, branch_from, num_segments=extended_size
        ) + jax.ops.segment_sum(to_terms, branch_to, num_segments=extended_size)
        local_sum = result + summed[:bus_count]
        for apply_direction, apply_ghost_rows, apply_target_rows, apply_source_rows in return_plan:
            arrived = shifted(summed[apply_ghost_rows], "net", apply_direction)
            local_sum = local_sum.at[apply_target_rows].add(arrived)
        step_size = energy / lax.psum(scenario_sum(search, local_sum), "net")
        update_field = update_field + widen(step_size) * search
        residual = residual - widen(step_size) * local_sum
        if iteration + 1 < ITERS:
            scaled = precondition(residual)
            energy_next = energy_of(residual, scaled)
            search = scaled + widen(energy_next / energy) * search
            energy = energy_next
    return (update_field, residual)


LANES = 128
ROWS = 8
TILE_A, TILE_B, TILE_C = 0, 2, 4
TILE_LOCAL = 6
TILE_INDEX = 9
PAYLOAD_ROWS = 11 * ROWS
CHUNK_FIELDS = ["gradient", "diag", "diag_off", "vm", "cosv", "sinv"]
CHUNK_FIELDS += ["wp", "wq", "g", "b", "extent"]
SLOT_FIELDS = ["local_main", "local_off", "at_from", "at_to"]
SET_RANKS = 4
SET_RANKS_OUTER = 4


def fits_fast_path(blocks, bus_count, ghost_count, slot_count, gen_count, scen_count):
    return (
        blocks == 8
        and scen_count == 2
        and bus_count == 2 * ghost_count
        and ghost_count <= LANES
        and 2 * LANES < slot_count < 3 * LANES
        and gen_count <= LANES
    )


def iota(shape, dim):
    return lax.broadcasted_iota(jnp.int32, shape, dim)


def lane_take(table, index):
    return jnp.take_along_axis(table, index, axis=1, mode="promise_in_bounds")


def take_chunks(tables, index):
    lane = index & (LANES - 1)
    chunk = index >> 7
    out = lane_take(tables[0], lane)
    for number in range(1, len(tables)):
        out = jnp.where(chunk == number, lane_take(tables[number], lane), out)
    return out


def take_listed(tables, index, default=0):
    lane = index & (LANES - 1)
    chunk = index >> 7
    out = jnp.full(index.shape, default, tables[0].dtype)
    for number, table in enumerate(tables):
        out = jnp.where(chunk == number, lane_take(table, lane), out)
    return out


def tall(row):
    return jnp.broadcast_to(row, (ROWS, LANES))


def column(row):
    return jnp.transpose(jnp.broadcast_to(row, (LANES, LANES)))


def block_entries(vi, ci, si, vj, cj, sj, g, b, wp, wq):
    cosine = ci * cj + si * sj
    sine = si * cj - ci * sj
    along = g * cosine + b * sine
    across = g * sine - b * cosine
    cross = vi * vj
    p0 = 2.0 * g * vi - vj * along
    p1 = cross * across
    p2 = -vi * along
    q0 = -2.0 * b * vi - vj * across
    q1 = -cross * along
    q2 = -vi * across

    def entry(pa, pb, qa, qb):
        return wp * pa * pb + wq * qa * qb

    return (
        entry(p0, p0, q0, q0),
        entry(p0, p1, q0, q1),
        entry(p1, p1, q1, q1),
        entry(p2, p2, q2, q2),
        entry(p1, p2, q1, q2),
        entry(p0, p2, q0, q2),
    )


def prepare_kernel(
    vm_ref,
    va_ref,
    grad_ref,
    from_ref,
    to_ref,
    count_ref,
    bound_ref,
    g_ref,
    b_ref,
    duals_ref,
    slacks_ref,
    gen_bus_ref,
    gen_curv_ref,
    out_ref,
    pos_ref,
    bus_scr,
    branch_scr,
    index_scr,
):
    bus_count = vm_ref.shape[1]
    ghost_count = bus_count // 2
    slot_count = from_ref.shape[0]
    gen_count = gen_bus_ref.shape[0]
    none = 3 * LANES - 1
    live_count = count_ref[...][None]

    bus_scr[...] = jnp.zeros_like(bus_scr)
    branch_scr[...] = jnp.zeros_like(branch_scr)
    index_scr[...] = jnp.full_like(index_scr, -9)
    for copy in range(4):
        bus_scr[2 * copy : 2 * copy + 2, :bus_count] = vm_ref[...]
        bus_scr[8 + 2 * copy : 10 + 2 * copy, :bus_count] = va_ref[...]
    for comp in range(2):
        bus_scr[16 + 2 * comp : 18 + 2 * comp, :bus_count] = grad_ref[comp]
    live = iota((2, slot_count), 1) < live_count
    for kind in range(2):
        weight = jnp.where(live, duals_ref[kind] / slacks_ref[kind], 0.0)
        branch_scr[2 * kind : 2 * kind + 2, :slot_count] = weight
    branch_scr[4:5, :slot_count] = g_ref[...][None]
    branch_scr[5:6, :slot_count] = b_ref[...][None]
    branch_scr[6:7, :slot_count] = from_ref[...][None].astype(jnp.float32)
    branch_scr[7:8, :slot_count] = to_ref[...][None].astype(jnp.float32)
    bus_scr[20:21, :gen_count] = gen_curv_ref[...][None]
    index_scr[0:1, :slot_count] = from_ref[...][None]
    index_scr[1:2, :slot_count] = to_ref[...][None]
    index_scr[2:3, :bus_count] = bound_ref[...][None]
    index_scr[3:4, :gen_count] = gen_bus_ref[...][None]

    def tiles(ref, first, chunks):
        return [ref[first : first + ROWS, LANES * c : LANES * (c + 1)] for c in range(chunks)]

    def row(ref, number, chunk):
        return ref[number : number + 1, LANES * chunk : LANES * (chunk + 1)]

    lane = iota((ROWS, LANES), 1)
    sub = iota((ROWS, LANES), 0)
    lane_row = iota((1, LANES), 1)
    sub_col = iota((LANES, LANES), 0).astype(jnp.float32)
    inside = lane < ghost_count

    raw_bound = [tall(row(index_scr, 2, c)) for c in range(2)]
    bound = [jnp.where(inside, take_chunks(raw_bound, lane + h * ghost_count), -1) for h in range(2)]
    fetch = [jnp.maximum(b, 0) for b in bound]
    bound_row = [b[0:1].astype(jnp.float32) for b in bound]
    vm_raw, va_raw, grad_raw = (tiles(bus_scr, 8 * f, 2) for f in range(3))
    vm = [jnp.where(inside, take_chunks(vm_raw, f), 1.0) for f in fetch]
    va = [jnp.where(inside, take_chunks(va_raw, f), 0.0) for f in fetch]
    grad = [jnp.where(inside, take_chunks(grad_raw, f), 0.0) for f in fetch]
    cosv = [jnp.cos(a) for a in va]
    sinv = [jnp.sin(a) for a in va]

    earlier = (iota((LANES, LANES), 0) < iota((LANES, LANES), 1)).astype(jnp.bfloat16)
    local, cross_key, place = [], [], []
    local_count = jnp.zeros((1, 1), jnp.float32)
    for c in range(3):
        slot = lane_row + LANES * c
        alive = (slot < live_count) & (slot < slot_count)
        to_raw = row(index_scr, 1, c)
        cross_key.append(jnp.where(alive, to_raw, 9999).astype(jnp.float32))
        keep = jnp.where(alive & (to_raw < bus_count), 1.0, 0.0)
        before = jnp.dot(
            tall(keep).astype(jnp.bfloat16), earlier, preferred_element_type=jnp.float32
        )
        place.append(jnp.where(keep > 0.0, before[0:1] + local_count, -1.0))
        local_count = local_count + jnp.sum(keep, axis=1, keepdims=True)
    place_col = [column(p) for p in place]
    lane_f = lane_row.astype(jnp.float32)
    branch_tiles = tiles(branch_scr, 0, 3)

    def lowest(masks):
        found = functools.reduce(
            jnp.minimum,
            [jnp.where(m, sub_col + float(LANES * c), float(none)) for c, m in masks],
        )
        return jnp.min(found, axis=0, keepdims=True)

    packed, from_key, to_key = [], [], []
    for c in range(3):
        source = lowest([(d, place_col[d] == lane_f + float(LANES * c)) for d in range(c, 3)])
        tile = take_chunks(branch_tiles, tall(source).astype(jnp.int32))
        packed.append(tile)
        empty = source == float(none)
        from_key.append(jnp.where(empty, 9998.0, tile[6:7]))
        to_key.append(jnp.where(empty, 9999.0, tile[7:8]))
    from_col = [column(k) for k in from_key]
    to_col = [column(k) for k in to_key]
    cross_col = [column(k) for k in cross_key[:2]]
    bound_col = [column(b) for b in bound_row]
    gen_col = column(row(index_scr, 3, 0).astype(jnp.float32))
    curv_col = column(row(bus_scr, 20, 0))

    def links(keys, cols):
        heads, counts, matches = [], [], []
        for h in range(2):
            equal = [cols[c] == bound_row[h] for c in range(3)]
            matches.append([jnp.where(e, 1.0, 0.0).astype(jnp.bfloat16) for e in equal])
            heads.append(lowest(list(enumerate(equal))))
            counts.append(
                jnp.sum(
                    functools.reduce(jnp.add, [jnp.where(e, 1.0, 0.0) for e in equal]),
                    axis=0,
                    keepdims=True,
                )
            )
        nexts = []
        for c in range(3):
            later = [(c, (cols[c] == keys[c]) & (sub_col > lane_f))]
            later += [(d, cols[d] == keys[c]) for d in range(c + 1, 3)]
            nexts.append(lowest(later))
        return heads, nexts, jnp.maximum(counts[0], counts[1]), matches

    head_f, next_f, count_f, match_f = links(from_key, from_col)
    head_t, next_t, count_t, match_t = links(to_key, to_col)
    degree = jnp.max(jnp.maximum(count_f, count_t))

    def position(keys):
        found = [
            jnp.where(bound_col[h] == keys, sub_col + float(LANES * h), 0.0) for h in range(2)
        ]
        return jnp.max(jnp.maximum(found[0], found[1]), axis=0, keepdims=True)

    pos_f = [position(k) for k in from_key]
    pos_t = [position(k) for k in to_key]
    for m in range(2):
        pos_ref[m : m + 1, :] = position((lane_row + LANES * m).astype(jnp.float32)).astype(jnp.int32)

    cross = []
    for h in range(2):
        target = jnp.where(lane_row < ghost_count, bus_count + h * ghost_count + lane_row, -5)
        slot = lowest([(c, cross_col[c] == target.astype(jnp.float32)) for c in range(2)])
        cross.append(take_chunks(branch_tiles, tall(slot).astype(jnp.int32)))

    gens = [
        jnp.sum(jnp.where(gen_col == bound_row[h], curv_col, 0.0), axis=0, keepdims=True)
        for h in range(2)
    ]

    pair = sub & 3

    def every_pair(x):
        x = jnp.where(sub < 2, x, pltpu.roll(x, 2, 0))
        return jnp.where(sub < 4, x, pltpu.roll(x, 4, 0))

    from_table, to_table = [], []
    for c in range(3):
        at_f = tall(pos_f[c]).astype(jnp.int32)
        at_t = tall(pos_t[c]).astype(jnp.int32)
        h00, h01, h11, h22, h12, h02 = block_entries(
            *(take_chunks(t, at_f) for t in (vm, cosv, sinv)),
            *(take_chunks(t, at_t) for t in (vm, cosv, sinv)),
            tall(packed[c][4:5]),
            tall(packed[c][5:6]),
            every_pair(packed[c]),
            every_pair(pltpu.roll(packed[c], 6, 0)),
        )
        main = jnp.where(pair < 2, h02, -h11)
        off = jnp.where(pair < 2, -h01, h12)
        first = ROWS * (TILE_LOCAL + c)
        out_ref[first : first + ROWS, :] = jnp.where(sub < 4, main, off)
        from_table.append(jnp.where(sub < 2, h00, jnp.where(sub < 4, h01, h11)))
        to_table.append(jnp.where(sub < 2, h22, jnp.where(sub < 4, -h12, h11)))

    def parts(x):
        high = x.astype(jnp.bfloat16).astype(jnp.float32)
        middle = (x - high).astype(jnp.bfloat16).astype(jnp.float32)
        rest = x - high - middle
        return jnp.concatenate([high, middle, rest, jnp.zeros_like(x)], axis=0).astype(jnp.bfloat16)

    terms = [parts(t) for t in from_table + to_table]
    acc = []
    for h in range(2):
        total = functools.reduce(
            jnp.add,
            [
                jnp.dot(term, match, preferred_element_type=jnp.float32)
                for term, match in zip(terms, match_f[h] + match_t[h])
            ],
        )
        acc.append(total[0:8] + total[8:16] + total[16:24])

    total_local = jnp.max(local_count)

    for h in range(2):
        below = vm[h] - volt_low
        above = volt_high - vm[h]
        barrier = barrier_weight / (below * below) + barrier_weight / (above * above)
        diag_vv = pltpu.roll(acc[h], 4, 0) + barrier + gens[h]
        diag_aa = pltpu.roll(acc[h], 2, 0) + angle_reg + gens[h]
        diag_va = pltpu.roll(acc[h], 6, 0)
        first = ROWS * (TILE_A + h)
        out_ref[first : first + ROWS, :] = jnp.where(
            sub < 4, grad[h], jnp.where(sub < 6, diag_vv, diag_aa)
        )
        first = ROWS * (TILE_B + h)
        out_ref[first : first + ROWS, :] = jnp.where(
            sub < 2, diag_va, jnp.where(sub < 4, vm[h], jnp.where(sub < 6, cosv[h], sinv[h]))
        )
        first = ROWS * (TILE_C + h)
        out_ref[first : first + ROWS, :] = jnp.where(
            sub < 6, cross[h], jnp.where(sub == 6, degree, total_local)
        )
    first = ROWS * TILE_INDEX
    for offset, value in enumerate(pos_f + pos_t + head_f + head_t + next_f + next_t):
        out_ref[first + offset : first + offset + 1, :] = value


def solve_kernel(me_ref, pos_ref, *refs):
    *all_refs, step_ref, residual_ref = refs[:-6]
    chain_scr, end_scr, row_scr, field_scr, step_scr, residual_scr = refs[-6:]
    blocks = len(all_refs)
    me = me_ref[0]
    half = blocks // 2
    bus_count = step_ref.shape[2]
    lane_pairs = [(j, h) for j in range(half) for h in range(2)]
    sub = iota((ROWS, LANES), 0)
    low = sub < 4
    even = (sub & 3) < 2

    def swap_component(x):
        return jnp.where(even, pltpu.roll(x, 6, 0), pltpu.roll(x, 2, 0))

    def swap_block(x):
        return pltpu.roll(x, 4, 0)

    upper = me >= half
    mine = jnp.where(upper, blocks - 1 - me, me)
    near = low != upper

    def halves(tile, j):
        here = all_refs[j][ROWS * tile : ROWS * (tile + 1), :]
        there = all_refs[blocks - 1 - j][ROWS * tile : ROWS * (tile + 1), :]
        first = jnp.where(upper, there, here)
        second = jnp.where(upper, here, there)
        return (
            jnp.where(low, first, swap_block(second)),
            jnp.where(low, swap_block(first), second),
        )

    def quarters(x):
        return (
            jnp.where(even, x, pltpu.roll(x, 2, 0)),
            jnp.where(even, pltpu.roll(x, 6, 0), x),
        )

    def single(number, j):
        return jnp.where(
            near,
            tall(all_refs[j][number : number + 1, :]),
            tall(all_refs[blocks - 1 - j][number : number + 1, :]),
        )

    def across(field):
        out = {}
        for j in range(half):
            inner = [
                field[j + 1, 1 - h] if j + 1 < half else swap_block(field[j, 1 - h])
                for h in range(2)
            ]
            outer = [field[j - 1, 1 - h] if j > 0 else 0.0 for h in range(2)]
            out[j, 0] = jnp.where(low, outer[0], inner[0])
            out[j, 1] = jnp.where(low, inner[1], outer[1])
        return out

    base = ROWS * TILE_INDEX
    names = [(name, h) for name in CHUNK_FIELDS for h in range(2)]
    names += [(name, c) for name in SLOT_FIELDS for c in range(3)]
    place = {name: number for number, name in enumerate(names)}
    for j in range(half):
        found = {}
        for h in range(2):
            found["gradient", h], found["diag", h] = halves(TILE_A + h, j)
            first, second = halves(TILE_B + h, j)
            found["diag_off", h], found["vm", h] = quarters(first)
            found["cosv", h], found["sinv", h] = quarters(second)
            first, _ = halves(TILE_C + h, j)
            found["wp", h], found["wq", h] = quarters(first)
            found["g", h] = single(ROWS * (TILE_C + h) + 4, j)
            found["b", h] = single(ROWS * (TILE_C + h) + 5, j)
            found["extent", h] = single(ROWS * TILE_C + 6 + h, j)
        for c in range(3):
            found["local_main", c], found["local_off", c] = halves(TILE_LOCAL + c, j)
            found["at_from", c] = single(base + c, j)
            found["at_to", c] = single(base + 3 + c, j)
        for name, number in place.items():
            field_scr[number, j ^ mine] = found[name]

    def load(name, chunks):
        return {
            (j, c): field_scr[place[name, c], j] for j in range(half) for c in range(chunks)
        }

    def load_index(name, chunks):
        return {key: value.astype(jnp.int32) for key, value in load(name, chunks).items()}

    gradient, diag, diag_off, vm, cosv, sinv, wp, wq, g, b, extent = (
        load(name, 2) for name in CHUNK_FIELDS
    )
    vm_to, cos_to, sin_to = across(vm), across(cosv), across(sinv)
    to_diag, to_off, main, off = {}, {}, {}, {}
    for key in lane_pairs:
        h00, h01, h11, h22, h12, h02 = block_entries(
            vm[key],
            cosv[key],
            sinv[key],
            vm_to[key],
            cos_to[key],
            sin_to[key],
            g[key],
            b[key],
            wp[key],
            wq[key],
        )
        diag[key] = diag[key] + jnp.where(even, h00, h11)
        diag_off[key] = diag_off[key] + h01
        to_diag[key] = jnp.where(even, h22, h11)
        to_off[key] = -h12
        main[key] = jnp.where(even, h02, -h11)
        off[key] = jnp.where(even, -h01, h12)
    to_diag, to_off = across(to_diag), across(to_off)
    main_to = across(main)
    off_to = across({key: swap_component(off[key]) for key in lane_pairs})
    inverse, inverse_off = {}, {}
    for key in lane_pairs:
        diag[key] = diag[key] + to_diag[key]
        diag_off[key] = diag_off[key] + to_off[key]
        main[key] = main[key] + main_to[key]
        off[key] = off[key] + off_to[key]
        flipped = swap_component(diag[key])
        determinant = diag[key] * flipped - diag_off[key] * diag_off[key]
        inverse[key] = flipped / determinant
        inverse_off[key] = -diag_off[key] / determinant

    local_main, local_off = (load(name, 3) for name in SLOT_FIELDS[:2])
    at_from, at_to = (load_index(name, 3) for name in SLOT_FIELDS[2:])

    def largest(h, pairs):
        return jnp.max(functools.reduce(jnp.maximum, [extent[j, h] for j in pairs]))

    outer_rank = largest(0, [0]).astype(jnp.int32)
    inner_rank = largest(0, range(1, half)).astype(jnp.int32)
    few = (largest(1, [0]) <= 2.0 * LANES) & (largest(1, range(1, half)) <= 1.0 * LANES)

    for number in range(10):
        for s, ref in enumerate(all_refs):
            row_scr[number, s : s + 1, :] = ref[base + 6 + number : base + 7 + number, :]
    links = [row_scr[number].astype(jnp.int32) for number in range(10)]
    heads, next_f, next_t = links[:4], links[4:7], links[7:]

    def follow(rank, ends):
        for kind in range(4):
            end_scr[rank, kind] = ends[kind]
            for j in range(half):
                here = tall(end_scr[rank, kind, j : j + 1, :])
                there = tall(end_scr[rank, kind, blocks - 1 - j : blocks - j, :])
                chain_scr[rank, kind, j ^ mine] = jnp.where(near, here, there)
        return tuple(
            take_chunks(next_f if kind < 2 else next_t, ends[kind]) for kind in range(4)
        )

    ends = tuple(heads)
    for rank in range(SET_RANKS_OUTER):
        ends = follow(rank, ends)
    lax.fori_loop(SET_RANKS_OUTER, jnp.maximum(outer_rank, inner_rank), follow, ends)

    def local_sums(v, sums, outer_chunks, inner_chunks):
        chunks = [outer_chunks] + [inner_chunks] * (half - 1)
        to_from, to_to = {}, {}
        for j in range(half):
            table = [v[j, 0], v[j, 1]]
            for c in range(chunks[j]):
                far = take_chunks(table, at_to[j, c])
                near = take_chunks(table, at_from[j, c])
                to_from[j, c] = local_main[j, c] * far + local_off[j, c] * swap_component(far)
                to_to[j, c] = local_main[j, c] * near + swap_component(local_off[j, c] * near)

        def add_rank(pairs, rank, sums):
            sums = list(sums)
            for number, (j, h) in enumerate(lane_pairs):
                if j in pairs:
                    for offset, terms in ((0, to_from), (2, to_to)):
                        sums[number] += take_listed(
                            [terms[j, c] for c in range(chunks[j])], chain_scr[rank, offset + h, j]
                        )
            return tuple(sums)

        for rank in range(SET_RANKS_OUTER):
            sums = add_rank(range(half if rank < SET_RANKS else 1), rank, sums)
        inner = functools.partial(add_rank, range(1, half))
        sums = lax.fori_loop(SET_RANKS, inner_rank, inner, sums)
        return lax.fori_loop(SET_RANKS_OUTER, outer_rank, functools.partial(add_rank, [0]), sums)

    def operator(v):
        flipped = {key: swap_component(v[key]) for key in lane_pairs}
        v_to, flipped_to = across(v), across(flipped)
        out = tuple(
            diag[key] * v[key]
            + diag_off[key] * flipped[key]
            + main[key] * v_to[key]
            + off[key] * flipped_to[key]
            for key in lane_pairs
        )
        sums = lax.cond(
            few, lambda: local_sums(v, out, 2, 1), lambda: local_sums(v, out, 3, 3)
        )
        return dict(zip(lane_pairs, sums))

    def scenario_total(left, right):
        total = functools.reduce(jnp.add, [left[key] * right[key] for key in lane_pairs])
        total = total + pltpu.roll(total, 2, 0)
        total = total + pltpu.roll(total, 4, 0)
        return jnp.broadcast_to(jnp.sum(total, axis=1, keepdims=True), (ROWS, LANES))

    def precondition(v):
        return {
            key: inverse[key] * v[key] + inverse_off[key] * swap_component(v[key])
            for key in lane_pairs
        }

    residual = gradient
    search = precondition(residual)
    energy = scenario_total(residual, search)
    update = None
    for iteration in range(ITERS):
        image = operator(search)
        step_size = energy / scenario_total(search, image)
        if update is None:
            update = {key: step_size * search[key] for key in lane_pairs}
        else:
            update = {key: update[key] + step_size * search[key] for key in lane_pairs}
        residual = {key: residual[key] - step_size * image[key] for key in lane_pairs}
        if iteration + 1 < ITERS:
            scaled = precondition(residual)
            energy_next = scenario_total(residual, scaled)
            ratio = energy_next / energy
            search = {key: scaled[key] + ratio * search[key] for key in lane_pairs}
            energy = energy_next

    for field, keep_scr, out_ref in (
        (update, step_scr, step_ref),
        (residual, residual_scr, residual_ref),
    ):
        for j, h in lane_pairs:
            keep_scr[j, h] = field[j, h]
        own = []
        for h in range(2):
            tile = keep_scr[mine, h]
            own.append(jnp.where(upper, swap_block(tile), tile))
        for m in range(2):
            width = min(LANES, bus_count - LANES * m)
            values = take_chunks(own, tall(pos_ref[m : m + 1, :]))
            for comp in range(2):
                out_ref[comp, :, LANES * m : LANES * m + width] = values[
                    2 * comp : 2 * comp + 2, :width
                ]


def fast_body(
    volt_mag,
    volt_ang,
    gradient,
    branch_from,
    branch_to,
    branch_count,
    boundary,
    conductance,
    susceptance,
    duals,
    slacks,
    gen_bus,
    gen_curvature,
):
    bus_count = volt_mag.shape[0]
    slot_count = branch_from.shape[0]
    blocks = lax.axis_size("net")
    vmem = pl.BlockSpec(memory_space=pltpu.VMEM)
    smem = pl.BlockSpec(memory_space=pltpu.SMEM)
    payload, position = pl.pallas_call(
        prepare_kernel,
        out_shape=(
            pltpu.VMEM((PAYLOAD_ROWS, LANES), jnp.float32),
            pltpu.VMEM((2, LANES), jnp.int32),
        ),
        in_specs=[vmem] * 13,
        out_specs=(vmem, vmem),
        scratch_shapes=[
            pltpu.VMEM((24, 2 * LANES), jnp.float32),
            pltpu.VMEM((8, 3 * LANES), jnp.float32),
            pltpu.VMEM((8, 3 * LANES), jnp.int32),
        ],
        name="prepare",
    )(
        volt_mag.T,
        volt_ang.T,
        jnp.transpose(gradient, (1, 2, 0)),
        branch_from,
        branch_to,
        branch_count,
        boundary,
        conductance,
        susceptance,
        jnp.transpose(duals, (0, 2, 1)),
        jnp.transpose(slacks, (0, 2, 1)),
        gen_bus,
        gen_curvature,
    )
    def passed(block, other):
        return lax.ppermute(block, "net", [(i, i ^ other) for i in range(blocks)])

    gathered = {0: payload, 1: passed(payload, 1)}
    for other in range(2, blocks):
        gathered[other] = passed(gathered[other % 2], other - other % 2)
    gathered = [gathered[other] for other in range(blocks)]
    me = lax.axis_index("net").astype(jnp.int32)[None]
    tile_pairs = (blocks // 2, 2, ROWS, LANES)
    field = jax.ShapeDtypeStruct((2, 2, bus_count), jnp.float32)
    step, residual = pl.pallas_call(
        solve_kernel,
        out_shape=(field, field),
        in_specs=[smem] + [vmem] * (1 + blocks),
        out_specs=(vmem, vmem),
        scratch_shapes=[
            pltpu.VMEM((slot_count, 4, blocks // 2, ROWS, LANES), jnp.int32),
            pltpu.VMEM((slot_count, 4, blocks, LANES), jnp.int32),
            pltpu.VMEM((10, blocks, LANES), jnp.float32),
            pltpu.VMEM(
                (2 * len(CHUNK_FIELDS) + 3 * len(SLOT_FIELDS), blocks // 2, ROWS, LANES),
                jnp.float32,
            ),
            pltpu.VMEM(tile_pairs, jnp.float32),
            pltpu.VMEM(tile_pairs, jnp.float32),
        ],
        compiler_params=pltpu.CompilerParams(vmem_limit_bytes=40 * 2**20),
        name="solve",
    )(me, position, *gathered)
    return jnp.transpose(step, (2, 0, 1)), jnp.transpose(residual, (2, 0, 1))


def any_body(*arrays):
    volt_mag, boundary, branch_from, gen_bus = arrays[0], arrays[6], arrays[3], arrays[11]
    fast = fits_fast_path(
        lax.axis_size("net"),
        volt_mag.shape[0],
        boundary.shape[0] // 2,
        branch_from.shape[0],
        gen_bus.shape[0],
        volt_mag.shape[1],
    )
    return fast_body(*arrays) if fast else body(*arrays)


def solution(mesh):
    placed = (
        P("net", "scen"),
        P("net", "scen"),
        P("net", None, "scen"),
        P("net"),
        P("net"),
        P("net"),
        P("net"),
        P("net"),
        P("net"),
        P(None, "net", "scen"),
        P(None, "net", "scen"),
        P("net"),
        P("net"),
    )
    return jax.shard_map(
        any_body,
        mesh=mesh,
        in_specs=placed,
        out_specs=(P("net", None, "scen"), P("net", None, "scen")),
        check_vma=False,
    )
```
